32 devices in a mesh: dp: 8 (over z, x), fsdp: 4 (over y, core).
Axes of the slice: x: 2, y: 2, z: 4, core: 2. Of those that a mesh axis runs over, the one named last changes fastest.
Arguments:
- tokens: bfloat16 [32768, 768], P(('dp', 'fsdp')), may hold values from -6 to 6
- w_query: float32 [768, 768], P(('dp', 'fsdp')), may hold values from -0.21875 to 0.21875
- w_pair: float32 [768, 128], P(('dp', 'fsdp')), may hold values from -0.21875 to 0.21875
- w_attn_out: float32 [768, 768], P(('dp', 'fsdp')), may hold values from -1.75 to 1.75
- w_up: float32 [768, 3072], P(('dp', 'fsdp')), may hold values from -0.21875 to 0.21875
- w_down: float32 [3072, 768], P(('dp', 'fsdp')), may hold values from -0.109375 to 0.109375
- ln_gains: float32 [2, 768], P(None, ('dp', 'fsdp')), may hold values from 0.5 to 1.5
- ln_biases: float32 [2, 768], P(None, ('dp', 'fsdp')), may hold values from -1.8 to 1.8
- cotangent: bfloat16 [32768, 768], P(('dp', 'fsdp')), may hold values from -6 to 6
- subset_tags: int32 [32], P(('dp', 'fsdp')), may hold values from 0 to 21
- subset_weights: float32 [22], replicated, may hold values from 0.25 to 4
Outputs:
- mixed: bfloat16 [32768, 768], P(('dp', 'fsdp'))
- grad_tokens: bfloat16 [32768, 768], P(('dp', 'fsdp'))
- grad_query: float32 [768, 768], P(('dp', 'fsdp'))
- grad_pair: float32 [768, 128], P(('dp', 'fsdp'))
- grad_attn_out: float32 [768, 768], P(('dp', 'fsdp'))
- grad_up: float32 [768, 3072], P(('dp', 'fsdp'))
- grad_down: float32 [3072, 768], P(('dp', 'fsdp'))
- grad_gains: float32 [2, 768], P(None, ('dp', 'fsdp'))
- grad_biases: float32 [2, 768], P(None, ('dp', 'fsdp'))
The draws below stay inside these ranges and needn't reach their ends.
All inputs are finite; a program needn't handle non-finite values.
Results may differ from the reference program's by a relative error of at most 0.012.
The reference program's roundings to bfloat16 on the way count: a program that leaves them out, or rounds other values in their place, can miss the bound.
Values may be sent and summed in bfloat16 or wider, within the bound.
A program may use at most 192 MiB of HBM per device.

```python
import math
import jax
import jax.numpy as jnp
from jax import lax

D = 768
H = 12
HD = 64
FF = 3072
ROT = 16
SUBSETS = 22
SEQ = 1024
ROWS = 32
TOKENS = 32768


def plant(array, key, least, top_value):
    dims = array.shape
    place = [jax.random.randint(jax.random.fold_in(key, axis), (), 0, dims[axis]) for axis in range(len(dims))]
    array = array.at[tuple(place)].set(least)
    longest = dims.index(max(dims))
    place[longest] = (place[longest] + 1) % dims[longest]
    return array.at[tuple(place)].set(top_value)


def block_levels(rng, extent, cuts, smallest, high):
    def one(position, blocks):
        draws = jax.random.uniform(jax.random.fold_in(jax.random.fold_in(rng, 6), position), (blocks,), jnp.float32, smallest / len(cuts), high / len(cuts))
        return jnp.repeat(jnp.exp(draws), extent[position] // blocks).reshape((-1,) + (1,) * (len(extent) - position - 1))

    factor_of = one(*cuts[0])
    for cut in cuts[1:]:
        factor_of = factor_of * one(*cut)
    return factor_of


def noise(rng, shape, width, most, shards=(), held_as=jnp.bfloat16):
    drawn = width * jax.random.normal(rng, shape, jnp.float32)
    if shards:
        drawn = drawn * block_levels(rng, shape, shards, -0.22, 0.18)
    return jnp.clip(drawn, -most, most).astype(held_as)


def setup_inputs(seed: int = 0) -> dict:
    arg_keys = jax.random.split(jax.random.key(seed), 12)
    tokens = noise(arg_keys[0], (TOKENS, D), 1.0, 6.0, ((0, 32),))
    w_query = noise(arg_keys[1], (D, D), D ** -0.5, 0.21875, ((0, 32),), jnp.float32)
    w_pair = noise(arg_keys[2], (D, 2 * HD), D ** -0.5, 0.21875, ((0, 32),), jnp.float32)
    w_attn_out = noise(arg_keys[3], (D, D), (D // 64) ** -0.5, 1.75, ((0, 32),), jnp.float32)
    w_up = noise(arg_keys[4], (D, FF), D ** -0.5, 0.21875, ((0, 32),), jnp.float32)
    w_down = noise(arg_keys[5], (FF, D), FF ** -0.5, 0.109375, ((0, 32),), jnp.float32)
    ln_gains = jnp.clip(1.0 + 0.1 * jax.random.normal(arg_keys[6], (2, D), jnp.float32), 0.5, 1.5)
    ln_biases = noise(arg_keys[7], (2, D), 0.3, 1.8, ((1, 32),), jnp.float32)
    cotangent = noise(arg_keys[8], (TOKENS, D), 1.0, 6.0, ((0, 32),))
    subset_tags = plant(jax.random.randint(arg_keys[9], (ROWS,), 0, SUBSETS), jax.random.fold_in(arg_keys[9], 1), 0, SUBSETS - 1).astype(jnp.int32)
    subset_weights = jnp.clip(jnp.exp(jax.random.uniform(arg_keys[10], (SUBSETS,), jnp.float32, math.log(0.25), math.log(4.0))), 0.25, 4.0)
    return dict(tokens=tokens, w_query=w_query, w_pair=w_pair, w_attn_out=w_attn_out, w_up=w_up, w_down=w_down, ln_gains=ln_gains, ln_biases=ln_biases, cotangent=cotangent, subset_tags=subset_tags, subset_weights=subset_weights)


@jax.custom_vjp
def low(v):
    return lax.optimization_barrier(v.astype(jnp.bfloat16)).astype(jnp.float32)

@jax.custom_vjp
def low_back(v):
    return v

def low_keep(v):
    return (low(v), None)

def low_pass(kept, grad):
    return (grad,)

def back_keep(v):
    return (v, None)

def back_low(kept, grad):
    return (low(grad),)
low.defvjp(low_keep, low_pass)
low_back.defvjp(back_keep, back_low)
eps_norm = 1e-05
highest = lax.Precision.HIGHEST

def angles(length):
    inverse = 10000.0 ** (-(jnp.arange(ROT // 2, dtype=jnp.float32) * 2.0) / ROT)
    phase = jnp.arange(length, dtype=jnp.float32)[:, None] * inverse[None, :]
    return (jnp.cos(phase), jnp.sin(phase))

def rotate(field, cos_table, sin_table):
    half = ROT // 2
    first = field[..., :half]
    second = field[..., half:ROT]
    return jnp.concatenate([first * cos_table - second * sin_table, second * cos_table + first * sin_table, field[..., ROT:]], axis=-1)

def layer_norm(inputs, gain, bias):
    row_mean = lax.optimization_barrier(jnp.mean(inputs, axis=-1, keepdims=True))
    centred = inputs - row_mean
    inv_std = lax.rsqrt(lax.optimization_barrier(jnp.mean(centred * centred, axis=-1, keepdims=True)) + eps_norm)
    return centred * inv_std * gain + bias

def forward(inputs, w_query, w_pair, w_attn_out, w_up, w_down, ln_gains, ln_biases):
    gain_rows = low(ln_gains)
    bias_rows = low(ln_biases)
    first_in = low(layer_norm(inputs, gain_rows[0], bias_rows[0]))
    second_in = low(layer_norm(inputs, gain_rows[1], bias_rows[1]))
    query_w, pair_w, out_w, up_w, down_w = (low(w_query), low(w_pair), low(w_attn_out), low(w_up), low(w_down))
    cos_table, sin_table = angles(SEQ)
    query = low_back(jnp.dot(first_in, query_w, precision=highest)).reshape(SEQ, H, HD)
    paired = low_back(jnp.dot(first_in, pair_w, precision=highest))
    query = low(rotate(query, cos_table[:, None, :], sin_table[:, None, :]))
    key_rows = low(rotate(paired[:, :HD], cos_table, sin_table))
    values = low(paired[:, HD:])
    block_len = min(512, SEQ)
    block_count = SEQ // block_len
    query_blocks = query.reshape(block_count, block_len, H, HD)
    starts = jnp.arange(block_count, dtype=jnp.int32) * block_len

    def attend(item):
        query_block, block_start = item
        scores = jnp.einsum('qhd,kd->hqk', query_block, key_rows, precision=highest) * 0.125
        scores = low_back(scores)
        query_pos = block_start + jnp.arange(block_len, dtype=jnp.int32)
        key_pos = jnp.arange(SEQ, dtype=jnp.int32)
        causal = key_pos[None, None, :] <= query_pos[None, :, None]
        scores = jnp.where(causal, scores, -jnp.inf)
        prob_rows = jax.nn.softmax(scores, axis=-1)
        return jnp.einsum('hqk,kd->qhd', low(prob_rows), values, precision=highest)
    attended = lax.map(jax.checkpoint(attend), (query_blocks, starts))
    attended = low(low_back(attended.reshape(SEQ, D)))
    up_pre = low_back(jnp.dot(second_in, up_w, precision=highest))
    hidden = low(jax.nn.gelu(up_pre, approximate=False))
    branch = jnp.dot(attended, out_w, precision=highest) + jnp.dot(hidden, down_w, precision=highest)
    return inputs + low_back(branch)

def reference(tokens, w_query, w_pair, w_attn_out, w_up, w_down, ln_gains, ln_biases, cotangent, subset_tags, subset_weights):
    onehot = (subset_tags[:, None] == jnp.arange(SUBSETS, dtype=jnp.int32)[None, :]).astype(jnp.float32)
    counts = lax.optimization_barrier(jnp.sum(onehot, axis=0))
    row_count = lax.optimization_barrier(jnp.sum(onehot * counts[None, :], axis=1))
    row_weight = lax.optimization_barrier(jnp.sum(onehot * subset_weights[None, :], axis=1))
    row_scale = row_weight / row_count * (ROWS / SUBSETS)
    row_inputs = tokens.astype(jnp.float32).reshape(ROWS, SEQ, D)
    row_cotan = cotangent.astype(jnp.float32).reshape(ROWS, SEQ, D)
    weights = (w_query, w_pair, w_attn_out, w_up, w_down, ln_gains, ln_biases)
    zeros = jax.tree.map(jnp.zeros_like, weights)

    def scan_step(totals, item):
        inputs, cotan, scale = item
        result, pull = jax.vjp(forward, inputs, *weights)
        grads = pull(cotan * scale)
        totals = jax.tree.map(jnp.add, totals, tuple(grads[1:]))
        return (totals, (result.astype(jnp.bfloat16), grads[0].astype(jnp.bfloat16)))
    totals, (results, input_grads) = lax.scan(scan_step, zeros, (row_inputs, row_cotan, row_scale))
    return (results.reshape(ROWS * SEQ, D), input_grads.reshape(ROWS * SEQ, D), totals[0], totals[1], totals[2], totals[3], totals[4], totals[5], totals[6])
```

```python
import functools

import jax
import jax.numpy as jnp
from jax import lax
from jax.experimental import pallas as pl
from jax.experimental.pallas import tpu as pltpu
from jax.sharding import PartitionSpec as P

D = 768
H = 12
HD = 64
ROT = 16
SUBSETS = 22
SEQ = 1024
PACK = 1024
MESH = pl.DeviceIdType.MESH


eps_norm = 1e-05


def place():
    dp, fs = lax.axis_index("dp"), lax.axis_index("fsdp")
    return dp // 2, dp % 2, fs // 2, fs % 2


def device(z, x, y, c):
    return (z * 2 + x, y * 2 + c)


def partners():
    z, x, y, c = place()
    xa, ya = jnp.where(c == 0, 1 - x, x), jnp.where(c == 0, y, 1 - y)
    xb, yb = jnp.where(c == 0, x, 1 - x), jnp.where(c == 0, 1 - y, y)
    return xa, ya, xb, yb


def greet(lines):
    z, x, y, c = place()
    barrier = pltpu.get_barrier_semaphore()
    others = [device(lax.rem(z + d, lines), x, y, c) for d in range(1, lines)]
    others += [device(z, 1 - x, y, c), device(z, x, 1 - y, c), device(z, x, y, 1 - c)]
    for other in others:
        pl.semaphore_signal(barrier, inc=1, device_id=other, device_id_type=MESH)
    pl.semaphore_wait(barrier, len(others))


def remote(src, dst, send, recv, where):
    return pltpu.make_async_remote_copy(
        src_ref=src, dst_ref=dst, send_sem=send, recv_sem=recv, device_id=where, device_id_type=MESH
    )


def layout(rows, rows_down):
    blocks = [(1, 2 * rows, PACK), (1, 2 * rows, D), (1, 2 * rows, 4 * D), (2, rows_down, D)]
    return blocks


def pieces_of(blocks):
    (_, r0, _), (_, r1, _), (_, r2, _), (_, r3, _) = blocks
    return [
        (0, 0, r0, 0, PACK // 2),
        (1, 0, r1, 0, D // 2),
        (2, 0, r2, 0, D),
        (2, 0, r2, D, D),
        (3, 0, r3 // 2, 0, D // 2),
        (3, r3 // 2, r3 // 2, 0, D // 2),
    ]


def lanes(start, size):
    return pl.ds(pl.multiple_of(start, 128), size)


def part(piece, halves, ref, z, x, y, c):
    t, r0, nr, c0, w = piece
    return ref.at[z, x, y, :, pl.ds(r0, nr), lanes(c * halves[t] + c0, w)]


def gather_kernel(lines, rows, blocks, *refs):
    query, pair, small, out, up, down = refs[:6]
    whole = refs[6:10]
    packed, stages = refs[10], refs[11:15]
    swap_send, swap_recv, send, recv = refs[15:19]
    pieces = pieces_of(blocks)
    halves = [b[2] // 2 for b in blocks]
    z, x, y, c = place()
    xa, ya, xb, yb = partners()
    sibling = device(z, x, y, 1 - c)
    packed[:, :D] = query[...]
    packed[:, D : D + 2 * HD] = pair[...]
    packed[:, D + 2 * HD :] = small[...]
    greet(lines)
    sources = [packed, out, up, down]

    def stage_rows(t, core):
        if blocks[t][0] == 2:
            return stages[t].at[core]
        return stages[t].at[0, pl.ds(pl.multiple_of(core * rows, 8), rows)]

    swaps = []
    for t in range(4):
        swaps.append(
            remote(
                sources[t].at[:, lanes((1 - c) * halves[t], halves[t])],
                stage_rows(t, c),
                swap_send.at[t],
                swap_recv.at[t],
                sibling,
            )
        )
        swaps[-1].start()
    started = []
    for t in range(4):
        h = halves[t]
        stage_rows(t, c)[...] = jnp.where(c == 0, sources[t][:, :h], sources[t][:, h:])
        swaps[t].wait_recv()
        whole[t][z, x, y, :, :, lanes(c * h, h)] = stages[t][...].astype(jnp.bfloat16)
        for p, piece in enumerate(pieces):
            if piece[0] != t:
                continue
            for d in range(1, lines):
                block = part(piece, halves, whole[t], z, x, y, c)
                copy = remote(
                    block, block, send.at[p, d - 1], recv.at[p, d - 1], device(lax.rem(z + d, lines), x, y, c)
                )
                copy.start()
                started.append(copy)

    n = lines - 1

    def share(p, k, sx, sy, half, where):
        column = part(pieces[p], halves, whole[pieces[p][0]], slice(None), sx, sy, half)
        return remote(column, column, send.at[p, k], recv.at[p, k], where)

    def go(copy):
        copy.start()
        started.append(copy)

    def first(p):
        t = pieces[p][0]
        for d in range(1, lines):
            block = part(pieces[p], halves, whole[t], lax.rem(z + lines - d, lines), x, y, c)
            remote(block, block, send.at[p, d - 1], recv.at[p, d - 1], sibling).wait_recv()
        go(share(p, n, x, y, c, device(z, xa, ya, c)))
        go(share(p, n + 1, x, y, c, device(z, xb, yb, c)))
        go(share(p, n + 3, x, y, c, sibling))

    def second(p):
        share(p, n, xa, ya, c, sibling).wait_recv()
        go(share(p, n + 2, xa, ya, c, device(z, xb, yb, c)))
        go(share(p, n + 4, xa, ya, c, sibling))

    def third(p):
        share(p, n + 1, xb, yb, c, sibling).wait_recv()
        go(share(p, n + 5, xb, yb, c, sibling))
        share(p, n + 2, 1 - x, 1 - y, c, sibling).wait_recv()
        go(share(p, n + 6, 1 - x, 1 - y, c, sibling))

    def fourth(p):
        for k, sx, sy in ((3, x, y), (4, xb, yb), (5, xa, ya), (6, 1 - x, 1 - y)):
            share(p, n + k, sx, sy, 1 - c, sibling).wait_recv()

    count = len(pieces)
    for s in range(count + 3):
        if s < count:
            first(s)
        if 0 <= s - 1 < count:
            second(s - 1)
        if 0 <= s - 2 < count:
            third(s - 2)
        if 0 <= s - 3 < count:
            fourth(s - 3)
    for copy in swaps + started:
        copy.wait_send()


def gather(lines, query, pair, small, out, up, down):
    rows, rows_down = query.shape[0], down.shape[0]
    blocks = layout(rows, rows_down)
    count, kinds = len(pieces_of(blocks)), lines + 6
    vmem = pl.BlockSpec(memory_space=pltpu.VMEM)
    f32 = jnp.float32
    scratch = [pltpu.VMEM((rows, PACK), f32)]
    scratch += [pltpu.VMEM((g, r, k // 2), f32) for g, r, k in blocks]
    scratch += [pltpu.SemaphoreType.DMA((4,))] * 2 + [pltpu.SemaphoreType.DMA((count, kinds))] * 2
    got = pl.pallas_call(
        functools.partial(gather_kernel, lines, rows, blocks),
        out_shape=[jax.ShapeDtypeStruct((lines, 2, 2, g, r, k), jnp.bfloat16) for g, r, k in blocks],
        in_specs=[vmem] * 6,
        out_specs=[vmem] * 4,
        scratch_shapes=scratch,
        compiler_params=pltpu.CompilerParams(
            collective_id=0, has_side_effects=True, vmem_limit_bytes=60 * 2**20
        ),
        name="gather",
    )(query, pair, small, out, up, down)
    return [a.reshape(-1, a.shape[-1]) for a in got]


def scatter_kernel(lines, rows, blocks, *refs):
    f32, bf16 = jnp.float32, jnp.bfloat16
    grads, outs = refs[:4], refs[4:8]
    near, to_b, from_b, to_a, from_a, to_z, from_z, total, last = (refs[8 + 4 * i : 12 + 4 * i] for i in range(9))
    send, recv = refs[44:46]
    pieces = pieces_of(blocks)
    halves = [b[2] // 2 for b in blocks]
    z, x, y, c = place()
    xa, ya, xb, yb = partners()
    sibling = device(z, x, y, 1 - c)
    greet(lines)
    started = []

    def go(copy):
        copy.start()
        started.append(copy)

    def cut(piece, ref, *lead):
        t, r0, nr, c0, w = piece
        return ref.at[(*lead, slice(None), pl.ds(r0, nr), pl.ds(c0, w))]

    def near_copy(p):
        t = pieces[p][0]
        r0, nr, c0, w = pieces[p][1:]
        return remote(
            grads[t].at[:, :, :, :, pl.ds(r0, nr), lanes((1 - c) * halves[t] + c0, w)],
            near[t].at[:, :, :, :, pl.ds(r0, nr), pl.ds(c0, w)],
            send.at[p, 0],
            recv.at[p, 0],
            sibling,
        )

    def b_copy(p):
        t = pieces[p][0]
        return remote(
            cut(pieces[p], to_b[t], slice(None), slice(None)),
            cut(pieces[p], from_b[t], slice(None), slice(None)),
            send.at[p, 1],
            recv.at[p, 1],
            device(z, xb, yb, c),
        )

    def a_copy(p):
        t = pieces[p][0]
        return remote(
            cut(pieces[p], to_a[t], slice(None)),
            cut(pieces[p], from_a[t], slice(None)),
            send.at[p, 2],
            recv.at[p, 2],
            device(z, xa, ya, c),
        )

    def z_copy(p, d):
        t = pieces[p][0]
        other = lax.rem(z + d, lines)
        return remote(
            cut(pieces[p], to_z[t], other),
            cut(pieces[p], from_z[t], d - 1),
            send.at[p, 2 + d],
            recv.at[p, 2 + d],
            device(other, x, y, c),
        )

    def last_copy(p):
        t, r0, nr, c0, w = pieces[p]
        if blocks[t][0] == 2:
            src = total[t].at[1 - c, pl.ds(r0, nr), pl.ds(c0, w)]
            dst = last[t].at[pl.ds(r0, nr), pl.ds(c0, w)]
        else:
            src = total[t].at[0, pl.ds(pl.multiple_of((1 - c) * rows, 8), rows), pl.ds(c0, w)]
            dst = last[t].at[:, pl.ds(c0, w)]
        return remote(src, dst, send.at[p, 2 + lines], recv.at[p, 2 + lines], sibling)

    def own(p, k, sx, sy):
        t = pieces[p][0]
        a = part(pieces[p], halves, grads[t], k, sx, sy, c)[...].astype(f32)
        return a + cut(pieces[p], near[t], k, sx, sy)[...].astype(f32)

    def first(p):
        go(near_copy(p))

    def second(p):
        t = pieces[p][0]
        near_copy(p).wait_recv()

        @pl.loop(0, lines)
        def _(k):
            cut(pieces[p], to_b[t], 0, k)[...] = own(p, k, xb, yb).astype(bf16)
            cut(pieces[p], to_b[t], 1, k)[...] = own(p, k, 1 - x, 1 - y).astype(bf16)

        go(b_copy(p))

    def third(p):
        t = pieces[p][0]
        b_copy(p).wait_recv()

        @pl.loop(0, lines)
        def _(k):
            got = cut(pieces[p], from_b[t], 1, k)[...].astype(f32)
            cut(pieces[p], to_a[t], k)[...] = (own(p, k, xa, ya) + got).astype(bf16)

        go(a_copy(p))

    def mine(p, k):
        t = pieces[p][0]
        got = cut(pieces[p], from_b[t], 0, k)[...].astype(f32) + cut(pieces[p], from_a[t], k)[...].astype(f32)
        return own(p, k, x, y) + got

    def fourth(p):
        t = pieces[p][0]
        a_copy(p).wait_recv()

        @pl.loop(1, lines)
        def _(d):
            k = lax.rem(z + d, lines)
            cut(pieces[p], to_z[t], k)[...] = mine(p, k).astype(bf16)

        for d in range(1, lines):
            go(z_copy(p, d))
        cut(pieces[p], total[t])[...] = mine(p, z)

    def fifth(p):
        t = pieces[p][0]
        for d in range(1, lines):
            z_copy(p, d).wait_recv()
        acc = cut(pieces[p], total[t])[...]
        for d in range(1, lines):
            acc = acc + cut(pieces[p], from_z[t], d - 1)[...].astype(f32)
        cut(pieces[p], total[t])[...] = acc
        go(last_copy(p))

    def sixth(p):
        t, r0, nr, c0, w = pieces[p]
        last_copy(p).wait_recv()
        if blocks[t][0] == 2:
            kept = total[t].at[c, pl.ds(r0, nr), pl.ds(c0, w)]
            got = last[t].at[pl.ds(r0, nr), pl.ds(c0, w)]
            dst = outs[t].at[pl.ds(r0, nr)]
        else:
            kept = total[t].at[0, pl.ds(pl.multiple_of(c * rows, 8), rows), pl.ds(c0, w)]
            got = last[t].at[:, pl.ds(c0, w)]
            dst = outs[t]
        kept, got = kept[...], got[...]
        h = halves[t]
        dst[:, c0 : c0 + w] = jnp.where(c == 0, kept, got)
        dst[:, h + c0 : h + c0 + w] = jnp.where(c == 0, got, kept)

    count = len(pieces)
    stages = [first, second, third, fourth, fifth, sixth]
    order = [count - 1 - i for i in range(count)]
    for s in range(count + len(stages) - 1):
        for k, stage in enumerate(stages):
            if 0 <= s - k < count:
                stage(order[s - k])
    for copy in started:
        copy.wait_send()


def scatter(lines, rows, rows_down, grads):
    blocks = layout(rows, rows_down)
    grads = [a.reshape(lines, 2, 2, g, r, k) for a, (g, r, k) in zip(grads, blocks)]
    count = len(pieces_of(blocks))
    vmem = pl.BlockSpec(memory_space=pltpu.VMEM)
    f32, bf16 = jnp.float32, jnp.bfloat16
    own_rows = [r if g == 2 else rows for g, r, k in blocks]
    scratch = []
    for lead in ((lines, 2, 2), (2, lines), (2, lines), (lines,), (lines,), (lines,), (lines - 1,)):
        scratch += [pltpu.VMEM((*lead, g, r, k // 2), bf16) for g, r, k in blocks]
    scratch += [pltpu.VMEM((g, r, k // 2), f32) for g, r, k in blocks]
    scratch += [pltpu.VMEM((o, k // 2), f32) for o, (g, r, k) in zip(own_rows, blocks)]
    scratch += [pltpu.SemaphoreType.DMA((count, lines + 3))] * 2
    return pl.pallas_call(
        functools.partial(scatter_kernel, lines, rows, blocks),
        out_shape=[jax.ShapeDtypeStruct((o, k), f32) for o, (g, r, k) in zip(own_rows, blocks)],
        in_specs=[vmem] * 4,
        out_specs=[vmem] * 4,
        scratch_shapes=scratch,
        compiler_params=pltpu.CompilerParams(
            collective_id=1, has_side_effects=True, vmem_limit_bytes=60 * 2**20
        ),
        name="scatter",
    )(*grads)


def angles(length):
    inverse = 10000.0 ** (-(jnp.arange(ROT // 2, dtype=jnp.float32) * 2.0) / ROT)
    phase = jnp.arange(length, dtype=jnp.float32)[:, None] * inverse[None, :]
    return (jnp.cos(phase), jnp.sin(phase))


def rotate(field, cos_table, sin_table):
    half = ROT // 2
    first = field[..., :half]
    second = field[..., half:ROT]
    return jnp.concatenate(
        [
            first * cos_table - second * sin_table,
            second * cos_table + first * sin_table,
            field[..., ROT:],
        ],
        axis=-1,
    )


def unrotate(field, cos_table, sin_table):
    half = ROT // 2
    first = field[..., :half]
    second = field[..., half:ROT]
    return jnp.concatenate(
        [
            first * cos_table + second * sin_table,
            second * cos_table - first * sin_table,
            field[..., ROT:],
        ],
        axis=-1,
    )


def gelu_exact(inputs):
    return jax.nn.gelu(inputs, approximate=False)


def fetch_weights(query_w, pair_w, small_w, out_w, up_w, down_w):
    lines, per_line = lax.axis_size("dp") // 2, lax.axis_size("fsdp")
    if lines >= 2 and per_line == 4 and query_w.shape[0] % 8 == 0:
        packed, out_w, up_w, down_w = gather(lines, query_w, pair_w, small_w, out_w, up_w, down_w)
        return packed, out_w, up_w, down_w
    packed = jnp.concatenate([query_w, pair_w, small_w], axis=1)
    return tuple(
        lax.all_gather(a.astype(jnp.bfloat16), ("dp", "fsdp"), axis=0, tiled=True)
        for a in (packed, out_w, up_w, down_w)
    )


def send_grads(rows, rows_down, grads):
    lines, per_line = lax.axis_size("dp") // 2, lax.axis_size("fsdp")
    if lines >= 2 and per_line == 4 and rows % 8 == 0:
        return scatter(lines, rows, rows_down, [g.astype(jnp.bfloat16) for g in grads])
    return [lax.psum_scatter(g, ("dp", "fsdp"), scatter_dimension=0, tiled=True) for g in grads]


def body(
    tokens,
    w_query,
    w_pair,
    w_attn_out,
    w_up,
    w_down,
    ln_gains,
    ln_biases,
    cotangent,
    subset_tags,
    subset_weights,
):
    bf16 = jnp.bfloat16
    f32 = jnp.float32
    rows_here = subset_tags.shape[0]
    token_count = rows_here * SEQ
    onehot = (subset_tags[:, None] == jnp.arange(SUBSETS, dtype=jnp.int32)[None, :]).astype(f32)
    first_row = (jnp.arange(w_query.shape[0]) == 0)[:, None]
    own_counts = jnp.where(first_row, jnp.sum(onehot, axis=0)[None, :], 0.0)
    small = jnp.concatenate([ln_gains.T, ln_biases.T, own_counts], axis=1)
    small = jnp.pad(small, ((0, 0), (0, 128 - small.shape[1])))
    packed, out_w, up_w, down_w = fetch_weights(w_query, w_pair, small, w_attn_out, w_up, w_down)
    query_w, pair_w = packed[:, :D], packed[:, D : D + 2 * HD]
    small = packed[:, D + 2 * HD :].astype(f32)
    counts = jnp.sum(small[:, 4 : 4 + SUBSETS], axis=0)
    gain_rows, bias_rows = small[:, 0:2].T, small[:, 2:4].T
    inputs = tokens.astype(f32)
    row_mean = jnp.mean(inputs, axis=-1, keepdims=True)
    centred = inputs - row_mean
    inv_std = lax.rsqrt(jnp.mean(centred * centred, axis=-1, keepdims=True) + eps_norm)
    normed = centred * inv_std
    gain_f, bias_f = gain_rows, bias_rows
    first_in = (normed * gain_f[0] + bias_f[0]).astype(bf16)
    second_in = (normed * gain_f[1] + bias_f[1]).astype(bf16)
    cos_table, sin_table = angles(SEQ)
    query = jnp.dot(first_in, query_w, preferred_element_type=f32).reshape(rows_here, SEQ, H, HD)
    query = rotate(query, cos_table[:, None, :], sin_table[:, None, :]).astype(bf16)
    paired = jnp.dot(first_in, pair_w, preferred_element_type=f32).reshape(rows_here, SEQ, 2 * HD)
    key_rows = rotate(paired[..., :HD], cos_table, sin_table).astype(bf16)
    values = paired[..., HD:].astype(bf16)
    block_len = min(512, SEQ)
    block_count = SEQ // block_len

    def block_scores(block_start, block_stop):
        scores = (
            jnp.einsum(
                "rqhd,rkd->rhqk",
                query[:, block_start:block_stop],
                key_rows[:, :block_stop],
                preferred_element_type=f32,
            )
            * 0.125
        )
        causal = jnp.arange(block_stop)[None, :] <= (block_start + jnp.arange(block_len))[:, None]
        return jnp.where(causal[None, None], scores, -jnp.inf)

    outputs = []
    logsums = []
    for block_number in range(block_count):
        block_start = block_number * block_len
        block_stop = block_start + block_len
        scores = block_scores(block_start, block_stop)
        row_peak = jnp.max(scores, axis=-1, keepdims=True)
        weights_exp = jnp.exp(scores - row_peak)
        row_total = jnp.sum(weights_exp, axis=-1, keepdims=True)
        prob_rows = (weights_exp / row_total).astype(bf16)
        outputs.append(
            jnp.einsum(
                "rhqk,rkd->rqhd", prob_rows, values[:, :block_stop], preferred_element_type=f32
            )
        )
        logsums.append(row_peak + jnp.log(row_total))
    attended = jnp.concatenate(outputs, axis=1).reshape(token_count, D).astype(bf16)
    up_pre = jnp.dot(second_in, up_w, preferred_element_type=f32)
    hidden = gelu_exact(up_pre).astype(bf16)
    branch = jnp.dot(attended, out_w, preferred_element_type=f32) + jnp.dot(
        hidden, down_w, preferred_element_type=f32
    )
    mixed = (inputs + branch).astype(bf16)
    row_count = jnp.sum(onehot * counts[None, :], axis=1)
    row_weight = jnp.sum(onehot * subset_weights[None, :], axis=1)
    total_rows = rows_here * lax.axis_size("dp") * lax.axis_size("fsdp")
    row_scale = row_weight / row_count * (total_rows / SUBSETS)
    grad_out = (
        cotangent.astype(f32).reshape(rows_here, SEQ, D) * row_scale[:, None, None]
    ).reshape(token_count, D)
    grad_branch = grad_out.astype(bf16)
    grad_down = jnp.einsum("nf,nd->fd", hidden, grad_branch, preferred_element_type=f32)
    d_hidden = jnp.einsum("nd,fd->nf", grad_branch, down_w, preferred_element_type=f32)
    gelu_pull = jax.vjp(gelu_exact, up_pre)[1]
    d_up = gelu_pull(d_hidden)[0].astype(bf16)
    grad_up = jnp.einsum("nd,nf->df", second_in, d_up, preferred_element_type=f32)
    d_second = jnp.einsum("nf,df->nd", d_up, up_w, preferred_element_type=f32)
    grad_attn = jnp.einsum("nd,ne->de", attended, grad_branch, preferred_element_type=f32)
    d_attended = (
        jnp.einsum("ne,de->nd", grad_branch, out_w, preferred_element_type=f32)
        .astype(bf16)
        .reshape(rows_here, SEQ, H, HD)
    )
    query_grads = []
    d_keys = jnp.zeros((rows_here, SEQ, HD), f32)
    d_values = jnp.zeros((rows_here, SEQ, HD), f32)
    for block_number in range(block_count):
        block_start = block_number * block_len
        block_stop = block_start + block_len
        scores = block_scores(block_start, block_stop)
        prob_rows = jnp.exp(scores - logsums[block_number])
        d_probs = jnp.einsum(
            "rqhd,rkd->rhqk",
            d_attended[:, block_start:block_stop],
            values[:, :block_stop],
            preferred_element_type=f32,
        )
        d_scores = (
            prob_rows * (d_probs - jnp.sum(d_probs * prob_rows, axis=-1, keepdims=True))
        ).astype(bf16)
        query_grads.append(
            jnp.einsum(
                "rhqk,rkd->rqhd", d_scores, key_rows[:, :block_stop], preferred_element_type=f32
            )
            * 0.125
        )
        d_keys = d_keys.at[:, :block_stop].add(
            jnp.einsum(
                "rhqk,rqhd->rkd",
                d_scores,
                query[:, block_start:block_stop],
                preferred_element_type=f32,
            )
            * 0.125
        )
        d_values = d_values.at[:, :block_stop].add(
            jnp.einsum(
                "rhqk,rqhd->rkd",
                prob_rows.astype(bf16),
                d_attended[:, block_start:block_stop],
                preferred_element_type=f32,
            )
        )
    d_query = jnp.concatenate(query_grads, axis=1)
    d_query = (
        unrotate(d_query, cos_table[:, None, :], sin_table[:, None, :])
        .reshape(token_count, D)
        .astype(bf16)
    )
    d_pair = (
        jnp.concatenate([unrotate(d_keys, cos_table, sin_table), d_values], axis=-1)
        .reshape(token_count, 2 * HD)
        .astype(bf16)
    )
    grad_query = jnp.einsum("nd,ne->de", first_in, d_query, preferred_element_type=f32)
    grad_pair = jnp.einsum("nd,ne->de", first_in, d_pair, preferred_element_type=f32)
    d_first = jnp.einsum("ne,de->nd", d_query, query_w, preferred_element_type=f32) + jnp.einsum(
        "ne,de->nd", d_pair, pair_w, preferred_element_type=f32
    )
    grad_gains = jnp.stack([jnp.sum(d_first * normed, axis=0), jnp.sum(d_second * normed, axis=0)])
    grad_biases = jnp.stack([jnp.sum(d_first, axis=0), jnp.sum(d_second, axis=0)])
    d_normed = d_first * gain_f[0] + d_second * gain_f[1]
    d_inputs = inv_std * (
        d_normed
        - jnp.mean(d_normed, axis=-1, keepdims=True)
        - normed * jnp.mean(d_normed * normed, axis=-1, keepdims=True)
    )
    grad_tokens = (grad_out + d_inputs).astype(bf16)
    small_g = jnp.pad(jnp.concatenate([grad_gains, grad_biases], axis=0).T, ((0, 0), (0, 124)))
    packed_g = jnp.concatenate([grad_query, grad_pair, small_g], axis=1)
    packed_g, out_g, up_g, down_g = send_grads(
        w_query.shape[0], w_down.shape[0], [packed_g, grad_attn, grad_up, grad_down]
    )
    small_g = packed_g[:, D + 2 * HD : D + 2 * HD + 4].T
    return (
        mixed,
        grad_tokens,
        packed_g[:, :D],
        packed_g[:, D : D + 2 * HD],
        out_g,
        up_g,
        down_g,
        small_g[:2],
        small_g[2:],
    )


def solution(mesh):
    in_specs = (
        P(("dp", "fsdp"), None),
        P(("dp", "fsdp"), None),
        P(("dp", "fsdp"), None),
        P(("dp", "fsdp"), None),
        P(("dp", "fsdp"), None),
        P(("dp", "fsdp"), None),
        P(None, ("dp", "fsdp")),
        P(None, ("dp", "fsdp")),
        P(("dp", "fsdp"), None),
        P(("dp", "fsdp")),
        P(),
    )
    out_specs = (
        P(("dp", "fsdp"), None),
        P(("dp", "fsdp"), None),
        P(("dp", "fsdp"), None),
        P(("dp", "fsdp"), None),
        P(("dp", "fsdp"), None),
        P(("dp", "fsdp"), None),
        P(("dp", "fsdp"), None),
        P(None, ("dp", "fsdp")),
        P(None, ("dp", "fsdp")),
    )
    return jax.shard_map(body, mesh=mesh, in_specs=in_specs, out_specs=out_specs, check_vma=False)
```

```python
import functools

import jax
import jax.numpy as jnp
from jax import lax
from jax.experimental import pallas as pl
from jax.experimental.pallas import tpu as pltpu
from jax.sharding import PartitionSpec as P

D = 768
H = 12
HD = 64
ROT = 16
SUBSETS = 22
SEQ = 1024
PACK = 1024
TILE = 256
LOG2E = 1.4426950408889634
MESH = pl.DeviceIdType.MESH


eps_norm = 1e-05


def place():
    dp, fs = lax.axis_index("dp"), lax.axis_index("fsdp")
    return dp // 2, dp % 2, fs // 2, fs % 2


def device(z, x, y, c):
    return (z * 2 + x, y * 2 + c)


def partners():
    z, x, y, c = place()
    xa, ya = jnp.where(c == 0, 1 - x, x), jnp.where(c == 0, y, 1 - y)
    xb, yb = jnp.where(c == 0, x, 1 - x), jnp.where(c == 0, 1 - y, y)
    return xa, ya, xb, yb


def greet(lines):
    z, x, y, c = place()
    barrier = pltpu.get_barrier_semaphore()
    others = [device(lax.rem(z + d, lines), x, y, c) for d in range(1, lines)]
    others += [device(z, 1 - x, y, c), device(z, x, 1 - y, c), device(z, x, y, 1 - c)]
    for other in others:
        pl.semaphore_signal(barrier, inc=1, device_id=other, device_id_type=MESH)
    pl.semaphore_wait(barrier, len(others))


def remote(src, dst, send, recv, where):
    return pltpu.make_async_remote_copy(
        src_ref=src, dst_ref=dst, send_sem=send, recv_sem=recv, device_id=where, device_id_type=MESH
    )


def layout(rows, rows_down):
    blocks = [(1, 2 * rows, PACK), (1, 2 * rows, D), (1, 2 * rows, 4 * D), (2, rows_down, D)]
    return blocks


def pieces_of(blocks):
    (_, r0, _), (_, r1, _), (_, r2, _), (_, r3, _) = blocks
    up, third = D // 2, r3 // 3 // 16 * 16
    downs = [(0, third), (third, third), (2 * third, r3 - 2 * third)]
    return (
        [(0, 0, r0, 0, PACK // 2)]
        + [(2, 0, r2, k * up, up) for k in range(4)]
        + [(1, 0, r1, 0, D // 2)]
        + [(3, r, n, 0, D // 2) for r, n in downs]
    )


def lanes(start, size):
    return pl.ds(pl.multiple_of(start, 128), size)


def part(piece, halves, ref, z, x, y, c):
    t, r0, nr, c0, w = piece
    return ref.at[z, x, y, :, pl.ds(r0, nr), lanes(c * halves[t] + c0, w)]


class Gather:
    def __init__(self, lines, rows, blocks, sources, stages, whole, sems):
        self.lines, self.rows, self.blocks = lines, rows, blocks
        self.sources, self.stages, self.whole = sources, stages, whole
        self.swap_send, self.swap_recv, self.send, self.recv = sems
        self.pieces = pieces_of(blocks)
        self.halves = [b[2] // 2 for b in blocks]
        self.z, self.x, self.y, self.c = place()
        self.xa, self.ya, self.xb, self.yb = partners()
        self.sibling = device(self.z, self.x, self.y, 1 - self.c)
        self.started = []

    def go(self, make):
        make().start()
        self.started.append(make)

    def stage_rows(self, t, core):
        if self.blocks[t][0] == 2:
            return self.stages[t].at[core]
        return self.stages[t].at[0, pl.ds(pl.multiple_of(core * self.rows, 8), self.rows)]

    def swap(self, t):
        h = self.halves[t]
        return remote(
            self.sources[t].at[:, lanes((1 - self.c) * h, h)],
            self.stage_rows(t, self.c),
            self.swap_send.at[t],
            self.swap_recv.at[t],
            self.sibling,
        )

    def direct(self, p, d, received=False):
        z, n = self.z, self.lines
        at = lax.rem(z + n - d, n) if received else z
        block = part(self.pieces[p], self.halves, self.whole[self.pieces[p][0]], at, self.x, self.y, self.c)
        where = device(lax.rem(z + d, n), self.x, self.y, self.c)
        return remote(block, block, self.send.at[p, d - 1], self.recv.at[p, d - 1], where)

    def share(self, p, k, sx, sy, half, where):
        column = part(self.pieces[p], self.halves, self.whole[self.pieces[p][0]], slice(None), sx, sy, half)
        k = k + self.lines - 1
        return remote(column, column, self.send.at[p, k], self.recv.at[p, k], where)

    def begin(self):
        for t in (0, 2, 1, 3):
            self.go(functools.partial(self.swap, t))
        for t in (0, 2, 1, 3):
            h = self.halves[t]
            self.stage_rows(t, self.c)[...] = jnp.where(self.c == 0, self.sources[t][:, :h], self.sources[t][:, h:])
            self.swap(t).wait_recv()
            self.whole[t][self.z, self.x, self.y, :, :, lanes(self.c * h, h)] = self.stages[t][...].astype(jnp.bfloat16)
            for p, piece in enumerate(self.pieces):
                if piece[0] == t:
                    for d in range(1, self.lines):
                        self.go(functools.partial(self.direct, p, d))

    def first(self, p):
        for d in range(1, self.lines):
            self.direct(p, d, received=True).wait_recv()
        x, y, c, z = self.x, self.y, self.c, self.z
        self.go(lambda: self.share(p, 0, x, y, c, device(z, self.xa, self.ya, c)))
        self.go(lambda: self.share(p, 1, x, y, c, device(z, self.xb, self.yb, c)))
        self.go(lambda: self.share(p, 3, x, y, c, self.sibling))

    def second(self, p):
        c, z = self.c, self.z
        self.share(p, 0, self.xa, self.ya, c, self.sibling).wait_recv()
        self.go(lambda: self.share(p, 2, self.xa, self.ya, c, device(z, self.xb, self.yb, c)))
        self.go(lambda: self.share(p, 4, self.xa, self.ya, c, self.sibling))

    def third(self, p):
        x, y, c = self.x, self.y, self.c
        self.share(p, 1, self.xb, self.yb, c, self.sibling).wait_recv()
        self.go(lambda: self.share(p, 5, self.xb, self.yb, c, self.sibling))
        self.share(p, 2, 1 - x, 1 - y, c, self.sibling).wait_recv()
        self.go(lambda: self.share(p, 6, 1 - x, 1 - y, c, self.sibling))

    def fourth(self, p):
        x, y, c = self.x, self.y, 1 - self.c
        for k, sx, sy in ((3, x, y), (4, self.xb, self.yb), (5, self.xa, self.ya), (6, 1 - x, 1 - y)):
            self.share(p, k, sx, sy, c, self.sibling).wait_recv()

    def events(self):
        count, order = len(self.pieces), []
        for s in range(count + 3):
            for k, step in enumerate((self.first, self.second, self.third, self.fourth)):
                if 0 <= s - k < count:
                    order.append((functools.partial(step, s - k), (k, s - k)))
        cut = order.index(next(o for o in order if o[1] == (3, 0))) + 1
        return order[:cut], order[cut:]


def spread(events, slots):
    plan = [[] for _ in range(slots)]
    for k, event in enumerate(events):
        plan[k * slots // max(len(events), 1)].append(event)
    return plan


def run_at(index, values):
    for value, events in values:
        if events:

            @pl.when(index == value)
            def _(events=events):
                for event in events:
                    event()


def columns(ref, start, size):
    return ref[:, :, :, :, :, pl.ds(start, size)].reshape(-1, size)


def turned(a, b):
    return lax.dot_general(a, b, (((1,), (1,)), ((), ())), preferred_element_type=jnp.float32)


def swapped(block, cosine, sine):
    lane = lax.broadcasted_iota(jnp.int32, block.shape, 1)
    other = jnp.where(lane % 16 < 8, pltpu.roll(block, 120, 1), pltpu.roll(block, 8, 1))
    return block * cosine + other * sine


def forward_kernel(lines, rows, blocks, linked, *refs):
    f32, bf16 = jnp.float32, jnp.bfloat16
    tokens, cosine, sine = refs[:3]
    given = refs[3:9] if linked else refs[3:7]
    refs = refs[9:] if linked else refs[7:]
    results, refs = refs[: 9 + 4 * linked], refs[9 + 4 * linked :]
    small, first_in, second_in, queries, kv, attended, logsums, hidden, slope, *rest = refs
    normed, keys, values_t, mask, out_sems, *rest = rest
    held = [small, first_in, second_in, queries, kv, attended, logsums, hidden, slope]
    flushed = []

    def flush(*which):
        for k in which:
            copy = pltpu.make_async_copy(held[k], results[k], out_sems.at[k])
            copy.start()
            flushed.append(copy)

    if linked:
        query, pair, extra, out, up, down = given
        whole, packed, stages, sems = rest[:4], rest[4], rest[5:9], rest[9:13]
        held += whole
        packed[:, :D] = query[...]
        packed[:, D : D + 2 * HD] = pair[...]
        packed[:, D + 2 * HD :] = extra[...]
        greet(lines)
        gather = Gather(lines, rows, blocks, [packed, out, up, down], stages, whole, sems)
        gather.begin()
        urgent, later = gather.events()
        cut = later.index(next(e for e in later if e[1] == (3, 4))) + 1
        early, late = [e[0] for e in later[:cut]], [e[0] for e in later[cut:]]
    else:
        whole, early, late = given, [], []
    packed_w, up_w = whole[0], whole[2]

    row = lax.broadcasted_iota(jnp.int32, (TILE, TILE), 0)
    column = lax.broadcasted_iota(jnp.int32, (TILE, TILE), 1)
    mask[...] = jnp.where(row <= column, 0.0, -1e30)
    tiles = SEQ // TILE

    def tile(k):
        return pl.ds(pl.multiple_of(k * TILE, TILE), TILE)

    @pl.loop(0, tiles)
    def _(k):
        inputs = tokens[tile(k), :].astype(f32)
        centred = inputs - jnp.mean(inputs, axis=-1, keepdims=True)
        normed[tile(k), :] = centred * lax.rsqrt(jnp.mean(centred * centred, axis=-1, keepdims=True) + eps_norm)

    if linked:
        for event, _ in urgent:
            event()
    small[...] = columns(packed_w, D + 2 * HD, 128).astype(f32).T
    plan = spread(early, 28)

    @pl.loop(0, tiles)
    def _(k):
        norm = normed[tile(k), :]
        a1 = (norm * small[0:1, :] + small[2:3, :]).astype(bf16)
        first_in[tile(k), :] = a1
        second_in[tile(k), :] = (norm * small[1:2, :] + small[3:4, :]).astype(bf16)
        mixed = jnp.dot(a1, columns(packed_w, 0, D + 2 * HD), preferred_element_type=f32)
        cos_t, sin_t = cosine[tile(k), :], sine[tile(k), :]
        left = lax.broadcasted_iota(jnp.int32, (TILE, 2 * HD), 1) < HD
        for p in range(H // 2):
            turn = swapped(mixed[:, 2 * HD * p : 2 * HD * (p + 1)], cos_t, sin_t).astype(bf16).astype(f32)
            turn = turn * (LOG2E / 8)
            high = turn.astype(bf16).astype(f32)
            low = turn - high
            queries[2 * p, tile(k), :] = jnp.where(left, high, pltpu.roll(low, HD, 1)).astype(bf16)
            queries[2 * p + 1, tile(k), :] = jnp.where(left, pltpu.roll(high, HD, 1), low).astype(bf16)
        pair_t = mixed[:, D : D + 2 * HD]
        pair_t = jnp.where(left, swapped(pair_t, cos_t, sin_t), pair_t).astype(bf16).astype(f32)
        kv[tile(k), :] = pair_t.astype(bf16)
        other = pltpu.roll(pair_t, HD, 1)
        keys[tile(k), :] = jnp.where(left, pair_t, other).astype(bf16)
        lane = lax.broadcasted_iota(jnp.int32, (TILE, 2 * HD), 1)
        ones = jnp.where(lane == HD, 1.0, 0.0)
        values_t[:, tile(k)] = jnp.where(left, other, ones).T.astype(bf16)
        run_at(k, [(v, plan[v]) for v in range(tiles)])

    flush(0, 1, 2, 3, 4)
    plan = plan[tiles:]

    @pl.loop(0, H // 2)
    def _(pr):
        for i in range(tiles):
            count = TILE * (i + 1)
            heads = []
            for hh in range(2):
                head = pr * 2 + hh
                scores = turned(keys[0:count, :], queries[head, i * TILE : count, :])
                last = scores[count - TILE :] + mask[...]
                peak = jnp.max(last, axis=0, keepdims=True)
                if i:
                    peak = jnp.maximum(peak, jnp.max(scores[: count - TILE], axis=0, keepdims=True))
                probs = jnp.exp2(last - peak).astype(bf16)
                if i:
                    probs = jnp.concatenate([jnp.exp2(scores[: count - TILE] - peak).astype(bf16), probs], axis=0)
                got = jnp.dot(values_t[:, 0:count], probs, preferred_element_type=f32)
                total = got[HD : HD + 1]
                heads.append(got[:HD] * (1.0 / total))
                logsums[head, :, i * TILE : count] = peak + jnp.log2(total)
            both = jnp.concatenate(heads, axis=0).T
            attended[i * TILE : count, lanes(pr * 2 * HD, 2 * HD)] = both.astype(bf16)
            run_at(pr, [(v, plan[v * tiles + i]) for v in range(H // 2)])

    flush(5, 6)
    plan = spread(late, 4 * tiles)

    @pl.loop(0, 4 * tiles)
    def _(s):
        chunk, k = s // tiles, s % tiles
        pre = jnp.dot(second_in[tile(k), :], columns(up_w, pl.multiple_of(chunk * D, D), D), preferred_element_type=f32)
        cdf = 0.5 + 0.5 * lax.erf(pre * 0.7071067811865476)
        hidden[tile(k), lanes(chunk * D, D)] = (pre * cdf).astype(bf16)
        density = jnp.exp2(pre * pre * (-0.5 * LOG2E)) * 0.3989422804014327
        slope[tile(k), lanes(chunk * D, D)] = (cdf + pre * density).astype(bf16)
        run_at(s, [(v, plan[v]) for v in range(4 * tiles)])

    flush(7, 8)
    if linked:
        flush(9, 10, 11, 12)
        for make in gather.started:
            make().wait_send()
    for copy in flushed:
        copy.wait()


def tables():
    cos_t, sin_t = angles(SEQ)
    rest = jnp.zeros((SEQ, HD - ROT), jnp.float32)
    cosine = jnp.concatenate([cos_t, cos_t, rest + 1.0] * 2, axis=1)
    sine = jnp.concatenate([-sin_t, sin_t, rest] * 2, axis=1)
    return cosine, sine


def forward(linked, lines, rows, rows_down, tokens, cosine, sine, weights):
    blocks = layout(rows, rows_down)
    f32, bf16 = jnp.float32, jnp.bfloat16
    shapes = [(lines, 2, 2, g, r, k) for g, r, k in blocks]
    if not linked:
        weights = [a.reshape(shape) for a, shape in zip(weights, shapes)]
    held = [
        ((128, D), f32),
        ((SEQ, D), bf16),
        ((SEQ, D), bf16),
        ((H, SEQ, 2 * HD), bf16),
        ((SEQ, 2 * HD), bf16),
        ((SEQ, D), bf16),
        ((H, 1, SEQ), f32),
        ((SEQ, 4 * D), bf16),
        ((SEQ, 4 * D), bf16),
    ]
    scratch = [pltpu.VMEM(shape, kind) for shape, kind in held]
    scratch += [
        pltpu.VMEM((SEQ, D), f32),
        pltpu.VMEM((SEQ, 2 * HD), bf16),
        pltpu.VMEM((2 * HD, SEQ), bf16),
        pltpu.VMEM((TILE, TILE), f32),
        pltpu.SemaphoreType.DMA((13,)),
    ]
    if linked:
        held += [(shape, bf16) for shape in shapes]
        scratch += [pltpu.VMEM(shape, bf16) for shape in shapes]
        scratch += [pltpu.VMEM((rows, PACK), f32)]
        scratch += [pltpu.VMEM((g, r, k // 2), f32) for g, r, k in blocks]
        count, kinds = len(pieces_of(blocks)), lines + 6
        scratch += [pltpu.SemaphoreType.DMA((4,))] * 2 + [pltpu.SemaphoreType.DMA((count, kinds))] * 2
    got = pl.pallas_call(
        functools.partial(forward_kernel, lines, rows, blocks, linked),
        out_shape=[jax.ShapeDtypeStruct(shape, kind) for shape, kind in held],
        in_specs=[pl.BlockSpec(memory_space=pltpu.VMEM)] * (3 + len(weights)),
        out_specs=[pl.BlockSpec(memory_space=pl.ANY)] * len(held),
        scratch_shapes=scratch,
        compiler_params=pltpu.CompilerParams(
            collective_id=0 if linked else None, has_side_effects=linked, vmem_limit_bytes=60 * 2**20
        ),
        name="forward",
    )(tokens, cosine, sine, *weights)
    return got[:9], list(got[9:]) if linked else weights


def scatter_kernel(lines, rows, blocks, *refs):
    f32, bf16 = jnp.float32, jnp.bfloat16
    grads, outs = refs[:4], refs[4:8]
    near, to_b, from_b, to_a, from_a, to_z, from_z, total, last = (refs[8 + 4 * i : 12 + 4 * i] for i in range(9))
    send, recv = refs[44:46]
    pieces = pieces_of(blocks)
    halves = [b[2] // 2 for b in blocks]
    z, x, y, c = place()
    xa, ya, xb, yb = partners()
    sibling = device(z, x, y, 1 - c)
    greet(lines)
    started = []

    def go(copy):
        copy.start()
        started.append(copy)

    def cut(piece, ref, *lead):
        t, r0, nr, c0, w = piece
        return ref.at[(*lead, slice(None), pl.ds(r0, nr), pl.ds(c0, w))]

    def near_copy(p):
        t = pieces[p][0]
        r0, nr, c0, w = pieces[p][1:]
        return remote(
            grads[t].at[:, :, :, :, pl.ds(r0, nr), lanes((1 - c) * halves[t] + c0, w)],
            near[t].at[:, :, :, :, pl.ds(r0, nr), pl.ds(c0, w)],
            send.at[p, 0],
            recv.at[p, 0],
            sibling,
        )

    def b_copy(p):
        t = pieces[p][0]
        return remote(
            cut(pieces[p], to_b[t], slice(None), slice(None)),
            cut(pieces[p], from_b[t], slice(None), slice(None)),
            send.at[p, 1],
            recv.at[p, 1],
            device(z, xb, yb, c),
        )

    def a_copy(p):
        t = pieces[p][0]
        return remote(
            cut(pieces[p], to_a[t], slice(None)),
            cut(pieces[p], from_a[t], slice(None)),
            send.at[p, 2],
            recv.at[p, 2],
            device(z, xa, ya, c),
        )

    def z_copy(p, d):
        t = pieces[p][0]
        other = lax.rem(z + d, lines)
        return remote(
            cut(pieces[p], to_z[t], other),
            cut(pieces[p], from_z[t], d - 1),
            send.at[p, 2 + d],
            recv.at[p, 2 + d],
            device(other, x, y, c),
        )

    def last_copy(p):
        t, r0, nr, c0, w = pieces[p]
        if blocks[t][0] == 2:
            src = total[t].at[1 - c, pl.ds(r0, nr), pl.ds(c0, w)]
            dst = last[t].at[pl.ds(r0, nr), pl.ds(c0, w)]
        else:
            src = total[t].at[0, pl.ds(pl.multiple_of((1 - c) * rows, 8), rows), pl.ds(c0, w)]
            dst = last[t].at[:, pl.ds(c0, w)]
        return remote(src, dst, send.at[p, 2 + lines], recv.at[p, 2 + lines], sibling)

    def own(p, k, sx, sy):
        t = pieces[p][0]
        a = part(pieces[p], halves, grads[t], k, sx, sy, c)[...].astype(f32)
        return a + cut(pieces[p], near[t], k, sx, sy)[...].astype(f32)

    def first(p):
        go(near_copy(p))

    def second(p):
        t = pieces[p][0]
        near_copy(p).wait_recv()

        @pl.loop(0, lines)
        def _(k):
            cut(pieces[p], to_b[t], 0, k)[...] = own(p, k, xb, yb).astype(bf16)
            cut(pieces[p], to_b[t], 1, k)[...] = own(p, k, 1 - x, 1 - y).astype(bf16)

        go(b_copy(p))

    def third(p):
        t = pieces[p][0]
        b_copy(p).wait_recv()

        @pl.loop(0, lines)
        def _(k):
            got = cut(pieces[p], from_b[t], 1, k)[...].astype(f32)
            cut(pieces[p], to_a[t], k)[...] = (own(p, k, xa, ya) + got).astype(bf16)

        go(a_copy(p))

    def mine(p, k):
        t = pieces[p][0]
        got = cut(pieces[p], from_b[t], 0, k)[...].astype(f32) + cut(pieces[p], from_a[t], k)[...].astype(f32)
        return own(p, k, x, y) + got

    def fourth(p):
        t = pieces[p][0]
        a_copy(p).wait_recv()

        @pl.loop(1, lines)
        def _(d):
            k = lax.rem(z + d, lines)
            cut(pieces[p], to_z[t], k)[...] = mine(p, k).astype(bf16)

        for d in range(1, lines):
            go(z_copy(p, d))
        cut(pieces[p], total[t])[...] = mine(p, z)

    def fifth(p):
        t = pieces[p][0]
        for d in range(1, lines):
            z_copy(p, d).wait_recv()
        acc = cut(pieces[p], total[t])[...]
        for d in range(1, lines):
            acc = acc + cut(pieces[p], from_z[t], d - 1)[...].astype(f32)
        cut(pieces[p], total[t])[...] = acc
        go(last_copy(p))

    def sixth(p):
        t, r0, nr, c0, w = pieces[p]
        last_copy(p).wait_recv()
        if blocks[t][0] == 2:
            kept = total[t].at[c, pl.ds(r0, nr), pl.ds(c0, w)]
            got = last[t].at[pl.ds(r0, nr), pl.ds(c0, w)]
            dst = outs[t].at[pl.ds(r0, nr)]
        else:
            kept = total[t].at[0, pl.ds(pl.multiple_of(c * rows, 8), rows), pl.ds(c0, w)]
            got = last[t].at[:, pl.ds(c0, w)]
            dst = outs[t]
        kept, got = kept[...], got[...]
        h = halves[t]
        dst[:, c0 : c0 + w] = jnp.where(c == 0, kept, got)
        dst[:, h + c0 : h + c0 + w] = jnp.where(c == 0, got, kept)

    count = len(pieces)
    stages = [first, second, third, fourth, fifth, sixth]
    order = [count - 1 - i for i in range(count)]
    for s in range(count + len(stages) - 1):
        for k, stage in enumerate(stages):
            if 0 <= s - k < count:
                stage(order[s - k])
    for copy in started:
        copy.wait_send()


def scatter(lines, rows, rows_down, grads):
    blocks = layout(rows, rows_down)
    grads = [a.reshape(lines, 2, 2, g, r, k) for a, (g, r, k) in zip(grads, blocks)]
    count = len(pieces_of(blocks))
    vmem = pl.BlockSpec(memory_space=pltpu.VMEM)
    f32, bf16 = jnp.float32, jnp.bfloat16
    own_rows = [r if g == 2 else rows for g, r, k in blocks]
    scratch = []
    for lead in ((lines, 2, 2), (2, lines), (2, lines), (lines,), (lines,), (lines,), (lines - 1,)):
        scratch += [pltpu.VMEM((*lead, g, r, k // 2), bf16) for g, r, k in blocks]
    scratch += [pltpu.VMEM((g, r, k // 2), f32) for g, r, k in blocks]
    scratch += [pltpu.VMEM((o, k // 2), f32) for o, (g, r, k) in zip(own_rows, blocks)]
    scratch += [pltpu.SemaphoreType.DMA((count, lines + 3))] * 2
    return pl.pallas_call(
        functools.partial(scatter_kernel, lines, rows, blocks),
        out_shape=[jax.ShapeDtypeStruct((o, k), f32) for o, (g, r, k) in zip(own_rows, blocks)],
        in_specs=[vmem] * 4,
        out_specs=[vmem] * 4,
        scratch_shapes=scratch,
        compiler_params=pltpu.CompilerParams(
            collective_id=1, has_side_effects=True, vmem_limit_bytes=60 * 2**20
        ),
        name="scatter",
    )(*grads)


def angles(length):
    inverse = 10000.0 ** (-(jnp.arange(ROT // 2, dtype=jnp.float32) * 2.0) / ROT)
    phase = jnp.arange(length, dtype=jnp.float32)[:, None] * inverse[None, :]
    return (jnp.cos(phase), jnp.sin(phase))


def rotate(field, cos_table, sin_table):
    half = ROT // 2
    first = field[..., :half]
    second = field[..., half:ROT]
    return jnp.concatenate(
        [
            first * cos_table - second * sin_table,
            second * cos_table + first * sin_table,
            field[..., ROT:],
        ],
        axis=-1,
    )


def unrotate(field, cos_table, sin_table):
    half = ROT // 2
    first = field[..., :half]
    second = field[..., half:ROT]
    return jnp.concatenate(
        [
            first * cos_table + second * sin_table,
            second * cos_table - first * sin_table,
            field[..., ROT:],
        ],
        axis=-1,
    )


def is_linked(rows):
    return lax.axis_size("dp") >= 4 and lax.axis_size("fsdp") == 4 and rows % 8 == 0


def fetch_weights(query_w, pair_w, small_w, out_w, up_w, down_w):
    packed = jnp.concatenate([query_w, pair_w, small_w], axis=1)
    return [
        lax.all_gather(a.astype(jnp.bfloat16), ("dp", "fsdp"), axis=0, tiled=True)
        for a in (packed, out_w, up_w, down_w)
    ]


def send_grads(rows, rows_down, grads):
    if is_linked(rows):
        return scatter(lax.axis_size("dp") // 2, rows, rows_down, [g.astype(jnp.bfloat16) for g in grads])
    return [lax.psum_scatter(g, ("dp", "fsdp"), scatter_dimension=0, tiled=True) for g in grads]


def body(
    tokens,
    w_query,
    w_pair,
    w_attn_out,
    w_up,
    w_down,
    ln_gains,
    ln_biases,
    cotangent,
    subset_tags,
    subset_weights,
):
    bf16 = jnp.bfloat16
    f32 = jnp.float32
    rows_here = subset_tags.shape[0]
    token_count = rows_here * SEQ
    onehot = (subset_tags[:, None] == jnp.arange(SUBSETS, dtype=jnp.int32)[None, :]).astype(f32)
    first_row = (jnp.arange(w_query.shape[0]) == 0)[:, None]
    own_counts = jnp.where(first_row, jnp.sum(onehot, axis=0)[None, :], 0.0)
    small = jnp.concatenate([ln_gains.T, ln_biases.T, own_counts], axis=1)
    small = jnp.pad(small, ((0, 0), (0, 128 - small.shape[1])))
    cosine, sine = tables()
    cos_table, sin_table = angles(SEQ)
    linked = is_linked(w_query.shape[0])
    shards = (w_query, w_pair, small, w_attn_out, w_up, w_down)
    if linked:
        lines, rows, rows_down = lax.axis_size("dp") // 2, w_query.shape[0], w_down.shape[0]
    else:
        lines, rows, rows_down = 4, D // 32, 4 * D // 32
        shards = fetch_weights(*shards)
    kept, whole = forward(linked, lines, rows, rows_down, tokens, cosine, sine, shards)
    small, first_in, second_in, queries, kv, attended, logsums, hidden, slope = kept
    packed, out_w, up_w, down_w = [a.reshape(-1, a.shape[-1]) for a in whole]
    query_w, pair_w = packed[:, :D], packed[:, D : D + 2 * HD]
    counts = jnp.sum(small[4 : 4 + SUBSETS], axis=1)
    gain_f = small[0:2]
    inputs = tokens.astype(f32)
    row_mean = jnp.mean(inputs, axis=-1, keepdims=True)
    centred = inputs - row_mean
    inv_std = lax.rsqrt(jnp.mean(centred * centred, axis=-1, keepdims=True) + eps_norm)
    normed = centred * inv_std
    query = (queries[:, :, :HD].astype(f32) + queries[:, :, HD:].astype(f32)) * (8 / LOG2E)
    query = query.astype(bf16).transpose(1, 0, 2)[None]
    key_rows, values = kv[None, :, :HD], kv[None, :, HD:]
    block_len = min(512, SEQ)
    block_count = SEQ // block_len
    logsums = logsums[:, 0, :] / LOG2E

    def block_scores(block_start, block_stop):
        scores = (
            jnp.einsum(
                "rqhd,rkd->rhqk",
                query[:, block_start:block_stop],
                key_rows[:, :block_stop],
                preferred_element_type=f32,
            )
            * 0.125
        )
        causal = jnp.arange(block_stop)[None, :] <= (block_start + jnp.arange(block_len))[:, None]
        return jnp.where(causal[None, None], scores, -jnp.inf)

    branch = jnp.dot(attended, out_w, preferred_element_type=f32) + jnp.dot(
        hidden, down_w, preferred_element_type=f32
    )
    mixed = (inputs + branch).astype(bf16)
    row_count = jnp.sum(onehot * counts[None, :], axis=1)
    row_weight = jnp.sum(onehot * subset_weights[None, :], axis=1)
    total_rows = rows_here * lax.axis_size("dp") * lax.axis_size("fsdp")
    row_scale = row_weight / row_count * (total_rows / SUBSETS)
    grad_out = (
        cotangent.astype(f32).reshape(rows_here, SEQ, D) * row_scale[:, None, None]
    ).reshape(token_count, D)
    grad_branch = grad_out.astype(bf16)
    grad_down = jnp.einsum("nf,nd->fd", hidden, grad_branch, preferred_element_type=f32)
    d_hidden = jnp.einsum("nd,fd->nf", grad_branch, down_w, preferred_element_type=f32)
    d_up = (d_hidden * slope.astype(f32)).astype(bf16)
    grad_up = jnp.einsum("nd,nf->df", second_in, d_up, preferred_element_type=f32)
    d_second = jnp.einsum("nf,df->nd", d_up, up_w, preferred_element_type=f32)
    grad_attn = jnp.einsum("nd,ne->de", attended, grad_branch, preferred_element_type=f32)
    d_attended = (
        jnp.einsum("ne,de->nd", grad_branch, out_w, preferred_element_type=f32)
        .astype(bf16)
        .reshape(rows_here, SEQ, H, HD)
    )
    query_grads = []
    d_keys = jnp.zeros((rows_here, SEQ, HD), f32)
    d_values = jnp.zeros((rows_here, SEQ, HD), f32)
    for block_number in range(block_count):
        block_start = block_number * block_len
        block_stop = block_start + block_len
        scores = block_scores(block_start, block_stop)
        prob_rows = jnp.exp(scores - logsums[None, :, block_start:block_stop, None])
        d_probs = jnp.einsum(
            "rqhd,rkd->rhqk",
            d_attended[:, block_start:block_stop],
            values[:, :block_stop],
            preferred_element_type=f32,
        )
        d_scores = (
            prob_rows * (d_probs - jnp.sum(d_probs * prob_rows, axis=-1, keepdims=True))
        ).astype(bf16)
        query_grads.append(
            jnp.einsum(
                "rhqk,rkd->rqhd", d_scores, key_rows[:, :block_stop], preferred_element_type=f32
            )
            * 0.125
        )
        d_keys = d_keys.at[:, :block_stop].add(
            jnp.einsum(
                "rhqk,rqhd->rkd",
                d_scores,
                query[:, block_start:block_stop],
                preferred_element_type=f32,
            )
            * 0.125
        )
        d_values = d_values.at[:, :block_stop].add(
            jnp.einsum(
                "rhqk,rqhd->rkd",
                prob_rows.astype(bf16),
                d_attended[:, block_start:block_stop],
                preferred_element_type=f32,
            )
        )
    d_query = jnp.concatenate(query_grads, axis=1)
    d_query = (
        unrotate(d_query, cos_table[:, None, :], sin_table[:, None, :])
        .reshape(token_count, D)
        .astype(bf16)
    )
    d_pair = (
        jnp.concatenate([unrotate(d_keys, cos_table, sin_table), d_values], axis=-1)
        .reshape(token_count, 2 * HD)
        .astype(bf16)
    )
    grad_query = jnp.einsum("nd,ne->de", first_in, d_query, preferred_element_type=f32)
    grad_pair = jnp.einsum("nd,ne->de", first_in, d_pair, preferred_element_type=f32)
    d_first = jnp.einsum("ne,de->nd", d_query, query_w, preferred_element_type=f32) + jnp.einsum(
        "ne,de->nd", d_pair, pair_w, preferred_element_type=f32
    )
    grad_gains = jnp.stack([jnp.sum(d_first * normed, axis=0), jnp.sum(d_second * normed, axis=0)])
    grad_biases = jnp.stack([jnp.sum(d_first, axis=0), jnp.sum(d_second, axis=0)])
    d_normed = d_first * gain_f[0] + d_second * gain_f[1]
    d_inputs = inv_std * (
        d_normed
        - jnp.mean(d_normed, axis=-1, keepdims=True)
        - normed * jnp.mean(d_normed * normed, axis=-1, keepdims=True)
    )
    grad_tokens = (grad_out + d_inputs).astype(bf16)
    small_g = jnp.pad(jnp.concatenate([grad_gains, grad_biases], axis=0).T, ((0, 0), (0, 124)))
    packed_g = jnp.concatenate([grad_query, grad_pair, small_g], axis=1)
    packed_g, out_g, up_g, down_g = send_grads(
        w_query.shape[0], w_down.shape[0], [packed_g, grad_attn, grad_up, grad_down]
    )
    small_g = packed_g[:, D + 2 * HD : D + 2 * HD + 4].T
    return (
        mixed,
        grad_tokens,
        packed_g[:, :D],
        packed_g[:, D : D + 2 * HD],
        out_g,
        up_g,
        down_g,
        small_g[:2],
        small_g[2:],
    )


def solution(mesh):
    in_specs = (
        P(("dp", "fsdp"), None),
        P(("dp", "fsdp"), None),
        P(("dp", "fsdp"), None),
        P(("dp", "fsdp"), None),
        P(("dp", "fsdp"), None),
        P(("dp", "fsdp"), None),
        P(None, ("dp", "fsdp")),
        P(None, ("dp", "fsdp")),
        P(("dp", "fsdp"), None),
        P(("dp", "fsdp")),
        P(),
    )
    out_specs = (
        P(("dp", "fsdp"), None),
        P(("dp", "fsdp"), None),
        P(("dp", "fsdp"), None),
        P(("dp", "fsdp"), None),
        P(("dp", "fsdp"), None),
        P(("dp", "fsdp"), None),
        P(("dp", "fsdp"), None),
        P(None, ("dp", "fsdp")),
        P(None, ("dp", "fsdp")),
    )
    return jax.shard_map(body, mesh=mesh, in_specs=in_specs, out_specs=out_specs, check_vma=False)
```

```python
import functools

import jax
import jax.numpy as jnp
import numpy as np
from jax import lax
from jax.experimental import pallas as pl
from jax.experimental.pallas import tpu as pltpu
from jax.sharding import PartitionSpec as P

D = 768
H = 12
HD = 64
ROT = 16
SUBSETS = 22
SEQ = 1024
PACK = 1024
TILE = 256
LOG2E = 1.4426950408889634
MESH = pl.DeviceIdType.MESH


eps_norm = 1e-05


def place():
    dp, fs = lax.axis_index("dp"), lax.axis_index("fsdp")
    return dp // 2, dp % 2, fs // 2, fs % 2


def device(z, x, y, c):
    return (z * 2 + x, y * 2 + c)


def partners():
    z, x, y, c = place()
    xa, ya = jnp.where(c == 0, 1 - x, x), jnp.where(c == 0, y, 1 - y)
    xb, yb = jnp.where(c == 0, x, 1 - x), jnp.where(c == 0, 1 - y, y)
    return xa, ya, xb, yb


def greet(lines):
    z, x, y, c = place()
    barrier = pltpu.get_barrier_semaphore()
    others = [device(lax.rem(z + d, lines), x, y, c) for d in range(1, lines)]
    others += [device(z, 1 - x, y, c), device(z, x, 1 - y, c), device(z, x, y, 1 - c)]
    for other in others:
        pl.semaphore_signal(barrier, inc=1, device_id=other, device_id_type=MESH)
    pl.semaphore_wait(barrier, len(others))


def remote(src, dst, send, recv, where):
    return pltpu.make_async_remote_copy(
        src_ref=src, dst_ref=dst, send_sem=send, recv_sem=recv, device_id=where, device_id_type=MESH
    )


def layout(rows, rows_down):
    blocks = [(1, 2 * rows, PACK), (1, 2 * rows, D), (1, 2 * rows, 4 * D), (2, rows_down, D)]
    return blocks


def pieces_of(blocks):
    (_, r0, _), (_, r1, _), (_, r2, _), (_, r3, _) = blocks
    up, third = D // 2, r3 // 3 // 16 * 16
    downs = [(0, third), (third, third), (2 * third, r3 - 2 * third)]
    return (
        [(0, 0, r0, 0, PACK // 2)]
        + [(2, 0, r2, k * up, up) for k in range(4)]
        + [(1, 0, r1, 0, D // 2)]
        + [(3, r, n, 0, D // 2) for r, n in downs]
    )


def lanes(start, size):
    return pl.ds(pl.multiple_of(start, 128), size)


def part(piece, halves, ref, z, x, y, c):
    t, r0, nr, c0, w = piece
    return ref.at[z, x, y, :, pl.ds(r0, nr), lanes(c * halves[t] + c0, w)]


class Gather:
    def __init__(self, lines, rows, blocks, sources, stages, whole, sems):
        self.lines, self.rows, self.blocks = lines, rows, blocks
        self.sources, self.stages, self.whole = sources, stages, whole
        self.swap_send, self.swap_recv, self.send, self.recv = sems
        self.pieces = pieces_of(blocks)
        self.halves = [b[2] // 2 for b in blocks]
        self.z, self.x, self.y, self.c = place()
        self.xa, self.ya, self.xb, self.yb = partners()
        self.sibling = device(self.z, self.x, self.y, 1 - self.c)
        self.started = []

    def go(self, make):
        make().start()
        self.started.append(make)

    def stage_rows(self, t, core):
        if self.blocks[t][0] == 2:
            return self.stages[t].at[core]
        return self.stages[t].at[0, pl.ds(pl.multiple_of(core * self.rows, 8), self.rows)]

    def swap(self, t):
        h = self.halves[t]
        return remote(
            self.sources[t].at[:, lanes((1 - self.c) * h, h)],
            self.stage_rows(t, self.c),
            self.swap_send.at[t],
            self.swap_recv.at[t],
            self.sibling,
        )

    def direct(self, p, d, received=False):
        z, n = self.z, self.lines
        at = lax.rem(z + n - d, n) if received else z
        block = part(self.pieces[p], self.halves, self.whole[self.pieces[p][0]], at, self.x, self.y, self.c)
        where = device(lax.rem(z + d, n), self.x, self.y, self.c)
        return remote(block, block, self.send.at[p, d - 1], self.recv.at[p, d - 1], where)

    def share(self, p, k, sx, sy, half, where):
        column = part(self.pieces[p], self.halves, self.whole[self.pieces[p][0]], slice(None), sx, sy, half)
        k = k + self.lines - 1
        return remote(column, column, self.send.at[p, k], self.recv.at[p, k], where)

    def begin(self):
        for t in (0, 2, 1, 3):
            self.go(functools.partial(self.swap, t))
        for t in (0, 2, 1, 3):
            h = self.halves[t]
            self.stage_rows(t, self.c)[...] = jnp.where(self.c == 0, self.sources[t][:, :h], self.sources[t][:, h:])
            self.swap(t).wait_recv()
            self.whole[t][self.z, self.x, self.y, :, :, lanes(self.c * h, h)] = self.stages[t][...].astype(jnp.bfloat16)
            for p, piece in enumerate(self.pieces):
                if piece[0] == t:
                    for d in range(1, self.lines):
                        self.go(functools.partial(self.direct, p, d))

    def first(self, p):
        for d in range(1, self.lines):
            self.direct(p, d, received=True).wait_recv()
        x, y, c, z = self.x, self.y, self.c, self.z
        self.go(lambda: self.share(p, 0, x, y, c, device(z, self.xa, self.ya, c)))
        self.go(lambda: self.share(p, 1, x, y, c, device(z, self.xb, self.yb, c)))
        self.go(lambda: self.share(p, 3, x, y, c, self.sibling))

    def second(self, p):
        c, z = self.c, self.z
        self.share(p, 0, self.xa, self.ya, c, self.sibling).wait_recv()
        self.go(lambda: self.share(p, 2, self.xa, self.ya, c, device(z, self.xb, self.yb, c)))
        self.go(lambda: self.share(p, 4, self.xa, self.ya, c, self.sibling))

    def third(self, p):
        x, y, c = self.x, self.y, self.c
        self.share(p, 1, self.xb, self.yb, c, self.sibling).wait_recv()
        self.go(lambda: self.share(p, 5, self.xb, self.yb, c, self.sibling))
        self.share(p, 2, 1 - x, 1 - y, c, self.sibling).wait_recv()
        self.go(lambda: self.share(p, 6, 1 - x, 1 - y, c, self.sibling))

    def fourth(self, p):
        x, y, c = self.x, self.y, 1 - self.c
        for k, sx, sy in ((3, x, y), (4, self.xb, self.yb), (5, self.xa, self.ya), (6, 1 - x, 1 - y)):
            self.share(p, k, sx, sy, c, self.sibling).wait_recv()

    def events(self):
        count, order = len(self.pieces), []
        for s in range(count + 3):
            for k, step in enumerate((self.first, self.second, self.third, self.fourth)):
                if 0 <= s - k < count:
                    order.append((functools.partial(step, s - k), (k, s - k)))
        cut = order.index(next(o for o in order if o[1] == (3, 0))) + 1
        return order[:cut], order[cut:]


def spread(events, slots):
    plan = [[] for _ in range(slots)]
    for k, event in enumerate(events):
        plan[k * slots // max(len(events), 1)].append(event)
    return plan


def run_at(index, values):
    for value, events in values:
        if events:

            @pl.when(index == value)
            def _(events=events):
                for event in events:
                    event()


def columns(ref, start, size):
    return ref[:, :, :, :, :, pl.ds(start, size)].reshape(-1, size)


def turned(a, b):
    return lax.dot_general(a, b, (((1,), (1,)), ((), ())), preferred_element_type=jnp.float32)


def swapped(block, cosine, sine):
    lane = lax.broadcasted_iota(jnp.int32, block.shape, 1)
    other = jnp.where(lane % 16 < 8, pltpu.roll(block, 120, 1), pltpu.roll(block, 8, 1))
    return block * cosine + other * sine


def forward_kernel(lines, rows, blocks, linked, *refs):
    f32, bf16 = jnp.float32, jnp.bfloat16
    tokens, cosine, sine = refs[:3]
    given = refs[3:11] if linked else refs[3:7]
    refs = refs[11:] if linked else refs[7:]
    results, refs = refs[: 9 + 4 * linked], refs[9 + 4 * linked :]
    small, first_in, second_in, queries, kv, attended, logsums, hidden, slope, *rest = refs
    normed, keys, values_t, mask, out_sems, *rest = rest
    held = [small, first_in, second_in, queries, kv, attended, logsums, hidden, slope]
    flushed = []

    def flush(*which):
        for k in which:
            copy = pltpu.make_async_copy(held[k], results[k], out_sems.at[k])
            copy.start()
            flushed.append(copy)

    if linked:
        query, pair, out, up, down, gains, biases, tags = given
        whole, packed, stages, sems, square = rest[:4], rest[4], rest[5:9], rest[9:13], rest[13]
        held += whole
        packed[:, :D] = query[...]
        packed[:, D : D + 2 * HD] = pair[...]
        square[...] = jnp.zeros_like(square)
        square[0:2, 0:rows] = gains[...]
        square[2:4, 0:rows] = biases[...]
        spot = lax.broadcasted_iota(jnp.int32, (rows, 128), 1) == tags[0] + 4
        spot = jnp.where(lax.broadcasted_iota(jnp.int32, (rows, 128), 0) == 0, spot.astype(f32), 0.0)
        packed[:, D + 2 * HD :] = square[...].T[:rows] + spot
        greet(lines)
        gather = Gather(lines, rows, blocks, [packed, out, up, down], stages, whole, sems)
        gather.begin()
        urgent, later = gather.events()
        cut = later.index(next(e for e in later if e[1] == (3, 4))) + 1
        early, late = [e[0] for e in later[:cut]], [e[0] for e in later[cut:]]
    else:
        whole, early, late = given, [], []
    packed_w, up_w = whole[0], whole[2]

    row = lax.broadcasted_iota(jnp.int32, (TILE, TILE), 0)
    column = lax.broadcasted_iota(jnp.int32, (TILE, TILE), 1)
    mask[...] = jnp.where(row <= column, 0.0, -1e30)
    tiles = SEQ // TILE

    def tile(k):
        return pl.ds(pl.multiple_of(k * TILE, TILE), TILE)

    @pl.loop(0, tiles)
    def _(k):
        inputs = tokens[tile(k), :].astype(f32)
        centred = inputs - jnp.mean(inputs, axis=-1, keepdims=True)
        normed[tile(k), :] = centred * lax.rsqrt(jnp.mean(centred * centred, axis=-1, keepdims=True) + eps_norm)

    if linked:
        for event, _ in urgent:
            event()
    small[...] = columns(packed_w, D + 2 * HD, 128).astype(f32).T
    plan = spread(early, 28)

    @pl.loop(0, tiles)
    def _(k):
        norm = normed[tile(k), :]
        a1 = (norm * small[0:1, :] + small[2:3, :]).astype(bf16)
        first_in[tile(k), :] = a1
        second_in[tile(k), :] = (norm * small[1:2, :] + small[3:4, :]).astype(bf16)
        mixed = jnp.dot(a1, columns(packed_w, 0, D + 2 * HD), preferred_element_type=f32)
        cos_t, sin_t = cosine[tile(k), :], sine[tile(k), :]
        left = lax.broadcasted_iota(jnp.int32, (TILE, 2 * HD), 1) < HD
        for p in range(H // 2):
            turn = swapped(mixed[:, 2 * HD * p : 2 * HD * (p + 1)], cos_t, sin_t).astype(bf16).astype(f32)
            turn = turn * (LOG2E / 8)
            high = turn.astype(bf16).astype(f32)
            low = turn - high
            queries[2 * p, tile(k), :] = jnp.where(left, high, pltpu.roll(low, HD, 1)).astype(bf16)
            queries[2 * p + 1, tile(k), :] = jnp.where(left, pltpu.roll(high, HD, 1), low).astype(bf16)
        pair_t = mixed[:, D : D + 2 * HD]
        pair_t = jnp.where(left, swapped(pair_t, cos_t, sin_t), pair_t).astype(bf16).astype(f32)
        kv[tile(k), :] = pair_t.astype(bf16)
        other = pltpu.roll(pair_t, HD, 1)
        keys[tile(k), :] = jnp.where(left, pair_t, other).astype(bf16)
        lane = lax.broadcasted_iota(jnp.int32, (TILE, 2 * HD), 1)
        ones = jnp.where(lane == HD, 1.0, 0.0)
        values_t[:, tile(k)] = jnp.where(left, other, ones).T.astype(bf16)
        run_at(k, [(v, plan[v]) for v in range(tiles)])

    flush(0, 1, 2, 3, 4)
    plan = plan[tiles:]

    @pl.loop(0, H // 2)
    def _(pr):
        for i in range(tiles):
            count = TILE * (i + 1)
            heads = []
            for hh in range(2):
                head = pr * 2 + hh
                scores = turned(keys[0:count, :], queries[head, i * TILE : count, :])
                last = scores[count - TILE :] + mask[...]
                peak = jnp.max(last, axis=0, keepdims=True)
                if i:
                    peak = jnp.maximum(peak, jnp.max(scores[: count - TILE], axis=0, keepdims=True))
                probs = jnp.exp2(last - peak).astype(bf16)
                if i:
                    probs = jnp.concatenate([jnp.exp2(scores[: count - TILE] - peak).astype(bf16), probs], axis=0)
                got = jnp.dot(values_t[:, 0:count], probs, preferred_element_type=f32)
                total = got[HD : HD + 1]
                heads.append(got[:HD] * (1.0 / total))
                logsums[head, :, i * TILE : count] = peak + jnp.log2(total)
            both = jnp.concatenate(heads, axis=0).T
            attended[i * TILE : count, lanes(pr * 2 * HD, 2 * HD)] = both.astype(bf16)
            run_at(pr, [(v, plan[v * tiles + i]) for v in range(H // 2)])

    flush(5, 6)
    plan = spread(late, 4 * tiles)

    @pl.loop(0, 4 * tiles)
    def _(s):
        chunk, k = s // tiles, s % tiles
        pre = jnp.dot(second_in[tile(k), :], columns(up_w, pl.multiple_of(chunk * D, D), D), preferred_element_type=f32)
        cdf = 0.5 + 0.5 * lax.erf(pre * 0.7071067811865476)
        hidden[tile(k), lanes(chunk * D, D)] = (pre * cdf).astype(bf16)
        density = jnp.exp2(pre * pre * (-0.5 * LOG2E)) * 0.3989422804014327
        slope[tile(k), lanes(chunk * D, D)] = (cdf + pre * density).astype(bf16)
        run_at(s, [(v, plan[v]) for v in range(4 * tiles)])

    flush(7, 8)
    if linked:
        flush(9, 10, 11, 12)
        for make in gather.started:
            make().wait_send()
    for copy in flushed:
        copy.wait()


def tables():
    half = ROT // 2
    inverse = np.float32(10000.0) ** (-(np.arange(half, dtype=np.float32) * 2) / ROT)
    phase = np.arange(SEQ, dtype=np.float32)[:, None] * inverse.astype(np.float32)[None, :]
    cos_t, sin_t = np.cos(phase.astype(np.float64)), np.sin(phase.astype(np.float64))
    rest = np.zeros((SEQ, HD - ROT))
    cosine = np.concatenate([cos_t, cos_t, rest + 1.0] * 2, axis=1)
    sine = np.concatenate([-sin_t, sin_t, rest] * 2, axis=1)
    return jnp.asarray(cosine.astype(np.float32)), jnp.asarray(sine.astype(np.float32))


def forward(linked, lines, rows, rows_down, tokens, cosine, sine, weights):
    blocks = layout(rows, rows_down)
    f32, bf16 = jnp.float32, jnp.bfloat16
    shapes = [(lines, 2, 2, g, r, k) for g, r, k in blocks]
    if not linked:
        weights = [a.reshape(shape) for a, shape in zip(weights, shapes)]
    held = [
        ((128, D), f32),
        ((SEQ, D), bf16),
        ((SEQ, D), bf16),
        ((H, SEQ, 2 * HD), bf16),
        ((SEQ, 2 * HD), bf16),
        ((SEQ, D), bf16),
        ((H, 1, SEQ), f32),
        ((SEQ, 4 * D), bf16),
        ((SEQ, 4 * D), bf16),
    ]
    scratch = [pltpu.VMEM(shape, kind) for shape, kind in held]
    scratch += [
        pltpu.VMEM((SEQ, D), f32),
        pltpu.VMEM((SEQ, 2 * HD), bf16),
        pltpu.VMEM((2 * HD, SEQ), bf16),
        pltpu.VMEM((TILE, TILE), f32),
        pltpu.SemaphoreType.DMA((13,)),
    ]
    if linked:
        held += [(shape, bf16) for shape in shapes]
        scratch += [pltpu.VMEM(shape, bf16) for shape in shapes]
        scratch += [pltpu.VMEM((rows, PACK), f32)]
        scratch += [pltpu.VMEM((g, r, k // 2), f32) for g, r, k in blocks]
        count, kinds = len(pieces_of(blocks)), lines + 6
        scratch += [pltpu.SemaphoreType.DMA((4,))] * 2 + [pltpu.SemaphoreType.DMA((count, kinds))] * 2
        scratch += [pltpu.VMEM((128, 128), f32)]
    specs = [pl.BlockSpec(memory_space=pltpu.VMEM)] * (3 + len(weights))
    if linked:
        specs[-1] = pl.BlockSpec(memory_space=pltpu.SMEM)
    got = pl.pallas_call(
        functools.partial(forward_kernel, lines, rows, blocks, linked),
        out_shape=[jax.ShapeDtypeStruct(shape, kind) for shape, kind in held],
        in_specs=specs,
        out_specs=[pl.BlockSpec(memory_space=pl.ANY)] * len(held),
        scratch_shapes=scratch,
        compiler_params=pltpu.CompilerParams(
            collective_id=0 if linked else None, has_side_effects=linked, vmem_limit_bytes=60 * 2**20
        ),
        name="forward",
    )(tokens, cosine, sine, *weights)
    return got[:9], list(got[9:]) if linked else weights


def scatter_pieces(blocks):
    (_, r0, _), (_, r1, _), (_, r2, _), (_, r3, _) = blocks
    w, half = D // 2, r3 // 2 // 16 * 16
    return (
        [(1, 0, r1, 0, w)]
        + [(2, 0, r2, k * w, w) for k in range(4)]
        + [(3, 0, half, 0, w), (3, half, r3 - half, 0, w), (0, 0, r0, 0, PACK // 2)]
    )


SLOTS = 2


class Scatter:
    def __init__(self, lines, rows, blocks, grads, outs, buffers, sems):
        self.lines, self.rows, self.blocks = lines, rows, blocks
        self.grads, self.outs = grads, outs
        self.near, self.near_last = buffers[0:2]
        self.from_b, self.from_a, self.from_z, self.total, self.last = (buffers[2 + 4 * k : 6 + 4 * k] for k in range(5))
        self.send, self.recv, self.credit = sems
        self.pieces = scatter_pieces(blocks)
        self.halves = [b[2] // 2 for b in blocks]
        self.z, self.x, self.y, self.c = place()
        self.xa, self.ya, self.xb, self.yb = partners()
        self.sibling = device(self.z, self.x, self.y, 1 - self.c)
        self.started = []

    def go(self, make):
        make().start()
        self.started.append(make)

    def cut(self, p, ref, *lead):
        t, r0, nr, c0, w = self.pieces[p]
        return ref[t].at[(*lead, slice(None), pl.ds(r0, nr), pl.ds(c0, w))]

    def grad(self, p, z, x, y, half=None):
        half = self.c if half is None else half
        return part(self.pieces[p], self.halves, self.grads[self.pieces[p][0]], z, x, y, half)

    def near_at(self, p):
        t, r0, nr, c0, w = self.pieces[p]
        if t == 0:
            return self.near_last
        return self.near.at[p % SLOTS, :, :, :, pl.ds(0, self.blocks[t][0]), pl.ds(0, nr), pl.ds(0, w)]

    def near_copy(self, p):
        every = slice(None)
        mine = self.grad(p, every, every, every, 1 - self.c)
        return remote(mine, self.near_at(p), self.send.at[p, 0], self.recv.at[p, 0], self.sibling)

    def b_copy(self, p, k):
        at = (self.xb, self.yb) if k == 0 else (1 - self.x, 1 - self.y)
        return remote(
            self.grad(p, slice(None), *at),
            self.cut(p, self.from_b, k, slice(None)),
            self.send.at[p, 1 + k],
            self.recv.at[p, 1 + k],
            device(self.z, self.xb, self.yb, self.c),
        )

    def a_copy(self, p):
        return remote(
            self.grad(p, slice(None), self.xa, self.ya),
            self.cut(p, self.from_a, slice(None)),
            self.send.at[p, 3],
            self.recv.at[p, 3],
            device(self.z, self.xa, self.ya, self.c),
        )

    def z_copy(self, p, d):
        other = lax.rem(self.z + d, self.lines)
        return remote(
            self.grad(p, other, self.x, self.y),
            self.cut(p, self.from_z, d - 1),
            self.send.at[p, 3 + d],
            self.recv.at[p, 3 + d],
            device(other, self.x, self.y, self.c),
        )

    def last_copy(self, p):
        t, r0, nr, c0, w = self.pieces[p]
        if self.blocks[t][0] == 2:
            src = self.total[t].at[1 - self.c, pl.ds(r0, nr), pl.ds(c0, w)]
            dst = self.last[t].at[pl.ds(r0, nr), pl.ds(c0, w)]
        else:
            away = pl.ds(pl.multiple_of((1 - self.c) * self.rows, 8), self.rows)
            src = self.total[t].at[0, away, pl.ds(c0, w)]
            dst = self.last[t].at[:, pl.ds(c0, w)]
        k = 3 + self.lines
        return remote(src, dst, self.send.at[p, k], self.recv.at[p, k], self.sibling)

    def first(self, p):
        if SLOTS <= p < len(self.pieces) - 1:
            pl.semaphore_wait(self.credit, 1)
        self.go(lambda: self.near_copy(p))

    def second(self, p):
        self.near_copy(p).wait_recv()
        near = self.near_at(p)

        @pl.loop(0, self.lines)
        def _(k):
            for x in range(2):
                for y in range(2):
                    kept = self.grad(p, k, x, y)
                    kept[...] = (kept[...].astype(jnp.float32) + near[k, x, y].astype(jnp.float32)).astype(jnp.bfloat16)

        if p + SLOTS < len(self.pieces) - 1:
            pl.semaphore_signal(self.credit, inc=1, device_id=self.sibling, device_id_type=MESH)
        self.go(lambda: self.b_copy(p, 1))
        self.go(lambda: self.b_copy(p, 0))

    def third(self, p):
        self.b_copy(p, 1).wait_recv()

        @pl.loop(0, self.lines)
        def _(k):
            kept, got = self.grad(p, k, self.xa, self.ya), self.cut(p, self.from_b, 1, k)
            kept[...] = (kept[...].astype(jnp.float32) + got[...].astype(jnp.float32)).astype(jnp.bfloat16)

        self.go(lambda: self.a_copy(p))

    def mine(self, p, k):
        got = self.cut(p, self.from_b, 0, k)[...].astype(jnp.float32) + self.cut(p, self.from_a, k)[...].astype(jnp.float32)
        return self.grad(p, k, self.x, self.y)[...].astype(jnp.float32) + got

    def fourth(self, p):
        self.b_copy(p, 0).wait_recv()
        self.a_copy(p).wait_recv()

        @pl.loop(1, self.lines)
        def _(d):
            k = lax.rem(self.z + d, self.lines)
            self.grad(p, k, self.x, self.y)[...] = self.mine(p, k).astype(jnp.bfloat16)

        for d in range(1, self.lines):
            self.go(functools.partial(self.z_copy, p, d))
        self.cut(p, self.total)[...] = self.mine(p, self.z)

    def fifth(self, p):
        for d in range(1, self.lines):
            self.z_copy(p, d).wait_recv()
        total = self.cut(p, self.total)
        acc = total[...]
        for d in range(1, self.lines):
            acc = acc + self.cut(p, self.from_z, d - 1)[...].astype(jnp.float32)
        total[...] = acc
        self.go(lambda: self.last_copy(p))

    def sixth(self, p):
        t, r0, nr, c0, w = self.pieces[p]
        self.last_copy(p).wait_recv()
        if self.blocks[t][0] == 2:
            kept = self.total[t][self.c, r0 : r0 + nr, c0 : c0 + w]
            got = self.last[t][r0 : r0 + nr, c0 : c0 + w]
            to = slice(r0, r0 + nr)
        else:
            kept = self.total[t][0, pl.ds(pl.multiple_of(self.c * self.rows, 8), self.rows), c0 : c0 + w]
            got = self.last[t][:, c0 : c0 + w]
            to = slice(None)
        h = self.halves[t]
        self.outs[t][to, c0 : c0 + w] = jnp.where(self.c == 0, kept, got)
        self.outs[t][to, h + c0 : h + c0 + w] = jnp.where(self.c == 0, got, kept)

    def steps(self):
        return [self.first, self.second, self.third, self.fourth, self.fifth, self.sixth]

    def events(self):
        count, steps = len(self.pieces) - 1, self.steps()
        return [
            [functools.partial(step, s - k) for k, step in enumerate(steps) if 0 <= s - k < count]
            for s in range(count + len(steps) - 1)
        ]


def crossed(a, b):
    return lax.dot_general(a, b, (((0,), (0,)), ((), ())), preferred_element_type=jnp.float32)


def backward_kernel(lines, rows, blocks, linked, total_rows, *refs):
    f32, bf16 = jnp.float32, jnp.bfloat16
    tags, subset_w, cosine, sine = refs[:4]
    (tokens_h, cotan_h, small_h, first_h, second_h, queries_h, kv_h, attended_h, logsums_h, hidden_h, slope_h) = refs[4:15]
    packed_h, out_h, up_h, down_h = refs[15:19]
    mixed_h, grad_tokens_h = refs[19:21]
    results, refs = refs[21:25], refs[25:]
    (tokens, cotan, small, ins, queries, kv, attended, logsums, hidden, slope, packed_w, out_w, up_w, down_w) = refs[:14]
    (branch, d_second, scaled, d_heads, keys, keys_t, values, d_keys, d_values, d_pair, mask, sums) = refs[14:26]
    grads, load_sems, chunk_sems, out_sems = refs[26:30], refs[30], refs[31], refs[32]
    refs = refs[33:]
    tiles, wide = SEQ // TILE, D // 2
    qkv = D + 2 * HD

    def tile(k):
        return pl.ds(pl.multiple_of(k * TILE, TILE), TILE)

    def load(k, src, dst):
        return pltpu.make_async_copy(src, dst, load_sems.at[k])

    loads = [
        load(0, small_h, small),
        load(1, cotan_h, cotan),
        load(2, out_h, out_w),
        load(3, tokens_h, tokens),
        load(4, attended_h, attended),
        load(5, second_h, ins),
        load(6, kv_h, kv),
        load(7, logsums_h, logsums),
        load(8, queries_h, queries),
        load(9, packed_h, packed_w),
    ]

    def chunk_of(j):
        return (j % 2) * 2 + j // 2

    def chunk_loads(j):
        q, slot = chunk_of(j), j % 2
        cols = lanes(q * D, D)
        pairs = [
            (hidden_h.at[:, cols], hidden.at[slot]),
            (slope_h.at[:, cols], slope.at[slot]),
            (up_h.at[:, :, :, :, :, cols], up_w.at[slot]),
            (down_h.at[q], down_w.at[slot]),
        ]
        return [pltpu.make_async_copy(a, b, chunk_sems.at[slot, k]) for k, (a, b) in enumerate(pairs)]

    for copy in loads[:5]:
        copy.start()
    for copy in chunk_loads(0):
        copy.start()
    for copy in loads[5:]:
        copy.start()
    if linked:
        greet(lines)
        scatter = Scatter(lines, rows, blocks, grads, results, refs[:22], refs[22:25])
        turns = scatter.events()
    else:
        scatter, turns = None, []

    def turn(a, b):
        return [event for events in turns[a:b] for event in events]

    row = lax.broadcasted_iota(jnp.int32, (TILE, TILE), 0)
    column = lax.broadcasted_iota(jnp.int32, (TILE, TILE), 1)
    mask[...] = jnp.where(row <= column, 0.0, -1e30)
    sums[...] = jnp.zeros_like(sums)
    d_keys[...] = jnp.zeros_like(d_keys)
    d_values[...] = jnp.zeros_like(d_values)
    lane = lax.broadcasted_iota(jnp.int32, (TILE, 2 * HD), 1)
    left = lane < HD

    for copy in loads[:5]:
        copy.wait()
    kind = lax.broadcasted_iota(jnp.int32, (128, D), 0)
    count = jnp.sum(jnp.where(kind == tags[0] + 4, small[...], 0.0), keepdims=True)
    subset = lax.broadcasted_iota(jnp.int32, subset_w.shape, 1)
    weight = jnp.sum(jnp.where(subset == tags[0], subset_w[...], 0.0), keepdims=True)
    scale = weight / count * (total_rows / SUBSETS)

    @pl.loop(0, tiles)
    def _(k):
        grad_out = (cotan[tile(k), :].astype(f32) * scale).astype(bf16)
        scaled[tile(k), :] = grad_out
        heads = attended[tile(k), :]
        out_m = out_w[...].reshape(D, D)
        branch[tile(k), :] = tokens[tile(k), :].astype(f32) + jnp.dot(heads, out_m, preferred_element_type=f32)
        d_heads_t = turned(grad_out, out_m).astype(bf16).astype(f32)
        for p in range(H // 2):
            block = d_heads_t[:, 2 * HD * p : 2 * HD * (p + 1)]
            product = block * heads[:, 2 * HD * p : 2 * HD * (p + 1)].astype(f32)
            for hh, (mine, there) in enumerate(((left, block), (~left, pltpu.roll(block, HD, 1)))):
                delta = jnp.sum(jnp.where(mine, product, 0.0), axis=1, keepdims=True)
                high = delta.astype(bf16).astype(f32)
                extra = jnp.where(lane == HD, high, jnp.where(lane == HD + 1, delta - high, 0.0))
                d_heads[2 * p + hh, tile(k), :] = jnp.where(left, there, extra).astype(bf16)

    @pl.loop(0, 2)
    def _(k):
        got = crossed(attended[:, lanes(k * wide, wide)], scaled[...]).astype(bf16)
        grads[1][pl.ds(2 * k, 2)] = got.reshape(2, 2, 2, 1, D // 16, D)

    for event in turn(0, 1):
        event()
    loads[5].wait()

    @pl.loop(0, 4)
    def _(j):
        slot, q = j % 2, chunk_of(j)
        for copy in chunk_loads(j):
            copy.wait()

        @pl.when(j < 3)
        def _():
            for copy in chunk_loads(j + 1):
                copy.start()

        run_at(j, [(2, turn(1, 2)), (3, turn(2, 3))])
        down_m, up_m = down_w[slot].reshape(D, D), up_w[slot].reshape(D, D)

        @pl.loop(0, tiles)
        def _(k):
            branch[tile(k), :] += jnp.dot(hidden[slot, tile(k), :], down_m, preferred_element_type=f32)
            d_hidden = turned(scaled[tile(k), :], down_m)
            d_up = (d_hidden * slope[slot, tile(k), :].astype(f32)).astype(bf16)
            slope[slot, tile(k), :] = d_up
            got = turned(d_up, up_m)
            d_second[tile(k), :] = jnp.where(j == 0, got, got + d_second[tile(k), :])

        @pl.loop(0, 2)
        def _(k):
            got = crossed(hidden[slot, :, lanes(k * wide, wide)], scaled[...]).astype(bf16)
            grads[3][q, k] = got.reshape(2, 2, 4 * D // 32, D)
            got = crossed(ins[:, lanes(k * wide, wide)], slope[slot]).astype(bf16)
            grads[2][pl.ds(2 * k, 2), :, :, :, :, lanes(q * D, D)] = got.reshape(2, 2, 2, 1, D // 16, D)

    copy_first = load(5, first_h, ins)
    copy_first.start()

    @pl.loop(0, tiles)
    def _(k):
        attended[tile(k), :] = branch[tile(k), :].astype(bf16)

    flushed = [pltpu.make_async_copy(attended, mixed_h, out_sems.at[0])]
    flushed[0].start()
    for copy in loads[6:9]:
        copy.wait()

    @pl.loop(0, tiles)
    def _(k):
        pair_t = kv[tile(k), :].astype(f32)
        other = pltpu.roll(pair_t, HD, 1)
        both = jnp.where(left, pair_t, other)
        keys[tile(k), :] = both.astype(bf16)
        keys_t[:, tile(k)] = both.T[:HD].astype(bf16)
        ones = jnp.where(lane < HD + 2, -1.0, 0.0)
        values[tile(k), :] = jnp.where(left, other, ones).astype(bf16)

    plan = spread(turn(3, len(turns)), 6 * tiles)

    @pl.loop(0, H // 2)
    def _(pr):
        for i in range(tiles):
            count = TILE * (i + 1)
            span = slice(i * TILE, count)
            probs_all, d_scores_all, d_query = [], [], []
            for hh in range(2):
                head = pr * 2 + hh
                scores = turned(keys[0:count, :], queries[head, span, :])
                shift = logsums[head, :, span]
                probs = jnp.exp2(scores[count - TILE :] + mask[...] - shift)
                if i:
                    probs = jnp.concatenate([jnp.exp2(scores[: count - TILE] - shift), probs], axis=0)
                d_probs = turned(values[0:count, :], d_heads[head, span, :])
                d_scores = (probs * d_probs).astype(bf16)
                probs_all.append(probs.astype(bf16))
                d_scores_all.append(d_scores)
                d_query.append(jnp.dot(keys_t[:, 0:count], d_scores, preferred_element_type=f32))
            for acc, parts, other in ((d_values, probs_all, d_heads), (d_keys, d_scores_all, queries)):
                two = jnp.concatenate([other[pr * 2, span, :], other[pr * 2 + 1, span, :]], axis=0)
                acc[0:count, :] += jnp.dot(jnp.concatenate(parts, axis=1), two, preferred_element_type=f32)
            d_q = jnp.concatenate(d_query, axis=0).T * 0.125
            d_q = swapped(d_q, cosine[span, :], -sine[span, :])
            scaled[span, lanes(pr * 2 * HD, 2 * HD)] = d_q.astype(bf16)
            run_at(pr, [(v, plan[v * tiles + i]) for v in range(H // 2)])

    copy_first.wait()
    loads[9].wait()

    @pl.loop(0, tiles)
    def _(k):
        d_key = d_keys[tile(k), :]
        d_key = (d_key + pltpu.roll(d_key, HD, 1)) * (1.0 / LOG2E)
        d_key = swapped(d_key, cosine[tile(k), :], -sine[tile(k), :])
        d_pair[tile(k), :] = jnp.where(left, d_key, pltpu.roll(d_values[tile(k), :], HD, 1)).astype(bf16)
        inputs = tokens[tile(k), :].astype(f32)
        centred = inputs - jnp.mean(inputs, axis=-1, keepdims=True)
        norm = centred * lax.rsqrt(jnp.mean(centred * centred, axis=-1, keepdims=True) + eps_norm)
        both = jnp.concatenate([scaled[tile(k), :], d_pair[tile(k), :]], axis=1)
        d_first = turned(both, columns(packed_w, 0, qkv))
        branch[tile(k), :] = d_first
        second = d_second[tile(k), :]
        for n, value in enumerate((d_first * norm, second * norm, d_first, second)):
            sums[n : n + 1, :] += jnp.sum(value, axis=0, keepdims=True)

    @pl.loop(0, 2)
    def _(k):
        side = ins[:, lanes(k * wide, wide)]
        got = crossed(side, scaled[...]).astype(bf16)
        grads[0][pl.ds(2 * k, 2), :, :, :, :, 0:D] = got.reshape(2, 2, 2, 1, D // 16, D)
        got = crossed(side, d_pair[...]).astype(bf16)
        grads[0][pl.ds(2 * k, 2), :, :, :, :, D:qkv] = got.reshape(2, 2, 2, 1, D // 16, 2 * HD)

    grads[0][:, :, :, :, :, qkv:PACK] = sums[...].T.astype(bf16).reshape(4, 2, 2, 1, D // 16, 128)
    if linked:
        steps = scatter.steps()
        last = [functools.partial(step, len(scatter.pieces) - 1) for step in steps]
    else:
        last = []
    plan = spread(last[1:3], tiles)
    for event in last[:1]:
        event()

    @pl.loop(0, tiles)
    def _(k):
        inputs = tokens[tile(k), :].astype(f32)
        centred = inputs - jnp.mean(inputs, axis=-1, keepdims=True)
        inv_std = lax.rsqrt(jnp.mean(centred * centred, axis=-1, keepdims=True) + eps_norm)
        norm = centred * inv_std
        d_normed = branch[tile(k), :] * small[0:1, :] + d_second[tile(k), :] * small[1:2, :]
        inner = jnp.mean(d_normed * norm, axis=-1, keepdims=True)
        d_inputs = inv_std * (d_normed - jnp.mean(d_normed, axis=-1, keepdims=True) - norm * inner)
        cotan[tile(k), :] = (cotan[tile(k), :].astype(f32) * scale + d_inputs).astype(bf16)
        run_at(k, [(v, plan[v]) for v in range(tiles)])

    flushed.append(pltpu.make_async_copy(cotan, grad_tokens_h, out_sems.at[1]))
    flushed[-1].start()
    for event in last[3:]:
        event()
    if linked:
        for make in scatter.started:
            make().wait_send()
    else:
        for t in range(4):
            flushed.append(pltpu.make_async_copy(grads[t], results[t], out_sems.at[2 + t]))
            flushed[-1].start()
    for copy in flushed:
        copy.wait()


def backward(linked, lines, rows, rows_down, total_rows, tags, subset_w, cosine, sine, tokens, cotan, kept, whole):
    blocks = layout(rows, rows_down)
    f32, bf16 = jnp.float32, jnp.bfloat16
    shapes = [(lines, 2, 2, g, r, k) for g, r, k in blocks]
    own_rows = [r if g == 2 else rows for g, r, k in blocks]
    vmem = pl.BlockSpec(memory_space=pltpu.VMEM)
    anywhere = pl.BlockSpec(memory_space=pl.ANY)
    if linked:
        results = [jax.ShapeDtypeStruct((o, k), f32) for o, (g, r, k) in zip(own_rows, blocks)]
    else:
        results = [jax.ShapeDtypeStruct(shape, bf16) for shape in shapes]
    tall = (SEQ, D)
    scratch = [
        pltpu.VMEM(tall, bf16),
        pltpu.VMEM(tall, bf16),
        pltpu.VMEM((128, D), f32),
        pltpu.VMEM(tall, bf16),
        pltpu.VMEM((H, SEQ, 2 * HD), bf16),
        pltpu.VMEM((SEQ, 2 * HD), bf16),
        pltpu.VMEM(tall, bf16),
        pltpu.VMEM((H, 1, SEQ), f32),
        pltpu.VMEM((2, *tall), bf16),
        pltpu.VMEM((2, *tall), bf16),
        pltpu.VMEM(shapes[0], bf16),
        pltpu.VMEM(shapes[1], bf16),
        pltpu.VMEM((2, *shapes[2][:-1], D), bf16),
        pltpu.VMEM((2, *shapes[3][1:]), bf16),
        pltpu.VMEM(tall, f32),
        pltpu.VMEM(tall, f32),
        pltpu.VMEM(tall, bf16),
        pltpu.VMEM((H, SEQ, 2 * HD), bf16),
        pltpu.VMEM((SEQ, 2 * HD), bf16),
        pltpu.VMEM((HD, SEQ), bf16),
        pltpu.VMEM((SEQ, 2 * HD), bf16),
        pltpu.VMEM((SEQ, 2 * HD), f32),
        pltpu.VMEM((SEQ, 2 * HD), f32),
        pltpu.VMEM((SEQ, 2 * HD), bf16),
        pltpu.VMEM((TILE, TILE), f32),
        pltpu.VMEM((128, D), f32),
    ]
    scratch += [pltpu.VMEM(shape, bf16) for shape in shapes]
    scratch += [pltpu.SemaphoreType.DMA((10,)), pltpu.SemaphoreType.DMA((2, 4)), pltpu.SemaphoreType.DMA((6,))]
    if linked:
        pieces = scatter_pieces(blocks)
        tallest = max(p[2] for p in pieces if p[0] == 3)
        scratch += [pltpu.VMEM((SLOTS, lines, 2, 2, 2, max(tallest, 2 * rows), D // 2), bf16)]
        scratch += [pltpu.VMEM((lines, 2, 2, 1, 2 * rows, PACK // 2), bf16)]
        for lead in ((2, lines), (lines,), (lines - 1,)):
            scratch += [pltpu.VMEM((*lead, g, r, k // 2), bf16) for g, r, k in blocks]
        scratch += [pltpu.VMEM((g, r, k // 2), f32) for g, r, k in blocks]
        scratch += [pltpu.VMEM((o, k // 2), f32) for o, (g, r, k) in zip(own_rows, blocks)]
        scratch += [pltpu.SemaphoreType.DMA((len(pieces), lines + 4))] * 2 + [pltpu.SemaphoreType.REGULAR]
    return pl.pallas_call(
        functools.partial(backward_kernel, lines, rows, blocks, linked, total_rows),
        out_shape=[jax.ShapeDtypeStruct(tall, bf16)] * 2 + results,
        in_specs=[pl.BlockSpec(memory_space=pltpu.SMEM)] + [vmem] * 3 + [anywhere] * 15,
        out_specs=[anywhere] * 2 + [vmem if linked else anywhere] * 4,
        scratch_shapes=scratch,
        compiler_params=pltpu.CompilerParams(
            collective_id=1 if linked else None, has_side_effects=linked, vmem_limit_bytes=63 * 2**20
        ),
        name="backward",
    )(tags, subset_w, cosine, sine, tokens, cotan, *kept, *whole)


def finish_kernel(rows, *refs):
    packed, *rest = refs[:5]
    query, pair, gains, biases, *to = refs[5:]
    query[...] = packed[:, :D]
    pair[...] = packed[:, D : D + 2 * HD]
    turned_back = packed[:, D + 2 * HD :].T
    gains[...] = turned_back[0:2]
    biases[...] = turned_back[2:4]
    for a, b in zip(rest, to):
        b[...] = a[...]


def finish(rows, packed, *rest):
    f32 = jnp.float32
    vmem = pl.BlockSpec(memory_space=pltpu.VMEM)
    shapes = [(rows, D), (rows, 2 * HD), (2, rows), (2, rows)]
    return pl.pallas_call(
        functools.partial(finish_kernel, rows),
        out_shape=[jax.ShapeDtypeStruct(a, f32) for a in shapes] + [jax.ShapeDtypeStruct(a.shape, a.dtype) for a in rest],
        in_specs=[vmem] * (1 + len(rest)),
        out_specs=[vmem] * (4 + len(rest)),
        compiler_params=pltpu.CompilerParams(vmem_limit_bytes=32 * 2**20),
        name="finish",
    )(packed, *rest)


def is_linked(rows):
    return lax.axis_size("dp") >= 4 and lax.axis_size("fsdp") == 4 and rows % 8 == 0


def fetch_weights(query_w, pair_w, out_w, up_w, down_w, gains, biases, tags):
    onehot = (tags[0] == jnp.arange(SUBSETS, dtype=jnp.int32)).astype(jnp.float32)
    own_counts = jnp.where((jnp.arange(query_w.shape[0]) == 0)[:, None], onehot[None, :], 0.0)
    small = jnp.concatenate([gains.T, biases.T, own_counts], axis=1)
    small = jnp.pad(small, ((0, 0), (0, 128 - small.shape[1])))
    packed = jnp.concatenate([query_w, pair_w, small], axis=1)
    return [
        lax.all_gather(a.astype(jnp.bfloat16), ("dp", "fsdp"), axis=0, tiled=True)
        for a in (packed, out_w, up_w, down_w)
    ]


def body(
    tokens,
    w_query,
    w_pair,
    w_attn_out,
    w_up,
    w_down,
    ln_gains,
    ln_biases,
    cotangent,
    subset_tags,
    subset_weights,
):
    cosine, sine = tables()
    linked = is_linked(w_query.shape[0])
    shards = (w_query, w_pair, w_attn_out, w_up, w_down, ln_gains, ln_biases, subset_tags)
    total_rows = lax.axis_size("dp") * lax.axis_size("fsdp")
    if linked:
        lines, rows, rows_down = lax.axis_size("dp") // 2, w_query.shape[0], w_down.shape[0]
    else:
        lines, rows, rows_down = 4, D // 32, 4 * D // 32
        shards = fetch_weights(*shards)
    kept, whole = forward(linked, lines, rows, rows_down, tokens, cosine, sine, shards)
    subset_w = subset_weights.reshape(1, SUBSETS)
    mixed, grad_tokens, packed_g, out_g, up_g, down_g = backward(
        linked, lines, rows, rows_down, total_rows, subset_tags, subset_w, cosine, sine, tokens, cotangent, kept, whole
    )
    if not linked:
        packed_g, out_g, up_g, down_g = [
            lax.psum_scatter(
                g.astype(jnp.float32).reshape(-1, g.shape[-1]), ("dp", "fsdp"), scatter_dimension=0, tiled=True
            )
            for g in (packed_g, out_g, up_g, down_g)
        ]
    query_g, pair_g, gains_g, biases_g, out_g, up_g, down_g, grad_tokens = finish(
        w_query.shape[0], packed_g, out_g, up_g, down_g, grad_tokens
    )
    return mixed, grad_tokens, query_g, pair_g, out_g, up_g, down_g, gains_g, biases_g


def solution(mesh):
    in_specs = (
        P(("dp", "fsdp"), None),
        P(("dp", "fsdp"), None),
        P(("dp", "fsdp"), None),
        P(("dp", "fsdp"), None),
        P(("dp", "fsdp"), None),
        P(("dp", "fsdp"), None),
        P(None, ("dp", "fsdp")),
        P(None, ("dp", "fsdp")),
        P(("dp", "fsdp"), None),
        P(("dp", "fsdp")),
        P(),
    )
    out_specs = (
        P(("dp", "fsdp"), None),
        P(("dp", "fsdp"), None),
        P(("dp", "fsdp"), None),
        P(("dp", "fsdp"), None),
        P(("dp", "fsdp"), None),
        P(("dp", "fsdp"), None),
        P(("dp", "fsdp"), None),
        P(None, ("dp", "fsdp")),
        P(None, ("dp", "fsdp")),
    )
    return jax.shard_map(body, mesh=mesh, in_specs=in_specs, out_specs=out_specs, check_vma=False)
```

```python
import functools

import jax
import jax.numpy as jnp
import numpy as np
from jax import lax
from jax.experimental import pallas as pl
from jax.experimental.pallas import tpu as pltpu
from jax.sharding import PartitionSpec as P

D = 768
H = 12
HD = 64
ROT = 16
SUBSETS = 22
SEQ = 1024
PACK = 1024
TILE = 256
LOG2E = 1.4426950408889634
PAIR = 3 * 128
SMALL = 256
GATHER_STARTS = (0.0, 0.0, 2.0, 7.0, 16.0, 21.0, 30.0, 35.0)
GATHER_LAGS = (0.0, 8.0, 16.0, 18.0)
SCATTER_LAGS = (0.0, 2.0, 8.0, 14.0, 20.0, 23.0)
PROJECT_STEPS = (1.25,) * 4
ATTEND_STEPS = (1.2, 2.8) * 6
OUTWARD_STEPS = (1.2,) * 4 + (0.85,) * 2
CLOSE_STEPS = (0.7,) * 4 + (1.0,)
CHUNK_STEPS = (1.6,) * 4 + (0.7,) * 4
TOKEN_STEPS = (0.7,) * 4
MESH = pl.DeviceIdType.MESH


eps_norm = 1e-05


def place_of(p):
    return (p % 2) * (PACK // 2) + (p // 2) * 2 * HD


def place():
    dp, fs = lax.axis_index("dp"), lax.axis_index("fsdp")
    return dp // 2, dp % 2, fs // 2, fs % 2


def device(z, x, y, c):
    return (z * 2 + x, y * 2 + c)


def partners():
    z, x, y, c = place()
    xa, ya = jnp.where(c == 0, 1 - x, x), jnp.where(c == 0, y, 1 - y)
    xb, yb = jnp.where(c == 0, x, 1 - x), jnp.where(c == 0, 1 - y, y)
    return xa, ya, xb, yb


def greet(lines):
    z, x, y, c = place()
    barrier = pltpu.get_barrier_semaphore()
    others = [device(lax.rem(z + d, lines), x, y, c) for d in range(1, lines)]
    others += [device(z, 1 - x, y, c), device(z, x, 1 - y, c), device(z, x, y, 1 - c)]
    for other in others:
        pl.semaphore_signal(barrier, inc=1, device_id=other, device_id_type=MESH)
    pl.semaphore_wait(barrier, len(others))


def remote(src, dst, send, recv, where):
    return pltpu.make_async_remote_copy(
        src_ref=src, dst_ref=dst, send_sem=send, recv_sem=recv, device_id=where, device_id_type=MESH
    )


def layout(rows, rows_down):
    return [(1, 2 * rows, PACK), (1, 2 * rows, D), (1, 2 * rows, 4 * D), (2, rows_down, D), (1, 2 * rows, SMALL)]


HALF = (PACK // 2, D // 2, D // 2, D // 2, SMALL // 2)


def lanes(start, size):
    return pl.ds(pl.multiple_of(start, 128), size)


def part(piece, ref, z, x, y, half):
    t, r0, nr, c0, _, w = piece
    return ref.at[z, x, y, :, pl.ds(r0, nr), lanes(half * HALF[t] + c0, w)]


def gather_pieces(blocks):
    r0, r1, r2, r3 = (r for _, r, _ in blocks[:4])
    w, half = D // 2, r3 // 2 // 16 * 16
    ups = [(2, 0, r2, 2 * w * k, w * k, w) for k in range(4)]
    downs = [(3, 0, half, 0, 0, w), (3, half, r3 - half, 0, 0, w)]
    return [(0, 0, r0, 0, 0, PACK // 2), (1, 0, r1, 0, 0, w), ups[0], downs[0], ups[1], downs[1], ups[2], ups[3]]


class Gather:
    def __init__(self, lines, rows, blocks, sources, stages, whole, sems):
        self.lines, self.rows, self.blocks = lines, rows, blocks
        self.sources, self.stages, self.whole = sources, stages, whole
        self.swap_send, self.swap_recv, self.send, self.recv = sems
        self.pieces = gather_pieces(blocks)
        self.z, self.x, self.y, self.c = place()
        self.xa, self.ya, self.xb, self.yb = partners()
        self.sibling = device(self.z, self.x, self.y, 1 - self.c)
        self.started = []

    def go(self, p, make):
        make().start()
        self.started.append((self.pieces[p][0], make))

    def stage_rows(self, p, core):
        t, r0, nr, _, l0, w = self.pieces[p]
        if self.blocks[t][0] == 2:
            return self.stages[t].at[core, pl.ds(r0, nr), pl.ds(l0, w)]
        return self.stages[t].at[0, pl.ds(pl.multiple_of(core * self.rows, 8), self.rows), pl.ds(l0, w)]

    def source(self, p):
        t, r0, nr, c0, _, w = self.pieces[p]
        return self.sources[t].at[pl.ds(r0, nr) if self.blocks[t][0] == 2 else slice(None)], c0, w

    def swap(self, p):
        source, c0, w = self.source(p)
        mine = source.at[:, lanes((1 - self.c) * HALF[self.pieces[p][0]] + c0, w)]
        return remote(mine, self.stage_rows(p, self.c), self.swap_send.at[p], self.swap_recv.at[p], self.sibling)

    def block(self, p, d, x, y):
        z = lax.rem(self.z + self.lines - d, self.lines)
        return part(self.pieces[p], self.whole[self.pieces[p][0]], z, x, y, self.c)

    def direct(self, p, d, back=0):
        block = self.block(p, back, self.x, self.y)
        where = device(lax.rem(self.z + d, self.lines), self.x, self.y, self.c)
        return remote(block, block, self.send.at[p, d - 1], self.recv.at[p, d - 1], where)

    def to_a(self, p, d, x, y):
        block, k = self.block(p, d, x, y), self.lines - 1 + d
        return remote(block, block, self.send.at[p, k], self.recv.at[p, k], device(self.z, self.xa, self.ya, self.c))

    def to_b(self, p, d, x, y, second=0):
        block, k = self.block(p, d, x, y), self.lines * (2 + second) - 1 + d
        return remote(block, block, self.send.at[p, k], self.recv.at[p, k], device(self.z, self.xb, self.yb, self.c))

    def share(self, p, k, x, y, half):
        column = part(self.pieces[p], self.whole[self.pieces[p][0]], slice(None), x, y, half)
        k = 4 * self.lines - 1 + k
        return remote(column, column, self.send.at[p, k], self.recv.at[p, k], self.sibling)

    def own(self, p):
        x, y = self.x, self.y
        self.go(p, lambda: self.to_a(p, 0, x, y))
        self.go(p, lambda: self.to_b(p, 0, x, y))

    def begin(self, ahead):
        for p in range(len(self.pieces)):
            self.go(p, functools.partial(self.swap, p))
        for p, piece in enumerate(self.pieces):
            t, r0, nr, c0, l0, w = piece
            source, _, _ = self.source(p)
            kept = jnp.where(self.c == 0, source[:, c0 : c0 + w], source[:, HALF[t] + c0 : HALF[t] + c0 + w])
            self.stage_rows(p, self.c)[...] = kept
            self.swap(p).wait_recv()
            held = self.stages[t][:, r0 : r0 + nr, l0 : l0 + w]
            self.block(p, 0, self.x, self.y)[...] = held.astype(jnp.bfloat16)
            for d in range(1, self.lines):
                self.go(p, functools.partial(self.direct, p, d))
            if p < ahead:
                self.own(p)
        self.ahead = ahead

    def first(self, p):
        x, y, c = self.x, self.y, self.c
        if p >= self.ahead:
            self.own(p)
        for d in range(1, self.lines):
            self.direct(p, d, back=d).wait_recv()
            self.go(p, functools.partial(self.to_a, p, d, x, y))
            self.go(p, functools.partial(self.to_b, p, d, x, y))
        self.go(p, lambda: self.share(p, 0, x, y, c))

    def second(self, p):
        for d in range(self.lines):
            self.to_a(p, d, self.xa, self.ya).wait_recv()
            self.go(p, functools.partial(self.to_b, p, d, self.xa, self.ya, 1))
        self.go(p, lambda: self.share(p, 1, self.xa, self.ya, self.c))

    def third(self, p):
        x, y = self.x, self.y
        for d in range(self.lines):
            self.to_b(p, d, self.xb, self.yb).wait_recv()
        self.go(p, lambda: self.share(p, 2, self.xb, self.yb, self.c))
        for d in range(self.lines):
            self.to_b(p, d, 1 - x, 1 - y, 1).wait_recv()
        self.go(p, lambda: self.share(p, 3, 1 - x, 1 - y, self.c))

    def fourth(self, p):
        x, y, c = self.x, self.y, 1 - self.c
        for k, sx, sy in ((0, x, y), (1, self.xb, self.yb), (2, self.xa, self.ya), (3, 1 - x, 1 - y)):
            self.share(p, k, sx, sy, c).wait_recv()

    def events(self):
        steps = (self.first, self.second, self.third, self.fourth)
        urgent = [(0, 0), (0, 1), (1, 0), (2, 0), (3, 0)]
        timed = []
        for p in range(1, len(self.pieces)):
            for k, lag in enumerate(GATHER_LAGS):
                if (k, p) not in urgent:
                    timed.append((GATHER_STARTS[p] + lag, len(timed), functools.partial(steps[k], p)))
        return [functools.partial(steps[k], p) for k, p in urgent], timed

    def sent(self, t):
        for kind, make in self.started:
            if kind == t:
                make().wait_send()


def deal(timed, times):
    plan = [[] for _ in range(len(times) + 1)]
    for when, _, event in sorted(timed, key=lambda e: e[:2]):
        plan[next((k for k, t in enumerate(times) if t >= when), len(times))].append(event)
    return plan


def ends(start, *steps):
    out = []
    for step in steps:
        start += step
        out.append(start)
    return out


def run_at(index, values):
    for value, events in values:
        if events:

            @pl.when(index == value)
            def _(events=events):
                for event in events:
                    event()


def columns(ref, start, size):
    return ref[:, :, :, :, :, pl.ds(start, size)].reshape(-1, size)


def turned(a, b):
    return lax.dot_general(a, b, (((1,), (1,)), ((), ())), preferred_element_type=jnp.float32)


def swapped(block, cosine, sine):
    lane = lax.broadcasted_iota(jnp.int32, block.shape, 1)
    other = jnp.where(lane % 16 < 8, pltpu.roll(block, 120, 1), pltpu.roll(block, 8, 1))
    return block * cosine + other * sine


def tables():
    half = ROT // 2
    inverse = np.float32(10000.0) ** (-(np.arange(half, dtype=np.float32) * 2) / ROT)
    phase = np.arange(SEQ, dtype=np.float32)[:, None] * inverse.astype(np.float32)[None, :]
    cos_t, sin_t = np.cos(phase.astype(np.float64)), np.sin(phase.astype(np.float64))
    rest = np.zeros((SEQ, HD - ROT))
    cosine = np.concatenate([cos_t, cos_t, rest + 1.0] * 2, axis=1)
    sine = np.concatenate([-sin_t, sin_t, rest] * 2, axis=1)
    return jnp.asarray(cosine.astype(np.float32)), jnp.asarray(sine.astype(np.float32))


def scatter_pieces(blocks):
    r0, r1, r2, r3, r4 = (r for _, r, _ in blocks)
    w, q = D // 2, PACK // 4
    pieces = [(1, 0, r1, 0, 0, w), (0, 0, r0, 0, 0, q), (0, 0, r0, q, q, q)]
    for k in range(4):
        pieces += [(3, 0, r3, 0, 0, w), (2, 0, r2, 2 * w * k, w * k, w)]
    return pieces + [(4, 0, r4, 0, 0, SMALL // 2)]


SLOTS = 2


class Scatter:
    def __init__(self, lines, rows, blocks, grads, outs, buffers, sems):
        self.lines, self.rows, self.blocks = lines, rows, blocks
        self.grads, self.outs = grads, outs
        kinds = len(blocks)
        self.near, self.from_b, self.from_a, self.from_z, self.total, self.last = (
            buffers[kinds * k : kinds * (k + 1)] for k in range(6)
        )
        self.send, self.recv, self.credit = sems
        self.pieces = scatter_pieces(blocks)
        self.only = [(p - 3) // 2 if piece[0] == 3 else None for p, piece in enumerate(self.pieces)]
        self.z, self.x, self.y, self.c = place()
        self.xa, self.ya, self.xb, self.yb = partners()
        self.sibling = device(self.z, self.x, self.y, 1 - self.c)
        self.started = []

    def go(self, make):
        make().start()
        self.started.append((None, make))

    def where(self, p, body):
        if self.only[p] is None:
            body()
        else:
            pl.when(self.z == self.only[p])(body)

    def every(self, p):
        return slice(None) if self.only[p] is None else pl.ds(self.only[p], 1)

    def planes(self, p, body):
        if self.only[p] is None:
            pl.loop(0, self.lines)(body)
        else:
            body(self.only[p])

    def cut(self, p, ref, *lead):
        t, r0, nr, _, l0, w = self.pieces[p]
        return ref[t].at[(*lead, slice(None), pl.ds(r0, nr), pl.ds(l0, w))]

    def grad(self, p, z, x, y, half=None):
        half = self.c if half is None else half
        return part(self.pieces[p], self.grads[self.pieces[p][0]], z, x, y, half)

    def slot(self, p):
        t, _, _, _, l0, w = self.pieces[p]
        return {0: l0 // w, 1: 0, 2: l0 // w % SLOTS, 3: (p - 3) // 2 % SLOTS, 4: 0}[t]

    def near_copy(self, p):
        every = slice(None)
        mine = self.grad(p, self.every(p), every, every, 1 - self.c)
        near = self.near[self.pieces[p][0]].at[self.slot(p)]
        return remote(mine, near, self.send.at[p, 0], self.recv.at[p, 0], self.sibling)

    def b_copy(self, p, k):
        at = (self.xb, self.yb) if k == 0 else (1 - self.x, 1 - self.y)
        return remote(
            self.grad(p, self.every(p), *at),
            self.cut(p, self.from_b, k, self.every(p)),
            self.send.at[p, 1 + k],
            self.recv.at[p, 1 + k],
            device(self.z, self.xb, self.yb, self.c),
        )

    def a_copy(self, p):
        return remote(
            self.grad(p, self.every(p), self.xa, self.ya),
            self.cut(p, self.from_a, self.every(p)),
            self.send.at[p, 3],
            self.recv.at[p, 3],
            device(self.z, self.xa, self.ya, self.c),
        )

    def z_copy(self, p, d):
        other = lax.rem(self.z + d, self.lines)
        return remote(
            self.grad(p, other, self.x, self.y),
            self.cut(p, self.from_z, d - 1),
            self.send.at[p, 3 + d],
            self.recv.at[p, 3 + d],
            device(other, self.x, self.y, self.c),
        )

    def last_copy(self, p):
        t, r0, nr, _, l0, w = self.pieces[p]
        if self.blocks[t][0] == 2:
            src = self.total[t].at[1 - self.c, pl.ds(r0, nr), pl.ds(l0, w)]
            dst = self.last[t].at[pl.ds(r0, nr), pl.ds(l0, w)]
        else:
            away = pl.ds(pl.multiple_of((1 - self.c) * self.rows, 8), self.rows)
            src = self.total[t].at[0, away, pl.ds(l0, w)]
            dst = self.last[t].at[:, pl.ds(l0, w)]
        k = 3 + self.lines
        return remote(src, dst, self.send.at[p, k], self.recv.at[p, k], self.sibling)

    def uses(self, p):
        t = self.pieces[p][0]
        if t not in (2, 3):
            return False, False
        return p - 2 * SLOTS >= 3, p + 2 * SLOTS <= 10

    def first(self, p):
        if self.uses(p)[0]:
            pl.semaphore_wait(self.credit.at[self.pieces[p][0] - 2], 1)
        self.go(lambda: self.near_copy(p))

    def second(self, p):
        f32 = jnp.float32
        self.near_copy(p).wait_recv()
        near = self.near[self.pieces[p][0]].at[self.slot(p)]

        def add(k):
            for x in range(2):
                for y in range(2):
                    kept = self.grad(p, k, x, y)
                    got = near[0 if self.only[p] is not None else k, x, y]
                    kept[...] = (kept[...].astype(f32) + got.astype(f32)).astype(jnp.bfloat16)

        self.planes(p, add)
        if self.uses(p)[1]:
            credit = self.credit.at[self.pieces[p][0] - 2]
            pl.semaphore_signal(credit, inc=1, device_id=self.sibling, device_id_type=MESH)
        self.go(lambda: self.b_copy(p, 1))
        self.go(lambda: self.b_copy(p, 0))

    def third(self, p):
        self.b_copy(p, 1).wait_recv()

        def add(k):
            kept, got = self.grad(p, k, self.xa, self.ya), self.cut(p, self.from_b, 1, k)
            kept[...] = (kept[...].astype(jnp.float32) + got[...].astype(jnp.float32)).astype(jnp.bfloat16)

        self.planes(p, add)
        self.go(lambda: self.a_copy(p))

    def mine(self, p, k):
        got = self.cut(p, self.from_b, 0, k)[...].astype(jnp.float32) + self.cut(p, self.from_a, k)[...].astype(jnp.float32)
        return self.grad(p, k, self.x, self.y)[...].astype(jnp.float32) + got

    def fourth(self, p):
        self.b_copy(p, 0).wait_recv()
        self.a_copy(p).wait_recv()
        q = self.only[p]

        def send():
            for d in range(1, self.lines):
                self.go(functools.partial(self.z_copy, p, d))

        def round_off(k):
            self.grad(p, k, self.x, self.y)[...] = self.mine(p, k).astype(jnp.bfloat16)

        if q is None:

            @pl.loop(1, self.lines)
            def _(d):
                round_off(lax.rem(self.z + d, self.lines))

            send()
        else:

            def to_owner():
                return self.z_copy(p, lax.rem(q - self.z + self.lines, self.lines))

            @pl.when(self.z != q)
            def _():
                round_off(q)
                to_owner().start()

            self.started.append((lambda: self.z != q, to_owner))

        def keep():
            self.cut(p, self.total)[...] = self.mine(p, self.z if q is None else q)

        self.where(p, keep)

    def fifth(self, p):
        def body():
            for d in range(1, self.lines):
                self.z_copy(p, d).wait_recv()
            total = self.cut(p, self.total)
            acc = total[...]
            for d in range(1, self.lines):
                acc = acc + self.cut(p, self.from_z, d - 1)[...].astype(jnp.float32)
            total[...] = acc
            self.last_copy(p).start()

        self.where(p, body)
        q = self.only[p]
        self.started.append((None if q is None else lambda: self.z == q, lambda: self.last_copy(p)))

    def sixth(self, p):
        t, r0, nr, c0, l0, w = self.pieces[p]

        def body():
            self.last_copy(p).wait_recv()
            if self.blocks[t][0] == 2:
                kept = self.total[t][self.c, r0 : r0 + nr, l0 : l0 + w]
                got = self.last[t][r0 : r0 + nr, l0 : l0 + w]
                to = slice(r0, r0 + nr)
            else:
                kept = self.total[t][0, pl.ds(pl.multiple_of(self.c * self.rows, 8), self.rows), l0 : l0 + w]
                got = self.last[t][:, l0 : l0 + w]
                to = slice(None)
            h = HALF[t] + c0
            self.outs[t][to, c0 : c0 + w] = jnp.where(self.c == 0, kept, got)
            self.outs[t][to, h : h + w] = jnp.where(self.c == 0, got, kept)

        self.where(p, body)

    def steps(self):
        return [self.first, self.second, self.third, self.fourth, self.fifth, self.sixth]

    def timed(self, p, start):
        return [(start + lag, p, functools.partial(step, p)) for step, lag in zip(self.steps(), SCATTER_LAGS)]

    def finish(self):
        for condition, make in self.started:
            if condition is None:
                make().wait_send()
            else:

                @pl.when(condition())
                def _(make=make):
                    make().wait_send()


def crossed(a, b):
    return lax.dot_general(a, b, (((0,), (0,)), ((), ())), preferred_element_type=jnp.float32)


def layer_kernel(lines, rows, blocks, linked, total_rows, *refs):
    f32, bf16 = jnp.float32, jnp.bfloat16
    tags, subset_w, tokens_h, cotan_h, cosine_h, sine_h = refs[:6]
    given, refs = (refs[6:13], refs[13:]) if linked else (refs[6:10], refs[10:])
    mixed_h, grad_tokens_h, *results = refs[:7]
    tokens, cotan, cosine, sine, normed, small, first_in, second_in, queries, pool, keys, keys_t = refs[7:19]
    values, values_t, attended, logsums, scaled, packed_d, mask, sums, d_keys, d_values, branch, d_second = refs[19:31]
    whole, grad_packed, grad_small, load_sems, out_sems = refs[31:35], refs[35], refs[36], refs[37], refs[38]
    refs = refs[39:]
    grads = [grad_packed, *whole[1:], grad_small]
    tiles, wide, qkv = SEQ // TILE, D // 2, D + 2 * HD

    def tile(k):
        return pl.ds(pl.multiple_of(k * TILE, TILE), TILE)

    pairs = [(tokens_h, tokens), (cosine_h, cosine), (sine_h, sine), (cotan_h, cotan)]
    if not linked:
        pairs += list(zip(given, whole))
    loads = [pltpu.make_async_copy(a, b, load_sems.at[k]) for k, (a, b) in enumerate(pairs)]
    for copy in loads:
        copy.start()
    if linked:
        query, pair, out, up, down, gains, biases = given
        packed, stages, square, gather_sems, refs = refs[0], refs[1:5], refs[5], refs[6:10], refs[10:]
        for p in range(H // 2):
            packed[:, place_of(p) : place_of(p) + 2 * HD] = query[:, 2 * HD * p : 2 * HD * (p + 1)]
        packed[:, PAIR : PAIR + 2 * HD] = pair[...]
        square[...] = jnp.zeros_like(square)
        square[0:2, 0:rows] = gains[...]
        square[2:4, 0:rows] = biases[...]
        spot = lax.broadcasted_iota(jnp.int32, (rows, 128), 1) == tags[0] + 4
        spot = jnp.where(lax.broadcasted_iota(jnp.int32, (rows, 128), 0) == 0, spot.astype(f32), 0.0)
        packed[:, qkv:] = square[...].T[:rows] + spot
        greet(lines)
        gather = Gather(lines, rows, blocks, [packed, out, up, down], stages, whole, gather_sems)
        scatter = Scatter(lines, rows, blocks, grads, results, refs[:30], refs[30:33])
        gather.begin(2)
        urgent, timed = gather.events()
    else:
        urgent, timed = [], []
    packed_w, out_w, up_w, down_w = whole

    steps = (PROJECT_STEPS, ATTEND_STEPS, OUTWARD_STEPS, ATTEND_STEPS, CLOSE_STEPS, CHUNK_STEPS * 4, TOKEN_STEPS)
    starts, slots = [0], [0]
    for part_steps in steps:
        starts.append(starts[-1] + sum(part_steps))
        slots.append(slots[-1] + len(part_steps))
    if linked:
        timed += scatter.timed(0, starts[3])
        ready = starts[3] + 4 * sum(ATTEND_STEPS[:2])
        timed += [(ready - 0.01, 100, lambda: query_grads(0, PACK // 4))] + scatter.timed(1, ready)
        timed += scatter.timed(2, starts[5])
        for q in range(4):
            start = starts[5] + q * sum(CHUNK_STEPS) + sum(CHUNK_STEPS[:6])
            timed += scatter.timed(3 + 2 * q, start) + scatter.timed(4 + 2 * q, start + sum(CHUNK_STEPS[6:]))
        timed += scatter.timed(11, starts[6])
    plan = deal(timed, ends(0.0, *(step for part_steps in steps for step in part_steps)))

    def slot(section, index, values):
        run_at(index, [(v, plan[slots[section] + v]) for v in values])

    row = lax.broadcasted_iota(jnp.int32, (TILE, TILE), 0)
    column = lax.broadcasted_iota(jnp.int32, (TILE, TILE), 1)
    mask[...] = jnp.where(row <= column, 0.0, -1e30)
    sums[...] = jnp.zeros_like(sums)
    d_keys[...] = jnp.zeros_like(d_keys)
    d_values[...] = jnp.zeros_like(d_values)
    lane = lax.broadcasted_iota(jnp.int32, (TILE, 2 * HD), 1)
    left = lane < HD
    loads[0].wait()

    @pl.loop(0, tiles)
    def _(k):
        inputs = tokens[tile(k), :].astype(f32)
        centred = inputs - jnp.mean(inputs, axis=-1, keepdims=True)
        normed[tile(k), :] = centred * lax.rsqrt(jnp.mean(centred * centred, axis=-1, keepdims=True) + eps_norm)

    for copy in loads[1:]:
        copy.wait()
    for event in urgent:
        event()
    small[...] = columns(packed_w, qkv, 128).astype(f32).T

    @pl.loop(0, tiles)
    def _(k):
        norm = normed[tile(k), :]
        a1 = (norm * small[0:1, :] + small[2:3, :]).astype(bf16)
        first_in[tile(k), :] = a1
        second_in[tile(k), :] = (norm * small[1:2, :] + small[3:4, :]).astype(bf16)
        mixed = jnp.dot(a1, columns(packed_w, 0, qkv), preferred_element_type=f32)
        cos_t, sin_t = cosine[tile(k), :], sine[tile(k), :]
        for p in range(H // 2):
            turn = swapped(mixed[:, place_of(p) : place_of(p) + 2 * HD], cos_t, sin_t).astype(bf16).astype(f32)
            turn = turn * (LOG2E / 8)
            high = turn.astype(bf16).astype(f32)
            low = turn - high
            queries[2 * p, tile(k), :] = jnp.where(left, high, pltpu.roll(low, HD, 1)).astype(bf16)
            queries[2 * p + 1, tile(k), :] = jnp.where(left, pltpu.roll(high, HD, 1), low).astype(bf16)
        pair_t = mixed[:, PAIR : PAIR + 2 * HD]
        pair_t = jnp.where(left, swapped(pair_t, cos_t, sin_t), pair_t).astype(bf16).astype(f32)
        other = pltpu.roll(pair_t, HD, 1)
        both = jnp.where(left, pair_t, other)
        keys[tile(k), :] = both.astype(bf16)
        keys_t[:, tile(k)] = both.T[:HD].astype(bf16)
        values[tile(k), :] = jnp.where(left, other, jnp.where(lane < HD + 2, -1.0, 0.0)).astype(bf16)
        values_t[:, tile(k)] = jnp.where(left, other, jnp.where(lane == HD, 1.0, 0.0)).T.astype(bf16)
        slot(0, k, range(tiles))

    @pl.loop(0, H // 2)
    def _(pr):
        for i in range(tiles):
            count = TILE * (i + 1)
            heads = []
            for hh in range(2):
                head = pr * 2 + hh
                scores = turned(keys[0:count, :], queries[head, i * TILE : count, :])
                last = scores[count - TILE :] + mask[...]
                peak = jnp.max(last, axis=0, keepdims=True)
                if i:
                    peak = jnp.maximum(peak, jnp.max(scores[: count - TILE], axis=0, keepdims=True))
                probs = jnp.exp2(last - peak).astype(bf16)
                if i:
                    probs = jnp.concatenate([jnp.exp2(scores[: count - TILE] - peak).astype(bf16), probs], axis=0)
                got = jnp.dot(values_t[:, 0:count], probs, preferred_element_type=f32)
                total = got[HD : HD + 1]
                heads.append(got[:HD] * (1.0 / total))
                logsums[head, :, i * TILE : count] = peak + jnp.log2(total)
            both = jnp.concatenate(heads, axis=0).T
            attended[i * TILE : count, lanes(pr * 2 * HD, 2 * HD)] = both.astype(bf16)
            if i % 2:
                slot(1, pr * 2 + i // 2, range(i // 2, 2 * (H // 2), 2))

    kind = lax.broadcasted_iota(jnp.int32, (128, D), 0)
    count = jnp.sum(jnp.where(kind == tags[0] + 4, small[...], 0.0), keepdims=True)
    subset = lax.broadcasted_iota(jnp.int32, subset_w.shape, 1)
    weight = jnp.sum(jnp.where(subset == tags[0], subset_w[...], 0.0), keepdims=True)
    scale = weight / count * (total_rows / SUBSETS)

    @pl.loop(0, tiles)
    def _(k):
        grad_out = (cotan[tile(k), :].astype(f32) * scale).astype(bf16)
        scaled[tile(k), :] = grad_out
        heads = attended[tile(k), :]
        out_m = out_w[...].reshape(D, D)
        branch[tile(k), :] = tokens[tile(k), :].astype(f32) + jnp.dot(heads, out_m, preferred_element_type=f32)
        d_heads_t = turned(grad_out, out_m).astype(bf16).astype(f32)
        for p in range(H // 2):
            block = d_heads_t[:, 2 * HD * p : 2 * HD * (p + 1)]
            product = block * heads[:, 2 * HD * p : 2 * HD * (p + 1)].astype(f32)
            for hh, (mine, there) in enumerate(((left, block), (~left, pltpu.roll(block, HD, 1)))):
                delta = jnp.sum(jnp.where(mine, product, 0.0), axis=1, keepdims=True)
                high = delta.astype(bf16).astype(f32)
                extra = jnp.where(lane == HD, high, jnp.where(lane == HD + 1, delta - high, 0.0))
                pool[2 * p + hh, tile(k), :] = jnp.where(left, there, extra).astype(bf16)
        slot(2, k, range(tiles))

    if linked:
        gather.sent(1)

    @pl.loop(0, 2)
    def _(k):
        got = crossed(attended[:, lanes(k * wide, wide)], scaled[...]).astype(bf16)
        grads[1][pl.ds(2 * k, 2)] = got.reshape(2, 2, 2, 1, D // 16, D)
        slot(2, tiles + k, range(tiles, tiles + 2))

    def query_grads(start, stop):
        for span in (slice(start, stop), slice(PACK // 2 + start, min(PACK // 2 + stop, qkv))):
            for k in range(2):
                got = crossed(first_in[:, k * wide : (k + 1) * wide], packed_d[:, span]).astype(bf16)
                grad_packed[2 * k : 2 * k + 2, :, :, :, :, span] = got.reshape(2, 2, 2, 1, D // 16, -1)

    @pl.loop(0, H // 2)
    def _(pr):
        for i in range(tiles):
            count = TILE * (i + 1)
            span = slice(i * TILE, count)
            probs_all, d_scores_all, d_query, ours = [], [], [], []
            d_out = [pool[pr * 2, span, :], pool[pr * 2 + 1, span, :]]
            for hh in range(2):
                query_t = queries[pr * 2 + hh, span, :]
                ours.append(query_t)
                scores = turned(keys[0:count, :], query_t)
                shift = logsums[pr * 2 + hh, :, span]
                probs = jnp.exp2(scores[count - TILE :] + mask[...] - shift)
                if i:
                    probs = jnp.concatenate([jnp.exp2(scores[: count - TILE] - shift), probs], axis=0)
                d_probs = turned(values[0:count, :], d_out[hh])
                d_scores = (probs * d_probs).astype(bf16)
                probs_all.append(probs.astype(bf16))
                d_scores_all.append(d_scores)
                d_query.append(jnp.dot(keys_t[:, 0:count], d_scores, preferred_element_type=f32))
            for acc, parts, other in ((d_values, probs_all, d_out), (d_keys, d_scores_all, ours)):
                two = jnp.concatenate(other, axis=0)
                acc[0:count, :] += jnp.dot(jnp.concatenate(parts, axis=1), two, preferred_element_type=f32)
            d_q = jnp.concatenate(d_query, axis=0).T * 0.125
            d_q = swapped(d_q, cosine[span, :], -sine[span, :])
            packed_d[span, lanes(place_of(pr), 2 * HD)] = d_q.astype(bf16)
            if i % 2:
                slot(3, pr * 2 + i // 2, range(i // 2, 2 * (H // 2), 2))

    @pl.loop(0, tiles)
    def _(k):
        d_key = d_keys[tile(k), :]
        d_key = (d_key + pltpu.roll(d_key, HD, 1)) * (1.0 / LOG2E)
        d_key = swapped(d_key, cosine[tile(k), :], -sine[tile(k), :])
        d_pair = jnp.where(left, d_key, pltpu.roll(d_values[tile(k), :], HD, 1)).astype(bf16)
        packed_d[tile(k), PAIR : PAIR + 2 * HD] = d_pair
        d_first = turned(packed_d[tile(k), 0:qkv], columns(packed_w, 0, qkv))
        sums[0:1, :] += jnp.sum(d_first * normed[tile(k), :], axis=0, keepdims=True)
        sums[2:3, :] += jnp.sum(d_first, axis=0, keepdims=True)
        slot(4, k, range(tiles))

    if not linked:
        query_grads(0, PACK // 4)
    query_grads(PACK // 4, PACK // 2)
    grad_packed[:, :, :, :, :, qkv:] = jnp.zeros((4, 2, 2, 1, D // 16, PACK - qkv), bf16)
    for event in plan[slots[4] + tiles]:
        event()
    if linked:
        gather.sent(2)
        gather.sent(3)

    @pl.loop(0, 4)
    def _(q):
        def up_m():
            return columns(up_w, pl.multiple_of(q * D, D), D)

        def down_m():
            return down_w[q].reshape(D, D)

        @pl.loop(0, tiles)
        def _(k):
            pre = jnp.dot(second_in[tile(k), :], up_m(), preferred_element_type=f32)
            d_hidden = turned(scaled[tile(k), :], down_m())
            cdf = 0.5 + 0.5 * lax.erf(pre * 0.7071067811865476)
            density = jnp.exp2(pre * pre * (-0.5 * LOG2E)) * 0.3989422804014327
            active = (pre * cdf).astype(bf16)
            d_up = (d_hidden * (cdf + pre * density)).astype(bf16)
            for b in range(6):
                pool[b, tile(k), :] = active[:, 128 * b : 128 * (b + 1)]
                pool[6 + b, tile(k), :] = d_up[:, 128 * b : 128 * (b + 1)]
            branch[tile(k), :] += jnp.dot(active, down_m(), preferred_element_type=f32)
            got = turned(d_up, up_m())
            d_second[tile(k), :] = jnp.where(q == 0, got, got + d_second[tile(k), :])
            slot(5, q * 8 + k, [v for v in range(32) if v % 8 < 4])

        @pl.loop(0, 2)
        def _(k):
            three = jnp.concatenate([pool[3 * k + b] for b in range(3)], axis=1)
            got = crossed(three, scaled[...]).astype(bf16)
            down_w[q, k] = got.reshape(2, 2, 4 * D // 32, D)
            slot(5, q * 8 + 4 + k, [v for v in range(32) if v % 8 in (4, 5)])

        @pl.loop(0, 2)
        def _(k):
            six = jnp.concatenate([pool[6 + b] for b in range(6)], axis=1)
            got = crossed(second_in[:, lanes(k * wide, wide)], six).astype(bf16)
            up_w[pl.ds(2 * k, 2), :, :, :, :, lanes(q * D, D)] = got.reshape(2, 2, 2, 1, D // 16, D)
            slot(5, q * 8 + 6 + k, [v for v in range(32) if v % 8 in (6, 7)])

    @pl.loop(0, tiles)
    def _(k):
        second = d_second[tile(k), :]
        sums[1:2, :] += jnp.sum(second * normed[tile(k), :], axis=0, keepdims=True)
        sums[3:4, :] += jnp.sum(second, axis=0, keepdims=True)
        attended[tile(k), :] = branch[tile(k), :].astype(bf16)

    flushed = [pltpu.make_async_copy(attended, mixed_h, out_sems.at[0])]
    flushed[0].start()
    grad_small[:, :, :, :, :, 0:128] = sums[...].T.astype(bf16).reshape(4, 2, 2, 1, D // 16, 128)
    grad_small[:, :, :, :, :, 128:] = jnp.zeros((4, 2, 2, 1, D // 16, SMALL - 128), bf16)

    @pl.loop(0, tiles)
    def _(k):
        inputs = tokens[tile(k), :].astype(f32)
        centred = inputs - jnp.mean(inputs, axis=-1, keepdims=True)
        inv_std = lax.rsqrt(jnp.mean(centred * centred, axis=-1, keepdims=True) + eps_norm)
        norm = centred * inv_std
        d_first = turned(packed_d[tile(k), 0:qkv], columns(packed_w, 0, qkv))
        d_normed = d_first * small[0:1, :] + d_second[tile(k), :] * small[1:2, :]
        inner = jnp.mean(d_normed * norm, axis=-1, keepdims=True)
        d_inputs = inv_std * (d_normed - jnp.mean(d_normed, axis=-1, keepdims=True) - norm * inner)
        first_in[tile(k), :] = (cotan[tile(k), :].astype(f32) * scale + d_inputs).astype(bf16)
        slot(6, k, range(tiles))

    flushed.append(pltpu.make_async_copy(first_in, grad_tokens_h, out_sems.at[1]))
    flushed[-1].start()
    for event in plan[-1]:
        event()
    if linked:
        gather.sent(0)
        scatter.finish()
    else:
        for t in range(5):
            flushed.append(pltpu.make_async_copy(grads[t], results[t], out_sems.at[2 + t]))
            flushed[-1].start()
    for copy in flushed:
        copy.wait()


def layer(linked, lines, rows, rows_down, total_rows, tags, subset_w, tokens, cotan, cosine, sine, weights):
    blocks = layout(rows, rows_down)
    f32, bf16 = jnp.float32, jnp.bfloat16
    shapes = [(lines, 2, 2, g, r, k) for g, r, k in blocks]
    own_rows = [r if g == 2 else rows for g, r, k in blocks]
    vmem = pl.BlockSpec(memory_space=pltpu.VMEM)
    anywhere = pl.BlockSpec(memory_space=pl.ANY)
    if linked:
        results = [jax.ShapeDtypeStruct((o, k), f32) for o, (g, r, k) in zip(own_rows, blocks)]
    else:
        weights = [a.reshape(shape) for a, shape in zip(weights, shapes)]
        results = [jax.ShapeDtypeStruct(shape, bf16) for shape in shapes]
    tall = (SEQ, D)
    buffers = [
        (tall, bf16),
        (tall, bf16),
        ((SEQ, 2 * HD), f32),
        ((SEQ, 2 * HD), f32),
        (tall, f32),
        ((128, D), f32),
        (tall, bf16),
        (tall, bf16),
        ((H, SEQ, 2 * HD), bf16),
        ((H, SEQ, 2 * HD), bf16),
        ((SEQ, 2 * HD), bf16),
        ((HD, SEQ), bf16),
        ((SEQ, 2 * HD), bf16),
        ((2 * HD, SEQ), bf16),
        (tall, bf16),
        ((H, 1, SEQ), f32),
        (tall, bf16),
        ((SEQ, D + 2 * HD), bf16),
        ((TILE, TILE), f32),
        ((128, D), f32),
        ((SEQ, 2 * HD), f32),
        ((SEQ, 2 * HD), f32),
        (tall, f32),
        (tall, f32),
    ]
    buffers += [(shape, bf16) for shape in shapes[:4]] + [(shapes[0], bf16), (shapes[4], bf16)]
    scratch = [pltpu.VMEM(shape, kind) for shape, kind in buffers]
    scratch += [pltpu.SemaphoreType.DMA((8,)), pltpu.SemaphoreType.DMA((7,))]
    if linked:
        scratch += [pltpu.VMEM((rows, PACK), f32)]
        scratch += [pltpu.VMEM((g, r, k // 2), f32) for g, r, k in blocks[:4]]
        scratch += [pltpu.VMEM((128, 128), f32)]
        count, kinds = len(gather_pieces(blocks)), 4 * lines + 3
        scratch += [pltpu.SemaphoreType.DMA((count,))] * 2 + [pltpu.SemaphoreType.DMA((count, kinds))] * 2
        near = [(2, lines, PACK // 4), (1, lines, D // 2), (SLOTS, lines, D // 2), (SLOTS, 1, D // 2), (1, lines, SMALL // 2)]
        scratch += [pltpu.VMEM((n, z, 2, 2, g, r, w), bf16) for (n, z, w), (g, r, k) in zip(near, blocks)]
        for lead in ((2, lines), (lines,), (lines - 1,)):
            scratch += [pltpu.VMEM((*lead, g, r, k // 2), bf16) for g, r, k in blocks]
        scratch += [pltpu.VMEM((g, r, k // 2), f32) for g, r, k in blocks]
        scratch += [pltpu.VMEM((o, k // 2), f32) for o, (g, r, k) in zip(own_rows, blocks)]
        count = len(scatter_pieces(blocks))
        scratch += [pltpu.SemaphoreType.DMA((count, lines + 4))] * 2 + [pltpu.SemaphoreType.REGULAR((2,))]
    return pl.pallas_call(
        functools.partial(layer_kernel, lines, rows, blocks, linked, total_rows),
        out_shape=[jax.ShapeDtypeStruct(tall, bf16)] * 2 + results,
        in_specs=[pl.BlockSpec(memory_space=pltpu.SMEM), vmem] + [anywhere] * 4 + [vmem if linked else anywhere] * len(weights),
        out_specs=[anywhere] * 2 + [vmem if linked else anywhere] * 5,
        scratch_shapes=scratch,
        compiler_params=pltpu.CompilerParams(
            collective_id=0 if linked else None, has_side_effects=linked, vmem_limit_bytes=63 * 2**20
        ),
        name="layer",
    )(tags, subset_w, tokens, cotan, cosine, sine, *weights)


def finish_kernel(rows, *refs):
    packed, small, *rest = refs[:7]
    query, pair, gains, biases, *to = refs[7:]
    for p in range(H // 2):
        query[:, 2 * HD * p : 2 * HD * (p + 1)] = packed[:, place_of(p) : place_of(p) + 2 * HD]
    pair[...] = packed[:, PAIR : PAIR + 2 * HD]
    turned_back = small[:, 0:128].T
    gains[...] = turned_back[0:2]
    biases[...] = turned_back[2:4]
    for a, b in zip(rest, to):
        b[...] = a[...]


def finish(rows, packed, small, *rest):
    f32 = jnp.float32
    vmem = pl.BlockSpec(memory_space=pltpu.VMEM)
    shapes = [(rows, D), (rows, 2 * HD), (2, rows), (2, rows)]
    return pl.pallas_call(
        functools.partial(finish_kernel, rows),
        out_shape=[jax.ShapeDtypeStruct(a, f32) for a in shapes] + [jax.ShapeDtypeStruct(a.shape, a.dtype) for a in rest],
        in_specs=[vmem] * (2 + len(rest)),
        out_specs=[vmem] * (4 + len(rest)),
        compiler_params=pltpu.CompilerParams(vmem_limit_bytes=63 * 2**20),
        name="finish",
    )(packed, small, *rest)


def is_linked(rows):
    return lax.axis_size("dp") == 8 and lax.axis_size("fsdp") == 4 and rows % 8 == 0


def fetch_weights(query_w, pair_w, out_w, up_w, down_w, gains, biases, tags):
    onehot = (tags[0] == jnp.arange(SUBSETS, dtype=jnp.int32)).astype(jnp.float32)
    own_counts = jnp.where((jnp.arange(query_w.shape[0]) == 0)[:, None], onehot[None, :], 0.0)
    small = jnp.concatenate([gains.T, biases.T, own_counts], axis=1)
    small = jnp.pad(small, ((0, 0), (0, 128 - small.shape[1])))
    pairs = [query_w[:, 2 * HD * p : 2 * HD * (p + 1)] for p in range(H // 2)]
    packed = jnp.concatenate([*pairs[0::2], pair_w, *pairs[1::2], small], axis=1)
    return [
        lax.all_gather(a.astype(jnp.bfloat16), ("dp", "fsdp"), axis=0, tiled=True)
        for a in (packed, out_w, up_w, down_w)
    ]


def body(
    tokens,
    w_query,
    w_pair,
    w_attn_out,
    w_up,
    w_down,
    ln_gains,
    ln_biases,
    cotangent,
    subset_tags,
    subset_weights,
):
    cosine, sine = tables()
    linked = is_linked(w_query.shape[0])
    shards = (w_query, w_pair, w_attn_out, w_up, w_down, ln_gains, ln_biases)
    total_rows = lax.axis_size("dp") * lax.axis_size("fsdp")
    if linked:
        lines, rows, rows_down = lax.axis_size("dp") // 2, w_query.shape[0], w_down.shape[0]
    else:
        lines, rows, rows_down = 4, D // 32, 4 * D // 32
        shards = fetch_weights(*shards, subset_tags)
    subset_w = subset_weights.reshape(1, SUBSETS)
    mixed, grad_tokens, *grads = layer(
        linked, lines, rows, rows_down, total_rows, subset_tags, subset_w, tokens, cotangent, cosine, sine, shards
    )
    if not linked:
        grads = [
            lax.psum_scatter(
                g.astype(jnp.float32).reshape(-1, g.shape[-1]), ("dp", "fsdp"), scatter_dimension=0, tiled=True
            )
            for g in grads
        ]
    packed_g, out_g, up_g, down_g, small_g = grads
    query_g, pair_g, gains_g, biases_g, out_g, up_g, down_g, grad_tokens, mixed = finish(
        w_query.shape[0], packed_g, small_g, out_g, up_g, down_g, grad_tokens, mixed
    )
    return mixed, grad_tokens, query_g, pair_g, out_g, up_g, down_g, gains_g, biases_g


def solution(mesh):
    in_specs = (
        P(("dp", "fsdp"), None),
        P(("dp", "fsdp"), None),
        P(("dp", "fsdp"), None),
        P(("dp", "fsdp"), None),
        P(("dp", "fsdp"), None),
        P(("dp", "fsdp"), None),
        P(None, ("dp", "fsdp")),
        P(None, ("dp", "fsdp")),
        P(("dp", "fsdp"), None),
        P(("dp", "fsdp")),
        P(),
    )
    out_specs = (
        P(("dp", "fsdp"), None),
        P(("dp", "fsdp"), None),
        P(("dp", "fsdp"), None),
        P(("dp", "fsdp"), None),
        P(("dp", "fsdp"), None),
        P(("dp", "fsdp"), None),
        P(("dp", "fsdp"), None),
        P(None, ("dp", "fsdp")),
        P(None, ("dp", "fsdp")),
    )
    return jax.shard_map(body, mesh=mesh, in_specs=in_specs, out_specs=out_specs, check_vma=False)
```

```python
import functools

import jax
import jax.numpy as jnp
import numpy as np
from jax import lax
from jax.experimental import pallas as pl
from jax.experimental.pallas import tpu as pltpu
from jax.sharding import PartitionSpec as P

D = 768
H = 12
HD = 64
ROT = 16
SUBSETS = 22
SEQ = 1024
PACK = 1024
TILE = 256
LOG2E = 1.4426950408889634
PAIR = 3 * 128
SMALL = 256
GATHER_STARTS = (0.0, -6.0, 0.0, 8.0, 17.0, 22.0, 27.0, 32.0)
GATHER_LAGS = (0.0, 10.0, 20.0, 22.0)
SCATTER_LAGS = (0.0, 2.5, 10.0, 17.0, 24.0, 27.0)
PROJECT_STEPS = (1.5,) * 4
FORWARD_STEPS = (1.7, 0.1) * 6
OUTWARD_STEPS = (1.5,) * 4 + (0.85,) * 2
BACKWARD_STEPS = (3.2, 0.1) * 6
CLOSE_STEPS = (0.7,) * 4 + (1.0,)
CHUNK_STEPS = (1.4, 1.4, 1.4, 1.4, 1.2, 0.1, 1.2, 0.1)
TOKEN_STEPS = (0.9,) * 4
MESH = pl.DeviceIdType.MESH


eps_norm = 1e-05


def place_of(p):
    return (p % 2) * (PACK // 2) + (p // 2) * 2 * HD


def place():
    dp, fs = lax.axis_index("dp"), lax.axis_index("fsdp")
    return dp // 2, dp % 2, fs // 2, fs % 2


def device(z, x, y, c):
    return (z * 2 + x, y * 2 + c)


def partners():
    z, x, y, c = place()
    xa, ya = jnp.where(c == 0, 1 - x, x), jnp.where(c == 0, y, 1 - y)
    xb, yb = jnp.where(c == 0, x, 1 - x), jnp.where(c == 0, 1 - y, y)
    return xa, ya, xb, yb


def greet(lines):
    z, x, y, c = place()
    barrier = pltpu.get_barrier_semaphore()
    others = [device(lax.rem(z + d, lines), x, y, c) for d in range(1, lines)]
    others += [device(z, 1 - x, y, c), device(z, x, 1 - y, c), device(z, x, y, 1 - c)]
    for other in others:
        pl.semaphore_signal(barrier, inc=1, device_id=other, device_id_type=MESH)
    pl.semaphore_wait(barrier, len(others))


def remote(src, dst, send, recv, where):
    return pltpu.make_async_remote_copy(
        src_ref=src, dst_ref=dst, send_sem=send, recv_sem=recv, device_id=where, device_id_type=MESH
    )


def layout(rows, rows_down):
    return [(1, 2 * rows, PACK), (1, 2 * rows, D), (1, 2 * rows, 4 * D), (2, rows_down, D), (1, 2 * rows, SMALL)]


HALF = (PACK // 2, D // 2, D // 2, D // 2, SMALL // 2)


def lanes(start, size):
    return pl.ds(pl.multiple_of(start, 128), size)


def part(piece, ref, z, x, y, half):
    t, r0, nr, c0, _, w = piece
    return ref.at[z, x, y, :, pl.ds(r0, nr), lanes(half * HALF[t] + c0, w)]


def gather_pieces(blocks):
    r0, r1, r2, r3 = (r for _, r, _ in blocks[:4])
    w, half = D // 2, r3 // 2 // 16 * 16
    ups = [(2, 0, r2, 2 * w * k, w * k, w) for k in range(4)]
    downs = [(3, 0, half, 0, 0, w), (3, half, r3 - half, 0, 0, w)]
    return [(0, 0, r0, 0, 0, PACK // 2), (1, 0, r1, 0, 0, w), *downs, *ups]


class Gather:
    def __init__(self, lines, rows, blocks, sources, stages, whole, sems):
        self.lines, self.rows, self.blocks = lines, rows, blocks
        self.sources, self.stages, self.whole = sources, stages, whole
        self.swap_send, self.swap_recv, self.send, self.recv = sems
        self.pieces = gather_pieces(blocks)
        self.z, self.x, self.y, self.c = place()
        self.xa, self.ya, self.xb, self.yb = partners()
        self.sibling = device(self.z, self.x, self.y, 1 - self.c)
        self.started = []

    def go(self, p, make):
        make().start()
        self.started.append((p, make))

    def stage_rows(self, p, core):
        t, r0, nr, _, l0, w = self.pieces[p]
        if self.blocks[t][0] == 2:
            return self.stages[t].at[core, pl.ds(r0, nr), pl.ds(l0, w)]
        return self.stages[t].at[0, pl.ds(pl.multiple_of(core * self.rows, 8), self.rows), pl.ds(l0, w)]

    def source(self, p):
        t, r0, nr, c0, _, w = self.pieces[p]
        return self.sources[t].at[pl.ds(r0, nr) if self.blocks[t][0] == 2 else slice(None)], c0, w

    def swap(self, p):
        source, c0, w = self.source(p)
        mine = source.at[:, lanes((1 - self.c) * HALF[self.pieces[p][0]] + c0, w)]
        return remote(mine, self.stage_rows(p, self.c), self.swap_send.at[p], self.swap_recv.at[p], self.sibling)

    def block(self, p, d, x, y):
        z = lax.rem(self.z + self.lines - d, self.lines)
        return part(self.pieces[p], self.whole[self.pieces[p][0]], z, x, y, self.c)

    def direct(self, p, d, back=0):
        block = self.block(p, back, self.x, self.y)
        where = device(lax.rem(self.z + d, self.lines), self.x, self.y, self.c)
        return remote(block, block, self.send.at[p, d - 1], self.recv.at[p, d - 1], where)

    def to_a(self, p, d, x, y):
        block, k = self.block(p, d, x, y), self.lines - 1 + d
        return remote(block, block, self.send.at[p, k], self.recv.at[p, k], device(self.z, self.xa, self.ya, self.c))

    def to_b(self, p, d, x, y, second=0):
        block, k = self.block(p, d, x, y), self.lines * (2 + second) - 1 + d
        return remote(block, block, self.send.at[p, k], self.recv.at[p, k], device(self.z, self.xb, self.yb, self.c))

    def share(self, p, k, x, y, half):
        column = part(self.pieces[p], self.whole[self.pieces[p][0]], slice(None), x, y, half)
        k = 4 * self.lines - 1 + k
        return remote(column, column, self.send.at[p, k], self.recv.at[p, k], self.sibling)

    def own(self, p):
        x, y = self.x, self.y
        self.go(p, lambda: self.to_a(p, 0, x, y))
        self.go(p, lambda: self.to_b(p, 0, x, y))

    def begin(self, ahead):
        for p in range(len(self.pieces)):
            self.go(p, functools.partial(self.swap, p))
        for p, piece in enumerate(self.pieces):
            t, r0, nr, c0, l0, w = piece
            source, _, _ = self.source(p)
            kept = jnp.where(self.c == 0, source[:, c0 : c0 + w], source[:, HALF[t] + c0 : HALF[t] + c0 + w])
            self.stage_rows(p, self.c)[...] = kept
            self.swap(p).wait_recv()
            held = self.stages[t][:, r0 : r0 + nr, l0 : l0 + w]
            self.block(p, 0, self.x, self.y)[...] = held.astype(jnp.bfloat16)
            for d in range(1, self.lines):
                self.go(p, functools.partial(self.direct, p, d))
            if p < ahead:
                self.own(p)
        self.ahead = ahead

    def first(self, p):
        x, y, c = self.x, self.y, self.c
        if p >= self.ahead:
            self.own(p)
        for d in range(1, self.lines):
            self.direct(p, d, back=d).wait_recv()
            self.go(p, functools.partial(self.to_a, p, d, x, y))
            self.go(p, functools.partial(self.to_b, p, d, x, y))
        self.go(p, lambda: self.share(p, 0, x, y, c))

    def second(self, p):
        for d in range(self.lines):
            self.to_a(p, d, self.xa, self.ya).wait_recv()
            self.go(p, functools.partial(self.to_b, p, d, self.xa, self.ya, 1))
        self.go(p, lambda: self.share(p, 1, self.xa, self.ya, self.c))

    def third(self, p):
        x, y = self.x, self.y
        for d in range(self.lines):
            self.to_b(p, d, self.xb, self.yb).wait_recv()
        self.go(p, lambda: self.share(p, 2, self.xb, self.yb, self.c))
        for d in range(self.lines):
            self.to_b(p, d, 1 - x, 1 - y, 1).wait_recv()
        self.go(p, lambda: self.share(p, 3, 1 - x, 1 - y, self.c))

    def fourth(self, p):
        x, y, c = self.x, self.y, 1 - self.c
        for k, sx, sy in ((0, x, y), (1, self.xb, self.yb), (2, self.xa, self.ya), (3, 1 - x, 1 - y)):
            self.share(p, k, sx, sy, c).wait_recv()

    def events(self):
        steps = (self.first, self.second, self.third, self.fourth)
        urgent = [(0, 0), (0, 1), (1, 0), (2, 0), (3, 0)]
        timed = []
        for p in range(1, len(self.pieces)):
            for k, lag in enumerate(GATHER_LAGS):
                if (k, p) not in urgent:
                    timed.append((GATHER_STARTS[p] + lag, len(timed), functools.partial(steps[k], p)))
        return [functools.partial(steps[k], p) for k, p in urgent], timed

    def sent(self, *pieces):
        for p, make in self.started:
            if p in pieces:
                make().wait_send()


def deal(timed, times):
    plan = [[] for _ in range(len(times) + 1)]
    for when, _, event in sorted(timed, key=lambda e: e[:2]):
        plan[next((k for k, t in enumerate(times) if t >= when), len(times))].append(event)
    return plan


def ends(start, *steps):
    out = []
    for step in steps:
        start += step
        out.append(start)
    return out


def run_at(index, values):
    for value, events in values:
        if events:

            @pl.when(index == value)
            def _(events=events):
                for event in events:
                    event()


def columns(ref, start, size):
    return ref[:, :, :, :, :, pl.ds(start, size)].reshape(-1, size)


def turned(a, b):
    return lax.dot_general(a, b, (((1,), (1,)), ((), ())), preferred_element_type=jnp.float32)


def tallest(scores):
    part_max = jnp.max(scores.reshape(-1, 64, scores.shape[1]), axis=0)
    return jnp.max(part_max, axis=0, keepdims=True)


def swapped(block, cosine, sine):
    lane = lax.broadcasted_iota(jnp.int32, block.shape, 1)
    other = jnp.where(lane % 16 < 8, pltpu.roll(block, 120, 1), pltpu.roll(block, 8, 1))
    return block * cosine + other * sine


def tables():
    half = ROT // 2
    inverse = np.float32(10000.0) ** (-(np.arange(half, dtype=np.float32) * 2) / ROT)
    phase = np.arange(SEQ, dtype=np.float32)[:, None] * inverse.astype(np.float32)[None, :]
    cos_t, sin_t = np.cos(phase.astype(np.float64)), np.sin(phase.astype(np.float64))
    rest = np.zeros((SEQ, HD - ROT))
    cosine = np.concatenate([cos_t, cos_t, rest + 1.0] * 2, axis=1)
    sine = np.concatenate([-sin_t, sin_t, rest] * 2, axis=1)
    return jnp.asarray(cosine.astype(np.float32)), jnp.asarray(sine.astype(np.float32))


def scatter_pieces(blocks):
    r0, r1, r2, r3, r4 = (r for _, r, _ in blocks)
    w, q = D // 2, PACK // 4
    pieces = [(1, 0, r1, 0, 0, w), (0, 0, r0, 0, 0, q), (0, 0, r0, q, q, q)]
    for k in range(4):
        pieces += [(3, 0, r3, 0, 0, w), (2, 0, r2, 2 * w * k, w * k, w)]
    return pieces + [(4, 0, r4, 0, 0, SMALL // 2)]


SLOTS = 2


class Scatter:
    def __init__(self, lines, rows, blocks, grads, outs, buffers, sems):
        self.lines, self.rows, self.blocks = lines, rows, blocks
        self.grads, self.outs = grads, outs
        kinds = len(blocks)
        self.near, self.from_b, self.from_a, self.from_z, self.total, self.last = (
            buffers[kinds * k : kinds * (k + 1)] for k in range(6)
        )
        self.send, self.recv, self.credit = sems
        self.pieces = scatter_pieces(blocks)
        self.only = [(p - 3) // 2 if piece[0] == 3 else None for p, piece in enumerate(self.pieces)]
        self.z, self.x, self.y, self.c = place()
        self.xa, self.ya, self.xb, self.yb = partners()
        self.sibling = device(self.z, self.x, self.y, 1 - self.c)
        self.started = []

    def go(self, make):
        make().start()
        self.started.append((None, make))

    def where(self, p, body):
        if self.only[p] is None:
            body()
        else:
            pl.when(self.z == self.only[p])(body)

    def every(self, p):
        return slice(None) if self.only[p] is None else pl.ds(self.only[p], 1)

    def planes(self, p, body):
        if self.only[p] is None:
            pl.loop(0, self.lines)(body)
        else:
            body(self.only[p])

    def cut(self, p, ref, *lead):
        t, r0, nr, _, l0, w = self.pieces[p]
        return ref[t].at[(*lead, slice(None), pl.ds(r0, nr), pl.ds(l0, w))]

    def grad(self, p, z, x, y, half=None):
        half = self.c if half is None else half
        return part(self.pieces[p], self.grads[self.pieces[p][0]], z, x, y, half)

    def slot(self, p):
        t, _, _, _, l0, w = self.pieces[p]
        return {0: l0 // w, 1: 0, 2: l0 // w % SLOTS, 3: (p - 3) // 2 % SLOTS, 4: 0}[t]

    def near_copy(self, p):
        every = slice(None)
        mine = self.grad(p, self.every(p), every, every, 1 - self.c)
        near = self.near[self.pieces[p][0]].at[self.slot(p)]
        return remote(mine, near, self.send.at[p, 0], self.recv.at[p, 0], self.sibling)

    def b_copy(self, p, k):
        at = (self.xb, self.yb) if k == 0 else (1 - self.x, 1 - self.y)
        return remote(
            self.grad(p, self.every(p), *at),
            self.cut(p, self.from_b, k, self.every(p)),
            self.send.at[p, 1 + k],
            self.recv.at[p, 1 + k],
            device(self.z, self.xb, self.yb, self.c),
        )

    def a_copy(self, p):
        return remote(
            self.grad(p, self.every(p), self.xa, self.ya),
            self.cut(p, self.from_a, self.every(p)),
            self.send.at[p, 3],
            self.recv.at[p, 3],
            device(self.z, self.xa, self.ya, self.c),
        )

    def z_copy(self, p, d):
        other = lax.rem(self.z + d, self.lines)
        return remote(
            self.grad(p, other, self.x, self.y),
            self.cut(p, self.from_z, d - 1),
            self.send.at[p, 3 + d],
            self.recv.at[p, 3 + d],
            device(other, self.x, self.y, self.c),
        )

    def last_copy(self, p):
        t, r0, nr, _, l0, w = self.pieces[p]
        if self.blocks[t][0] == 2:
            src = self.total[t].at[1 - self.c, pl.ds(r0, nr), pl.ds(l0, w)]
            dst = self.last[t].at[pl.ds(r0, nr), pl.ds(l0, w)]
        else:
            away = pl.ds(pl.multiple_of((1 - self.c) * self.rows, 8), self.rows)
            src = self.total[t].at[0, away, pl.ds(l0, w)]
            dst = self.last[t].at[:, pl.ds(l0, w)]
        k = 3 + self.lines
        return remote(src, dst, self.send.at[p, k], self.recv.at[p, k], self.sibling)

    def uses(self, p):
        t = self.pieces[p][0]
        if t not in (2, 3):
            return False, False
        return p - 2 * SLOTS >= 3, p + 2 * SLOTS <= 10

    def first(self, p):
        if self.uses(p)[0]:
            pl.semaphore_wait(self.credit.at[self.pieces[p][0] - 2], 1)
        self.go(lambda: self.near_copy(p))

    def second(self, p):
        f32 = jnp.float32
        self.near_copy(p).wait_recv()
        near = self.near[self.pieces[p][0]].at[self.slot(p)]

        def add(k):
            for x in range(2):
                for y in range(2):
                    kept = self.grad(p, k, x, y)
                    got = near[0 if self.only[p] is not None else k, x, y]
                    kept[...] = (kept[...].astype(f32) + got.astype(f32)).astype(jnp.bfloat16)

        self.planes(p, add)
        if self.uses(p)[1]:
            credit = self.credit.at[self.pieces[p][0] - 2]
            pl.semaphore_signal(credit, inc=1, device_id=self.sibling, device_id_type=MESH)
        self.go(lambda: self.b_copy(p, 1))
        self.go(lambda: self.b_copy(p, 0))

    def third(self, p):
        self.b_copy(p, 1).wait_recv()

        def add(k):
            kept, got = self.grad(p, k, self.xa, self.ya), self.cut(p, self.from_b, 1, k)
            kept[...] = (kept[...].astype(jnp.float32) + got[...].astype(jnp.float32)).astype(jnp.bfloat16)

        self.planes(p, add)
        self.go(lambda: self.a_copy(p))

    def mine(self, p, k):
        got = self.cut(p, self.from_b, 0, k)[...].astype(jnp.float32) + self.cut(p, self.from_a, k)[...].astype(jnp.float32)
        return self.grad(p, k, self.x, self.y)[...].astype(jnp.float32) + got

    def fourth(self, p):
        self.b_copy(p, 0).wait_recv()
        self.a_copy(p).wait_recv()
        q = self.only[p]

        def send():
            for d in range(1, self.lines):
                self.go(functools.partial(self.z_copy, p, d))

        def round_off(k):
            self.grad(p, k, self.x, self.y)[...] = self.mine(p, k).astype(jnp.bfloat16)

        if q is None:

            @pl.loop(1, self.lines)
            def _(d):
                round_off(lax.rem(self.z + d, self.lines))

            send()
        else:

            def to_owner():
                return self.z_copy(p, lax.rem(q - self.z + self.lines, self.lines))

            @pl.when(self.z != q)
            def _():
                round_off(q)
                to_owner().start()

            self.started.append((lambda: self.z != q, to_owner))

        def keep():
            self.cut(p, self.total)[...] = self.mine(p, self.z if q is None else q)

        self.where(p, keep)

    def fifth(self, p):
        def body():
            for d in range(1, self.lines):
                self.z_copy(p, d).wait_recv()
            total = self.cut(p, self.total)
            acc = total[...]
            for d in range(1, self.lines):
                acc = acc + self.cut(p, self.from_z, d - 1)[...].astype(jnp.float32)
            total[...] = acc
            self.last_copy(p).start()

        self.where(p, body)
        q = self.only[p]
        self.started.append((None if q is None else lambda: self.z == q, lambda: self.last_copy(p)))

    def sixth(self, p):
        t, r0, nr, c0, l0, w = self.pieces[p]

        def body():
            self.last_copy(p).wait_recv()
            if self.blocks[t][0] == 2:
                kept = self.total[t][self.c, r0 : r0 + nr, l0 : l0 + w]
                got = self.last[t][r0 : r0 + nr, l0 : l0 + w]
                to = slice(r0, r0 + nr)
            else:
                kept = self.total[t][0, pl.ds(pl.multiple_of(self.c * self.rows, 8), self.rows), l0 : l0 + w]
                got = self.last[t][:, l0 : l0 + w]
                to = slice(None)
            h = HALF[t] + c0
            self.outs[t][to, c0 : c0 + w] = jnp.where(self.c == 0, kept, got)
            self.outs[t][to, h : h + w] = jnp.where(self.c == 0, got, kept)

        self.where(p, body)

    def steps(self):
        return [self.first, self.second, self.third, self.fourth, self.fifth, self.sixth]

    def timed(self, p, start):
        return [(start + lag, p, functools.partial(step, p)) for step, lag in zip(self.steps(), SCATTER_LAGS)]

    def finish(self):
        for condition, make in self.started:
            if condition is None:
                make().wait_send()
            else:

                @pl.when(condition())
                def _(make=make):
                    make().wait_send()


def crossed(a, b):
    return lax.dot_general(a, b, (((0,), (0,)), ((), ())), preferred_element_type=jnp.float32)


def layer_kernel(lines, rows, blocks, linked, total_rows, *refs):
    f32, bf16 = jnp.float32, jnp.bfloat16
    tags, subset_w, tokens_h, cotan_h, cosine_h, sine_h = refs[:6]
    given, refs = (refs[6:13], refs[13:]) if linked else (refs[6:10], refs[10:])
    mixed_h, grad_tokens_h, *results = refs[:7]
    tokens, cotan, cosine, sine, d_second, small, first_t, second_in, queries, pool, keys, keys_t = refs[7:19]
    values, values_t, attended, logsums, scaled, packed_d, mask, sums, d_keys, d_values, branch, second_t = refs[19:31]
    whole, grad_packed, grad_small, load_sems, out_sems = refs[31:35], refs[35], refs[36], refs[37], refs[38]
    refs = refs[39:]
    grads = [grad_packed, *whole[1:], grad_small]
    tiles, wide, qkv = SEQ // TILE, D // 2, D + 2 * HD

    def tile(k):
        return pl.ds(pl.multiple_of(k * TILE, TILE), TILE)

    pairs = [(tokens_h, tokens), (cosine_h, cosine), (sine_h, sine), (cotan_h, cotan)]
    if not linked:
        pairs += list(zip(given, whole))
    loads = [pltpu.make_async_copy(a, b, load_sems.at[k]) for k, (a, b) in enumerate(pairs)]
    for copy in loads:
        copy.start()
    if linked:
        query, pair, out, up, down, gains, biases = given
        packed, stages, square, gather_sems, refs = refs[0], refs[1:5], refs[5], refs[6:10], refs[10:]
        for p in range(H // 2):
            packed[:, place_of(p) : place_of(p) + 2 * HD] = query[:, 2 * HD * p : 2 * HD * (p + 1)]
        packed[:, PAIR : PAIR + 2 * HD] = pair[...]
        square[...] = jnp.zeros_like(square)
        square[0:2, 0:rows] = gains[...]
        square[2:4, 0:rows] = biases[...]
        spot = lax.broadcasted_iota(jnp.int32, (rows, 128), 1) == tags[0] + 4
        spot = jnp.where(lax.broadcasted_iota(jnp.int32, (rows, 128), 0) == 0, spot.astype(f32), 0.0)
        packed[:, qkv:] = square[...].T[:rows] + spot
        greet(lines)
        gather = Gather(lines, rows, blocks, [packed, out, up, down], stages, whole, gather_sems)
        scatter = Scatter(lines, rows, blocks, grads, results, refs[:30], refs[30:33])
        gather.begin(2)
        urgent, timed = gather.events()
    else:
        urgent, timed = [], []
    packed_w, out_w, up_w, down_w = whole

    steps = (PROJECT_STEPS, FORWARD_STEPS, OUTWARD_STEPS, BACKWARD_STEPS, CLOSE_STEPS, CHUNK_STEPS * 4, TOKEN_STEPS)
    starts, slots = [0], [0]
    for part_steps in steps:
        starts.append(starts[-1] + sum(part_steps))
        slots.append(slots[-1] + len(part_steps))
    if linked:
        edge = 0.01
        timed += scatter.timed(0, starts[3] - edge)
        ready = starts[3] + 4 * sum(BACKWARD_STEPS[:2])
        timed += [(ready - 2 * edge, 100, lambda: query_grads(0, PACK // 4))] + scatter.timed(1, ready - edge)
        timed += scatter.timed(2, starts[5] - edge)
        for q in range(4):
            start = starts[5] + q * sum(CHUNK_STEPS) + sum(CHUNK_STEPS[:6]) - edge
            timed += scatter.timed(3 + 2 * q, start) + scatter.timed(4 + 2 * q, start + sum(CHUNK_STEPS[6:]))
        timed += scatter.timed(11, starts[6] + edge)
    plan = deal(timed, ends(0.0, *(step for part_steps in steps for step in part_steps)))

    def slot(section, index, values):
        run_at(index, [(v, plan[slots[section] + v]) for v in values])

    row = lax.broadcasted_iota(jnp.int32, (TILE, TILE), 0)
    column = lax.broadcasted_iota(jnp.int32, (TILE, TILE), 1)
    mask[...] = jnp.where(row <= column, 0.0, -1e30)
    sums[...] = jnp.zeros_like(sums)
    d_keys[...] = jnp.zeros_like(d_keys)
    d_values[...] = jnp.zeros_like(d_values)
    lane = lax.broadcasted_iota(jnp.int32, (TILE, 2 * HD), 1)
    left = lane < HD
    loads[0].wait()

    def normed(k):
        inputs = tokens[tile(k), :].astype(f32)
        centred = inputs - jnp.mean(inputs, axis=-1, keepdims=True)
        inv_std = lax.rsqrt(jnp.mean(centred * centred, axis=-1, keepdims=True) + eps_norm)
        return centred * inv_std, inv_std

    @pl.loop(0, tiles)
    def _(k):
        d_second[tile(k), :] = normed(k)[0]

    for copy in loads[1:]:
        copy.wait()
    for event in urgent:
        event()
    small[...] = columns(packed_w, qkv, 128).astype(f32).T

    @pl.loop(0, tiles)
    def _(k):
        norm = d_second[tile(k), :]
        a1 = (norm * small[0:1, :] + small[2:3, :]).astype(bf16)
        a2 = norm * small[1:2, :] + small[3:4, :]
        first_t[:, tile(k)] = a1.T
        second_in[tile(k), :] = a2.astype(bf16)
        second_t[:, tile(k)] = a2.astype(bf16).T
        mixed = jnp.dot(a1, columns(packed_w, 0, qkv), preferred_element_type=f32)
        cos_t, sin_t = cosine[tile(k), :], sine[tile(k), :]
        for p in range(H // 2):
            turn = swapped(mixed[:, place_of(p) : place_of(p) + 2 * HD], cos_t, sin_t).astype(bf16).astype(f32)
            turn = turn * (LOG2E / 8)
            high = turn.astype(bf16).astype(f32)
            low = turn - high
            queries[2 * p, tile(k), :] = jnp.where(left, high, pltpu.roll(low, HD, 1)).astype(bf16)
            queries[2 * p + 1, tile(k), :] = jnp.where(left, pltpu.roll(high, HD, 1), low).astype(bf16)
        pair_t = mixed[:, PAIR : PAIR + 2 * HD]
        pair_t = jnp.where(left, swapped(pair_t, cos_t, sin_t), pair_t).astype(bf16).astype(f32)
        other = pltpu.roll(pair_t, HD, 1)
        both = jnp.where(left, pair_t, other)
        keys[tile(k), :] = both.astype(bf16)
        keys_t[:, tile(k)] = both.T[:HD].astype(bf16)
        values[tile(k), :] = jnp.where(left, other, jnp.where(lane < HD + 2, -1.0, 0.0)).astype(bf16)
        values_t[:, tile(k)] = jnp.where(left, other, jnp.where(lane == HD, 1.0, 0.0)).T.astype(bf16)
        slot(0, k, range(tiles))

    @pl.loop(0, H // 2)
    def _(pr):
        work = [(i, hh) for i in range(tiles) for hh in range(2)]
        ready, shares, heads = {}, {}, {}

        def score(n):
            i, hh = work[n]
            count = TILE * (i + 1)
            ready[n] = turned(keys[0:count, :], queries[pr * 2 + hh, i * TILE : count, :])

        def weigh(n):
            i, hh = work[n]
            count = TILE * (i + 1)
            scores = ready.pop(n)
            last = scores[count - TILE :] + mask[...]
            peak = tallest(last)
            if i:
                peak = jnp.maximum(peak, tallest(scores[: count - TILE]))
            probs = jnp.exp2(last - peak).astype(bf16)
            if i:
                probs = jnp.concatenate([jnp.exp2(scores[: count - TILE] - peak).astype(bf16), probs], axis=0)
            shares[n] = peak, probs

        def collect(n):
            i, hh = work[n]
            count = TILE * (i + 1)
            peak, probs = shares.pop(n)
            got = jnp.dot(values_t[0:80, 0:count], probs, preferred_element_type=f32)
            total = got[HD : HD + 1]
            heads[hh] = got[:HD] * (1.0 / total)
            logsums[pr * 2 + hh, :, i * TILE : count] = peak + jnp.log2(total)
            if hh:
                both = jnp.concatenate([heads[0], heads[1]], axis=0).T
                attended[i * TILE : count, lanes(pr * 2 * HD, 2 * HD)] = both.astype(bf16)

        ahead = 2
        for n in range(len(work) + ahead + 2):
            if n < len(work):
                score(n)
            if 0 <= n - ahead < len(work):
                weigh(n - ahead)
            if 0 <= n - ahead - 2 < len(work):
                collect(n - ahead - 2)
        for i in (0, 1):
            slot(1, pr * 2 + i, range(i, 2 * (H // 2), 2))

    kind = lax.broadcasted_iota(jnp.int32, (128, D), 0)
    count = jnp.sum(jnp.where(kind == tags[0] + 4, small[...], 0.0), keepdims=True)
    subset = lax.broadcasted_iota(jnp.int32, subset_w.shape, 1)
    weight = jnp.sum(jnp.where(subset == tags[0], subset_w[...], 0.0), keepdims=True)
    scale = weight / count * (total_rows / SUBSETS)

    @pl.loop(0, tiles)
    def _(k):
        grad_out = (cotan[tile(k), :].astype(f32) * scale).astype(bf16)
        scaled[tile(k), :] = grad_out
        heads = attended[tile(k), :]
        out_m = out_w[...].reshape(D, D)
        branch[tile(k), :] = tokens[tile(k), :].astype(f32) + jnp.dot(heads, out_m, preferred_element_type=f32)
        d_heads_t = turned(grad_out, out_m).astype(bf16).astype(f32)
        for p in range(H // 2):
            block = d_heads_t[:, 2 * HD * p : 2 * HD * (p + 1)]
            product = block * heads[:, 2 * HD * p : 2 * HD * (p + 1)].astype(f32)
            for hh, (mine, there) in enumerate(((left, block), (~left, pltpu.roll(block, HD, 1)))):
                delta = jnp.sum(jnp.where(mine, product, 0.0), axis=1, keepdims=True)
                high = delta.astype(bf16).astype(f32)
                extra = jnp.where(lane == HD, high, jnp.where(lane == HD + 1, delta - high, 0.0))
                pool[2 * p + hh, tile(k), :] = jnp.where(left, there, extra).astype(bf16)
        slot(2, k, range(tiles))

    if linked:
        gather.sent(1)

    @pl.loop(0, 2)
    def _(k):
        got = crossed(attended[:, lanes(k * wide, wide)], scaled[...]).astype(bf16)
        grads[1][pl.ds(2 * k, 2)] = got.reshape(2, 2, 2, 1, D // 16, D)
        slot(2, tiles + k, range(tiles, tiles + 2))

    def query_grads(start, stop):
        for span in (slice(start, stop), slice(PACK // 2 + start, min(PACK // 2 + stop, qkv))):
            for k in range(2):
                got = jnp.dot(first_t[k * wide : (k + 1) * wide, :], packed_d[:, span], preferred_element_type=f32).astype(bf16)
                grad_packed[2 * k : 2 * k + 2, :, :, :, :, span] = got.reshape(2, 2, 2, 1, D // 16, -1)

    @pl.loop(0, H // 2)
    def _(pr):
        work = [(i, hh) for i in range(tiles) for hh in range(2)]
        ready, shares, d_query = {}, {}, {}

        def score(n):
            i, hh = work[n]
            count, span = TILE * (i + 1), slice(i * TILE, TILE * (i + 1))
            head = pr * 2 + hh
            ready[n] = turned(keys[0:count, :], queries[head, span, :]), turned(values[0:count, :], pool[head, span, :])

        def weigh(n):
            i, hh = work[n]
            count, span = TILE * (i + 1), slice(i * TILE, TILE * (i + 1))
            scores, d_probs = ready.pop(n)
            shift = logsums[pr * 2 + hh, :, span]
            probs = jnp.exp2(scores[count - TILE :] + mask[...] - shift)
            if i:
                probs = jnp.concatenate([jnp.exp2(scores[: count - TILE] - shift), probs], axis=0)
            shares[n] = probs.astype(bf16), (probs * d_probs).astype(bf16)

        def collect(n):
            i, hh = work[n]
            count, span = TILE * (i + 1), slice(i * TILE, TILE * (i + 1))
            d_query[hh] = jnp.dot(keys_t[:, 0:count], shares[n][1], preferred_element_type=f32)
            if hh:
                both = [shares.pop(n - 1), shares.pop(n)]
                for acc, k, other in ((d_values, 0, pool), (d_keys, 1, queries)):
                    two = jnp.concatenate([other[pr * 2, span, :], other[pr * 2 + 1, span, :]], axis=0)
                    parts = jnp.concatenate([both[0][k], both[1][k]], axis=1)
                    acc[0:count, :] += jnp.dot(parts, two, preferred_element_type=f32)
                d_q = jnp.concatenate([d_query[0], d_query[1]], axis=0).T * 0.125
                d_q = swapped(d_q, cosine[span, :], -sine[span, :])
                packed_d[span, lanes(place_of(pr), 2 * HD)] = d_q.astype(bf16)

        for n in range(len(work) + 2 + 1):
            if n < len(work):
                score(n)
            if 0 <= n - 2 < len(work):
                weigh(n - 2)
            if 0 <= n - 2 - 1 < len(work):
                collect(n - 2 - 1)
        for i in (0, 1):
            slot(3, pr * 2 + i, range(i, 2 * (H // 2), 2))

    @pl.loop(0, tiles)
    def _(k):
        d_key = d_keys[tile(k), :]
        d_key = (d_key + pltpu.roll(d_key, HD, 1)) * (1.0 / LOG2E)
        d_key = swapped(d_key, cosine[tile(k), :], -sine[tile(k), :])
        d_pair = jnp.where(left, d_key, pltpu.roll(d_values[tile(k), :], HD, 1)).astype(bf16)
        packed_d[tile(k), PAIR : PAIR + 2 * HD] = d_pair
        d_first = turned(packed_d[tile(k), 0:qkv], columns(packed_w, 0, qkv))
        sums[0:1, :] += jnp.sum(d_first * normed(k)[0], axis=0, keepdims=True)
        sums[2:3, :] += jnp.sum(d_first, axis=0, keepdims=True)
        slot(4, k, range(tiles))

    if not linked:
        query_grads(0, PACK // 4)
    query_grads(PACK // 4, PACK // 2)
    grad_packed[:, :, :, :, :, qkv:] = jnp.zeros((4, 2, 2, 1, D // 16, PACK - qkv), bf16)
    for event in plan[slots[4] + tiles]:
        event()
    if linked:
        gather.sent(2, 3)

    @pl.loop(0, 4)
    def _(q):
        def up_m():
            return columns(up_w, pl.multiple_of(q * D, D), D)

        def down_m():
            return down_w[q].reshape(D, D)

        @pl.loop(0, tiles)
        def _(k):
            pre = jnp.dot(second_in[tile(k), :], up_m(), preferred_element_type=f32)
            d_hidden = turned(scaled[tile(k), :], down_m())
            cdf = 0.5 + 0.5 * lax.erf(pre * 0.7071067811865476)
            density = jnp.exp2(pre * pre * (-0.5 * LOG2E)) * 0.3989422804014327
            active = (pre * cdf).astype(bf16)
            d_up = (d_hidden * (cdf + pre * density)).astype(bf16)
            active_t = active.T
            for b in range(2):
                queries[2 * k + b, 0:D, :] = active_t[:, 128 * b : 128 * (b + 1)]
            for b in range(6):
                pool[b, tile(k), :] = d_up[:, 128 * b : 128 * (b + 1)]
            branch[tile(k), :] += jnp.dot(active, down_m(), preferred_element_type=f32)
            got = turned(d_up, up_m())
            d_second[tile(k), :] = jnp.where(q == 0, got, got + d_second[tile(k), :])
            slot(5, q * 8 + k, [v for v in range(32) if v % 8 < 4])

        hidden_t = jnp.concatenate([queries[b, 0:D, :] for b in range(8)], axis=1)
        got = jnp.dot(hidden_t, scaled[...], preferred_element_type=f32).astype(bf16)
        down_w[q] = got.reshape(2, 2, 2, 4 * D // 32, D)
        for v in (4, 5):
            slot(5, q * 8 + v, [8 * p + v for p in range(4)])
        if linked:
            run_at(q, [(v, [functools.partial(gather.sent, 4 + v)]) for v in range(4)])
        d_ups = jnp.concatenate([pool[b] for b in range(6)], axis=1)
        got = jnp.dot(second_t[...], d_ups, preferred_element_type=f32).astype(bf16)
        up_w[:, :, :, :, :, lanes(q * D, D)] = got.reshape(4, 2, 2, 1, D // 16, D)
        for v in (6, 7):
            slot(5, q * 8 + v, [8 * p + v for p in range(4)])

    @pl.loop(0, tiles)
    def _(k):
        second = d_second[tile(k), :]
        sums[1:2, :] += jnp.sum(second * normed(k)[0], axis=0, keepdims=True)
        sums[3:4, :] += jnp.sum(second, axis=0, keepdims=True)
        attended[tile(k), :] = branch[tile(k), :].astype(bf16)

    flushed = [pltpu.make_async_copy(attended, mixed_h, out_sems.at[0])]
    flushed[0].start()
    grad_small[:, :, :, :, :, 0:128] = sums[...].T.astype(bf16).reshape(4, 2, 2, 1, D // 16, 128)
    grad_small[:, :, :, :, :, 128:] = jnp.zeros((4, 2, 2, 1, D // 16, SMALL - 128), bf16)

    @pl.loop(0, tiles)
    def _(k):
        norm, inv_std = normed(k)
        d_first = turned(packed_d[tile(k), 0:qkv], columns(packed_w, 0, qkv))
        d_normed = d_first * small[0:1, :] + d_second[tile(k), :] * small[1:2, :]
        inner = jnp.mean(d_normed * norm, axis=-1, keepdims=True)
        d_inputs = inv_std * (d_normed - jnp.mean(d_normed, axis=-1, keepdims=True) - norm * inner)
        second_in[tile(k), :] = (cotan[tile(k), :].astype(f32) * scale + d_inputs).astype(bf16)
        slot(6, k, range(tiles))

    flushed.append(pltpu.make_async_copy(second_in, grad_tokens_h, out_sems.at[1]))
    flushed[-1].start()
    for event in plan[-1]:
        event()
    if linked:
        gather.sent(0)
        scatter.finish()
    else:
        for t in range(5):
            flushed.append(pltpu.make_async_copy(grads[t], results[t], out_sems.at[2 + t]))
            flushed[-1].start()
    for copy in flushed:
        copy.wait()


def layer(linked, lines, rows, rows_down, total_rows, tags, subset_w, tokens, cotan, cosine, sine, weights):
    blocks = layout(rows, rows_down)
    f32, bf16 = jnp.float32, jnp.bfloat16
    shapes = [(lines, 2, 2, g, r, k) for g, r, k in blocks]
    own_rows = [r if g == 2 else rows for g, r, k in blocks]
    vmem = pl.BlockSpec(memory_space=pltpu.VMEM)
    anywhere = pl.BlockSpec(memory_space=pl.ANY)
    if linked:
        results = [jax.ShapeDtypeStruct((o, k), f32) for o, (g, r, k) in zip(own_rows, blocks)]
    else:
        weights = [a.reshape(shape) for a, shape in zip(weights, shapes)]
        results = [jax.ShapeDtypeStruct(shape, bf16) for shape in shapes]
    tall = (SEQ, D)
    buffers = [
        (tall, bf16),
        (tall, bf16),
        ((SEQ, 2 * HD), f32),
        ((SEQ, 2 * HD), f32),
        (tall, f32),
        ((128, D), f32),
        ((D, SEQ), bf16),
        (tall, bf16),
        ((H, SEQ, 2 * HD), bf16),
        ((H, SEQ, 2 * HD), bf16),
        ((SEQ, 2 * HD), bf16),
        ((HD, SEQ), bf16),
        ((SEQ, 2 * HD), bf16),
        ((2 * HD, SEQ), bf16),
        (tall, bf16),
        ((H, 1, SEQ), f32),
        (tall, bf16),
        ((SEQ, D + 2 * HD), bf16),
        ((TILE, TILE), f32),
        ((128, D), f32),
        ((SEQ, 2 * HD), f32),
        ((SEQ, 2 * HD), f32),
        (tall, f32),
        ((D, SEQ), bf16),
    ]
    buffers += [(shape, bf16) for shape in shapes[:4]] + [(shapes[0], bf16), (shapes[4], bf16)]
    scratch = [pltpu.VMEM(shape, kind) for shape, kind in buffers]
    scratch += [pltpu.SemaphoreType.DMA((8,)), pltpu.SemaphoreType.DMA((7,))]
    if linked:
        scratch += [pltpu.VMEM((rows, PACK), f32)]
        scratch += [pltpu.VMEM((g, r, k // 2), f32) for g, r, k in blocks[:4]]
        scratch += [pltpu.VMEM((128, 128), f32)]
        count, kinds = len(gather_pieces(blocks)), 4 * lines + 3
        scratch += [pltpu.SemaphoreType.DMA((count,))] * 2 + [pltpu.SemaphoreType.DMA((count, kinds))] * 2
        near = [(2, lines, PACK // 4), (1, lines, D // 2), (SLOTS, lines, D // 2), (SLOTS, 1, D // 2), (1, lines, SMALL // 2)]
        scratch += [pltpu.VMEM((n, z, 2, 2, g, r, w), bf16) for (n, z, w), (g, r, k) in zip(near, blocks)]
        for lead in ((2, lines), (lines,), (lines - 1,)):
            scratch += [pltpu.VMEM((*lead, g, r, k // 2), bf16) for g, r, k in blocks]
        scratch += [pltpu.VMEM((g, r, k // 2), f32) for g, r, k in blocks]
        scratch += [pltpu.VMEM((o, k // 2), f32) for o, (g, r, k) in zip(own_rows, blocks)]
        count = len(scatter_pieces(blocks))
        scratch += [pltpu.SemaphoreType.DMA((count, lines + 4))] * 2 + [pltpu.SemaphoreType.REGULAR((2,))]
    return pl.pallas_call(
        functools.partial(layer_kernel, lines, rows, blocks, linked, total_rows),
        out_shape=[jax.ShapeDtypeStruct(tall, bf16)] * 2 + results,
        in_specs=[pl.BlockSpec(memory_space=pltpu.SMEM), vmem] + [anywhere] * 4 + [vmem if linked else anywhere] * len(weights),
        out_specs=[anywhere] * 2 + [vmem if linked else anywhere] * 5,
        scratch_shapes=scratch,
        compiler_params=pltpu.CompilerParams(
            collective_id=0 if linked else None, has_side_effects=linked, vmem_limit_bytes=63 * 2**20
        ),
        name="layer",
    )(tags, subset_w, tokens, cotan, cosine, sine, *weights)


def finish_kernel(rows, *refs):
    packed, small, *rest = refs[:7]
    query, pair, gains, biases, *to = refs[7:]
    for p in range(H // 2):
        query[:, 2 * HD * p : 2 * HD * (p + 1)] = packed[:, place_of(p) : place_of(p) + 2 * HD]
    pair[...] = packed[:, PAIR : PAIR + 2 * HD]
    turned_back = small[:, 0:128].T
    gains[...] = turned_back[0:2]
    biases[...] = turned_back[2:4]
    for a, b in zip(rest, to):
        b[...] = a[...]


def finish(rows, packed, small, *rest):
    f32 = jnp.float32
    vmem = pl.BlockSpec(memory_space=pltpu.VMEM)
    shapes = [(rows, D), (rows, 2 * HD), (2, rows), (2, rows)]
    return pl.pallas_call(
        functools.partial(finish_kernel, rows),
        out_shape=[jax.ShapeDtypeStruct(a, f32) for a in shapes] + [jax.ShapeDtypeStruct(a.shape, a.dtype) for a in rest],
        in_specs=[vmem] * (2 + len(rest)),
        out_specs=[vmem] * (4 + len(rest)),
        compiler_params=pltpu.CompilerParams(vmem_limit_bytes=63 * 2**20),
        name="finish",
    )(packed, small, *rest)


def is_linked(rows):
    return lax.axis_size("dp") == 8 and lax.axis_size("fsdp") == 4 and rows % 8 == 0


def fetch_weights(query_w, pair_w, out_w, up_w, down_w, gains, biases, tags):
    onehot = (tags[0] == jnp.arange(SUBSETS, dtype=jnp.int32)).astype(jnp.float32)
    own_counts = jnp.where((jnp.arange(query_w.shape[0]) == 0)[:, None], onehot[None, :], 0.0)
    small = jnp.concatenate([gains.T, biases.T, own_counts], axis=1)
    small = jnp.pad(small, ((0, 0), (0, 128 - small.shape[1])))
    pairs = [query_w[:, 2 * HD * p : 2 * HD * (p + 1)] for p in range(H // 2)]
    packed = jnp.concatenate([*pairs[0::2], pair_w, *pairs[1::2], small], axis=1)
    return [
        lax.all_gather(a.astype(jnp.bfloat16), ("dp", "fsdp"), axis=0, tiled=True)
        for a in (packed, out_w, up_w, down_w)
    ]


def body(
    tokens,
    w_query,
    w_pair,
    w_attn_out,
    w_up,
    w_down,
    ln_gains,
    ln_biases,
    cotangent,
    subset_tags,
    subset_weights,
):
    cosine, sine = tables()
    linked = is_linked(w_query.shape[0])
    shards = (w_query, w_pair, w_attn_out, w_up, w_down, ln_gains, ln_biases)
    total_rows = lax.axis_size("dp") * lax.axis_size("fsdp")
    if linked:
        lines, rows, rows_down = lax.axis_size("dp") // 2, w_query.shape[0], w_down.shape[0]
    else:
        lines, rows, rows_down = 4, D // 32, 4 * D // 32
        shards = fetch_weights(*shards, subset_tags)
    subset_w = subset_weights.reshape(1, SUBSETS)
    mixed, grad_tokens, *grads = layer(
        linked, lines, rows, rows_down, total_rows, subset_tags, subset_w, tokens, cotangent, cosine, sine, shards
    )
    if not linked:
        grads = [
            lax.psum_scatter(
                g.astype(jnp.float32).reshape(-1, g.shape[-1]), ("dp", "fsdp"), scatter_dimension=0, tiled=True
            )
            for g in grads
        ]
    packed_g, out_g, up_g, down_g, small_g = grads
    query_g, pair_g, gains_g, biases_g, out_g, up_g, down_g, grad_tokens, mixed = finish(
        w_query.shape[0], packed_g, small_g, out_g, up_g, down_g, grad_tokens, mixed
    )
    return mixed, grad_tokens, query_g, pair_g, out_g, up_g, down_g, gains_g, biases_g


def solution(mesh):
    in_specs = (
        P(("dp", "fsdp"), None),
        P(("dp", "fsdp"), None),
        P(("dp", "fsdp"), None),
        P(("dp", "fsdp"), None),
        P(("dp", "fsdp"), None),
        P(("dp", "fsdp"), None),
        P(None, ("dp", "fsdp")),
        P(None, ("dp", "fsdp")),
        P(("dp", "fsdp"), None),
        P(("dp", "fsdp")),
        P(),
    )
    out_specs = (
        P(("dp", "fsdp"), None),
        P(("dp", "fsdp"), None),
        P(("dp", "fsdp"), None),
        P(("dp", "fsdp"), None),
        P(("dp", "fsdp"), None),
        P(("dp", "fsdp"), None),
        P(("dp", "fsdp"), None),
        P(None, ("dp", "fsdp")),
        P(None, ("dp", "fsdp")),
    )
    return jax.shard_map(body, mesh=mesh, in_specs=in_specs, out_specs=out_specs, check_vma=False)
```

```python
import functools

import jax
import jax.numpy as jnp
import numpy as np
from jax import lax
from jax.experimental import pallas as pl
from jax.experimental.pallas import tpu as pltpu
from jax.sharding import PartitionSpec as P

D = 768
H = 12
HD = 64
ROT = 16
SUBSETS = 22
SEQ = 1024
PACK = 1024
TILE = 256
LOG2E = 1.4426950408889634
PAIR = 3 * 128
SMALL = 256
GATHER_STARTS = (0.0, -6.0, 0.0, 8.0, 17.0, 22.0, 27.0, 32.0)
GATHER_LAGS = (0.0, 10.0, 20.0, 22.0)
SCATTER_LAGS = (0.0, 2.5, 10.0, 17.0, 24.0, 27.0)
PROJECT_STEPS = (1.5,) * 4
FORWARD_STEPS = (1.7, 0.1) * 6
OUTWARD_STEPS = (1.5,) * 4 + (0.85,) * 2
BACKWARD_STEPS = (3.2, 0.1) * 6
CLOSE_STEPS = (0.2,) * 4 + (1.0,)
CHUNK_STEPS = (1.4, 1.4, 1.4, 1.4, 1.2, 0.1, 1.2, 0.1)
TOKEN_STEPS = (0.7,) * 4 + (0.5,) * 4
MESH = pl.DeviceIdType.MESH


eps_norm = 1e-05


def place_of(p):
    return (p % 2) * (PACK // 2) + (p // 2) * 2 * HD


def place():
    dp, fs = lax.axis_index("dp"), lax.axis_index("fsdp")
    return dp // 2, dp % 2, fs // 2, fs % 2


def device(z, x, y, c):
    return (z * 2 + x, y * 2 + c)


def partners():
    z, x, y, c = place()
    xa, ya = jnp.where(c == 0, 1 - x, x), jnp.where(c == 0, y, 1 - y)
    xb, yb = jnp.where(c == 0, x, 1 - x), jnp.where(c == 0, 1 - y, y)
    return xa, ya, xb, yb


def greet(lines):
    z, x, y, c = place()
    barrier = pltpu.get_barrier_semaphore()
    others = [device(lax.rem(z + d, lines), x, y, c) for d in range(1, lines)]
    others += [device(z, 1 - x, y, c), device(z, x, 1 - y, c), device(z, x, y, 1 - c)]
    for other in others:
        pl.semaphore_signal(barrier, inc=1, device_id=other, device_id_type=MESH)
    pl.semaphore_wait(barrier, len(others))


def remote(src, dst, send, recv, where):
    return pltpu.make_async_remote_copy(
        src_ref=src, dst_ref=dst, send_sem=send, recv_sem=recv, device_id=where, device_id_type=MESH
    )


def layout(rows, rows_down):
    return [(1, 2 * rows, PACK), (1, 2 * rows, D), (1, 2 * rows, 4 * D), (2, rows_down, D), (1, 2 * rows, SMALL)]


HALF = (PACK // 2, D // 2, D // 2, D // 2, SMALL // 2)


def lanes(start, size):
    return pl.ds(pl.multiple_of(start, 128), size)


def part(piece, ref, z, x, y, half):
    t, r0, nr, c0, _, w = piece
    return ref.at[z, x, y, :, pl.ds(r0, nr), lanes(half * HALF[t] + c0, w)]


def gather_pieces(blocks):
    r0, r1, r2, r3 = (r for _, r, _ in blocks[:4])
    w, half = D // 2, r3 // 2 // 16 * 16
    ups = [(2, 0, r2, 2 * w * k, w * k, w) for k in range(4)]
    downs = [(3, 0, half, 0, 0, w), (3, half, r3 - half, 0, 0, w)]
    return [(0, 0, r0, 0, 0, PACK // 2), (1, 0, r1, 0, 0, w), *downs, *ups]


class Gather:
    def __init__(self, lines, rows, blocks, sources, stages, whole, sems):
        self.lines, self.rows, self.blocks = lines, rows, blocks
        self.sources, self.stages, self.whole = sources, stages, whole
        self.swap_send, self.swap_recv, self.send, self.recv = sems
        self.pieces = gather_pieces(blocks)
        self.z, self.x, self.y, self.c = place()
        self.xa, self.ya, self.xb, self.yb = partners()
        self.sibling = device(self.z, self.x, self.y, 1 - self.c)
        self.started = []

    def go(self, p, make):
        make().start()
        self.started.append((p, make))

    def stage_rows(self, p, core):
        t, r0, nr, _, l0, w = self.pieces[p]
        if self.blocks[t][0] == 2:
            return self.stages[t].at[core, pl.ds(r0, nr), pl.ds(l0, w)]
        return self.stages[t].at[0, pl.ds(pl.multiple_of(core * self.rows, 8), self.rows), pl.ds(l0, w)]

    def source(self, p):
        t, r0, nr, c0, _, w = self.pieces[p]
        return self.sources[t].at[pl.ds(r0, nr) if self.blocks[t][0] == 2 else slice(None)], c0, w

    def swap(self, p):
        source, c0, w = self.source(p)
        mine = source.at[:, lanes((1 - self.c) * HALF[self.pieces[p][0]] + c0, w)]
        return remote(mine, self.stage_rows(p, self.c), self.swap_send.at[p], self.swap_recv.at[p], self.sibling)

    def block(self, p, d, x, y):
        z = lax.rem(self.z + self.lines - d, self.lines)
        return part(self.pieces[p], self.whole[self.pieces[p][0]], z, x, y, self.c)

    def direct(self, p, d, back=0):
        block = self.block(p, back, self.x, self.y)
        where = device(lax.rem(self.z + d, self.lines), self.x, self.y, self.c)
        return remote(block, block, self.send.at[p, d - 1], self.recv.at[p, d - 1], where)

    def to_a(self, p, d, x, y):
        block, k = self.block(p, d, x, y), self.lines - 1 + d
        return remote(block, block, self.send.at[p, k], self.recv.at[p, k], device(self.z, self.xa, self.ya, self.c))

    def to_b(self, p, d, x, y, second=0):
        block, k = self.block(p, d, x, y), self.lines * (2 + second) - 1 + d
        return remote(block, block, self.send.at[p, k], self.recv.at[p, k], device(self.z, self.xb, self.yb, self.c))

    def share(self, p, k, x, y, half):
        column = part(self.pieces[p], self.whole[self.pieces[p][0]], slice(None), x, y, half)
        k = 4 * self.lines - 1 + k
        return remote(column, column, self.send.at[p, k], self.recv.at[p, k], self.sibling)

    def own(self, p):
        x, y = self.x, self.y
        self.go(p, lambda: self.to_a(p, 0, x, y))
        self.go(p, lambda: self.to_b(p, 0, x, y))

    def begin(self, ahead):
        for p in range(len(self.pieces)):
            self.go(p, functools.partial(self.swap, p))
        self.ahead = ahead
        self.place_own(range(ahead))

    def place_own(self, some):
        for p in some:
            t, r0, nr, c0, l0, w = self.pieces[p]
            source, _, _ = self.source(p)
            kept = jnp.where(self.c == 0, source[:, c0 : c0 + w], source[:, HALF[t] + c0 : HALF[t] + c0 + w])
            self.stage_rows(p, self.c)[...] = kept
            self.swap(p).wait_recv()
            held = self.stages[t][:, r0 : r0 + nr, l0 : l0 + w]
            self.block(p, 0, self.x, self.y)[...] = held.astype(jnp.bfloat16)
            for d in range(1, self.lines):
                self.go(p, functools.partial(self.direct, p, d))
            if p < self.ahead:
                self.own(p)

    def first(self, p):
        x, y, c = self.x, self.y, self.c
        if p >= self.ahead:
            self.own(p)
        for d in range(1, self.lines):
            self.direct(p, d, back=d).wait_recv()
            self.go(p, functools.partial(self.to_a, p, d, x, y))
            self.go(p, functools.partial(self.to_b, p, d, x, y))
        self.go(p, lambda: self.share(p, 0, x, y, c))

    def second(self, p):
        for d in range(self.lines):
            self.to_a(p, d, self.xa, self.ya).wait_recv()
            self.go(p, functools.partial(self.to_b, p, d, self.xa, self.ya, 1))
        self.go(p, lambda: self.share(p, 1, self.xa, self.ya, self.c))

    def third(self, p):
        x, y = self.x, self.y
        for d in range(self.lines):
            self.to_b(p, d, self.xb, self.yb).wait_recv()
        self.go(p, lambda: self.share(p, 2, self.xb, self.yb, self.c))
        for d in range(self.lines):
            self.to_b(p, d, 1 - x, 1 - y, 1).wait_recv()
        self.go(p, lambda: self.share(p, 3, 1 - x, 1 - y, self.c))

    def fourth(self, p):
        x, y, c = self.x, self.y, 1 - self.c
        for k, sx, sy in ((0, x, y), (1, self.xb, self.yb), (2, self.xa, self.ya), (3, 1 - x, 1 - y)):
            self.share(p, k, sx, sy, c).wait_recv()

    def events(self):
        steps = (self.first, self.second, self.third, self.fourth)
        urgent = [(0, 0), (0, 1), (1, 0), (2, 0), (3, 0)]
        timed = []
        for p in range(1, len(self.pieces)):
            for k, lag in enumerate(GATHER_LAGS):
                if (k, p) not in urgent:
                    timed.append((GATHER_STARTS[p] + lag, len(timed), functools.partial(steps[k], p)))
        urgent = [functools.partial(steps[k], p) for k, p in urgent]
        rest = functools.partial(self.place_own, range(self.ahead, len(self.pieces)))
        return urgent[:1] + [rest] + urgent[1:], timed

    def sent(self, *pieces):
        for p, make in self.started:
            if p in pieces:
                make().wait_send()


def deal(timed, times):
    plan = [[] for _ in range(len(times) + 1)]
    for when, _, event in sorted(timed, key=lambda e: e[:2]):
        plan[next((k for k, t in enumerate(times) if t >= when), len(times))].append(event)
    return plan


def ends(start, *steps):
    out = []
    for step in steps:
        start += step
        out.append(start)
    return out


def run_at(index, values):
    for value, events in values:
        if events:

            @pl.when(index == value)
            def _(events=events):
                for event in events:
                    event()


def columns(ref, start, size):
    return ref[:, :, :, :, :, pl.ds(start, size)].reshape(-1, size)


def turned(a, b):
    return lax.dot_general(a, b, (((1,), (1,)), ((), ())), preferred_element_type=jnp.float32)


def tallest(scores):
    part_max = jnp.max(scores.reshape(-1, 64, scores.shape[1]), axis=0)
    return jnp.max(part_max, axis=0, keepdims=True)


def swapped(block, cosine, sine):
    lane = lax.broadcasted_iota(jnp.int32, block.shape, 1)
    other = jnp.where(lane % 16 < 8, pltpu.roll(block, 120, 1), pltpu.roll(block, 8, 1))
    return block * cosine + other * sine


def tables():
    half = ROT // 2
    inverse = np.float32(10000.0) ** (-(np.arange(half, dtype=np.float32) * 2) / ROT)
    phase = np.arange(SEQ, dtype=np.float32)[:, None] * inverse.astype(np.float32)[None, :]
    cos_t, sin_t = np.cos(phase.astype(np.float64)), np.sin(phase.astype(np.float64))
    rest = np.zeros((SEQ, HD - ROT))
    cosine = np.concatenate([cos_t, cos_t, rest + 1.0] * 2, axis=1)
    sine = np.concatenate([-sin_t, sin_t, rest] * 2, axis=1)
    return jnp.asarray(cosine.astype(np.float32)), jnp.asarray(sine.astype(np.float32))


def scatter_pieces(blocks):
    r0, r1, r2, r3, r4 = (r for _, r, _ in blocks)
    w, q = D // 2, PACK // 4
    pieces = [(1, 0, r1, 0, 0, w), (0, 0, r0, 0, 0, q), (0, 0, r0, q, q, q)]
    for k in range(4):
        pieces += [(3, 0, r3, 0, 0, w), (2, 0, r2, 2 * w * k, w * k, w)]
    return pieces + [(4, 0, r4, 0, 0, SMALL // 2)]


SLOTS = 2


class Scatter:
    def __init__(self, lines, rows, blocks, grads, outs, buffers, sems):
        self.lines, self.rows, self.blocks = lines, rows, blocks
        self.grads, self.outs = grads, outs
        kinds = len(blocks)
        self.near, self.from_b, self.from_a, self.from_z, self.total, self.last = (
            buffers[kinds * k : kinds * (k + 1)] for k in range(6)
        )
        self.send, self.recv, self.credit = sems
        self.pieces = scatter_pieces(blocks)
        self.only = [(p - 3) // 2 if piece[0] == 3 else None for p, piece in enumerate(self.pieces)]
        self.z, self.x, self.y, self.c = place()
        self.xa, self.ya, self.xb, self.yb = partners()
        self.sibling = device(self.z, self.x, self.y, 1 - self.c)
        self.started = []

    def go(self, make):
        make().start()
        self.started.append((None, make))

    def where(self, p, body):
        if self.only[p] is None:
            body()
        else:
            pl.when(self.z == self.only[p])(body)

    def every(self, p):
        return slice(None) if self.only[p] is None else pl.ds(self.only[p], 1)

    def planes(self, p, body):
        if self.only[p] is None:
            pl.loop(0, self.lines)(body)
        else:
            body(self.only[p])

    def cut(self, p, ref, *lead):
        t, r0, nr, _, l0, w = self.pieces[p]
        return ref[t].at[(*lead, slice(None), pl.ds(r0, nr), pl.ds(l0, w))]

    def grad(self, p, z, x, y, half=None):
        half = self.c if half is None else half
        return part(self.pieces[p], self.grads[self.pieces[p][0]], z, x, y, half)

    def slot(self, p):
        t, _, _, _, l0, w = self.pieces[p]
        return {0: l0 // w, 1: 0, 2: l0 // w % SLOTS, 3: (p - 3) // 2 % SLOTS, 4: 0}[t]

    def near_copy(self, p):
        every = slice(None)
        mine = self.grad(p, self.every(p), every, every, 1 - self.c)
        near = self.near[self.pieces[p][0]].at[self.slot(p)]
        return remote(mine, near, self.send.at[p, 0], self.recv.at[p, 0], self.sibling)

    def b_copy(self, p, k):
        at = (self.xb, self.yb) if k == 0 else (1 - self.x, 1 - self.y)
        return remote(
            self.grad(p, self.every(p), *at),
            self.cut(p, self.from_b, k, self.every(p)),
            self.send.at[p, 1 + k],
            self.recv.at[p, 1 + k],
            device(self.z, self.xb, self.yb, self.c),
        )

    def a_copy(self, p):
        return remote(
            self.grad(p, self.every(p), self.xa, self.ya),
            self.cut(p, self.from_a, self.every(p)),
            self.send.at[p, 3],
            self.recv.at[p, 3],
            device(self.z, self.xa, self.ya, self.c),
        )

    def z_copy(self, p, d):
        other = lax.rem(self.z + d, self.lines)
        return remote(
            self.grad(p, other, self.x, self.y),
            self.cut(p, self.from_z, d - 1),
            self.send.at[p, 3 + d],
            self.recv.at[p, 3 + d],
            device(other, self.x, self.y, self.c),
        )

    def last_copy(self, p):
        t, r0, nr, _, l0, w = self.pieces[p]
        if self.blocks[t][0] == 2:
            src = self.total[t].at[1 - self.c, pl.ds(r0, nr), pl.ds(l0, w)]
            dst = self.last[t].at[pl.ds(r0, nr), pl.ds(l0, w)]
        else:
            away = pl.ds(pl.multiple_of((1 - self.c) * self.rows, 8), self.rows)
            src = self.total[t].at[0, away, pl.ds(l0, w)]
            dst = self.last[t].at[:, pl.ds(l0, w)]
        k = 3 + self.lines
        return remote(src, dst, self.send.at[p, k], self.recv.at[p, k], self.sibling)

    def uses(self, p):
        t = self.pieces[p][0]
        if t not in (2, 3):
            return False, False
        return p - 2 * SLOTS >= 3, p + 2 * SLOTS <= 10

    def first(self, p):
        if self.uses(p)[0]:
            pl.semaphore_wait(self.credit.at[self.pieces[p][0] - 2], 1)
        self.go(lambda: self.near_copy(p))

    def second(self, p):
        f32 = jnp.float32
        self.near_copy(p).wait_recv()
        near = self.near[self.pieces[p][0]].at[self.slot(p)]

        def add(k):
            for x in range(2):
                for y in range(2):
                    kept = self.grad(p, k, x, y)
                    got = near[0 if self.only[p] is not None else k, x, y]
                    kept[...] = (kept[...].astype(f32) + got.astype(f32)).astype(jnp.bfloat16)

        self.planes(p, add)
        if self.uses(p)[1]:
            credit = self.credit.at[self.pieces[p][0] - 2]
            pl.semaphore_signal(credit, inc=1, device_id=self.sibling, device_id_type=MESH)
        self.go(lambda: self.b_copy(p, 1))
        self.go(lambda: self.b_copy(p, 0))

    def third(self, p):
        self.b_copy(p, 1).wait_recv()

        def add(k):
            kept, got = self.grad(p, k, self.xa, self.ya), self.cut(p, self.from_b, 1, k)
            kept[...] = (kept[...].astype(jnp.float32) + got[...].astype(jnp.float32)).astype(jnp.bfloat16)

        self.planes(p, add)
        self.go(lambda: self.a_copy(p))

    def mine(self, p, k):
        got = self.cut(p, self.from_b, 0, k)[...].astype(jnp.float32) + self.cut(p, self.from_a, k)[...].astype(jnp.float32)
        return self.grad(p, k, self.x, self.y)[...].astype(jnp.float32) + got

    def fourth(self, p):
        self.b_copy(p, 0).wait_recv()
        self.a_copy(p).wait_recv()
        q = self.only[p]

        def send():
            for d in range(1, self.lines):
                self.go(functools.partial(self.z_copy, p, d))

        def round_off(k):
            self.grad(p, k, self.x, self.y)[...] = self.mine(p, k).astype(jnp.bfloat16)

        if q is None:

            @pl.loop(1, self.lines)
            def _(d):
                round_off(lax.rem(self.z + d, self.lines))

            send()
        else:

            def to_owner():
                return self.z_copy(p, lax.rem(q - self.z + self.lines, self.lines))

            @pl.when(self.z != q)
            def _():
                round_off(q)
                to_owner().start()

            self.started.append((lambda: self.z != q, to_owner))

        def keep():
            self.cut(p, self.total)[...] = self.mine(p, self.z if q is None else q)

        self.where(p, keep)

    def fifth(self, p):
        def body():
            for d in range(1, self.lines):
                self.z_copy(p, d).wait_recv()
            total = self.cut(p, self.total)
            acc = total[...]
            for d in range(1, self.lines):
                acc = acc + self.cut(p, self.from_z, d - 1)[...].astype(jnp.float32)
            total[...] = acc
            self.last_copy(p).start()

        self.where(p, body)
        q = self.only[p]
        self.started.append((None if q is None else lambda: self.z == q, lambda: self.last_copy(p)))

    def sixth(self, p):
        t, r0, nr, c0, l0, w = self.pieces[p]

        def body():
            self.last_copy(p).wait_recv()
            if self.blocks[t][0] == 2:
                kept = self.total[t][self.c, r0 : r0 + nr, l0 : l0 + w]
                got = self.last[t][r0 : r0 + nr, l0 : l0 + w]
                to = slice(r0, r0 + nr)
            else:
                kept = self.total[t][0, pl.ds(pl.multiple_of(self.c * self.rows, 8), self.rows), l0 : l0 + w]
                got = self.last[t][:, l0 : l0 + w]
                to = slice(None)
            h = HALF[t] + c0
            self.outs[t][to, c0 : c0 + w] = jnp.where(self.c == 0, kept, got)
            self.outs[t][to, h : h + w] = jnp.where(self.c == 0, got, kept)

        self.where(p, body)

    def steps(self):
        return [self.first, self.second, self.third, self.fourth, self.fifth, self.sixth]

    def timed(self, p, start):
        return [(start + lag, p, functools.partial(step, p)) for step, lag in zip(self.steps(), SCATTER_LAGS)]

    def finish(self):
        for condition, make in self.started:
            if condition is None:
                make().wait_send()
            else:

                @pl.when(condition())
                def _(make=make):
                    make().wait_send()


def crossed(a, b):
    return lax.dot_general(a, b, (((0,), (0,)), ((), ())), preferred_element_type=jnp.float32)


def layer_kernel(lines, rows, blocks, linked, total_rows, *refs):
    f32, bf16 = jnp.float32, jnp.bfloat16
    tags, subset_w, tokens_h, cotan_h, cosine_h, sine_h = refs[:6]
    given, refs = (refs[6:13], refs[13:]) if linked else (refs[6:10], refs[10:])
    mixed_h, grad_tokens_h, *results = refs[:7]
    tokens, cotan, cosine, sine, d_second, small, first_t, second_in, queries, pool, keys, keys_t = refs[7:19]
    values, values_t, attended, logsums, scaled, packed_d, mask, sums, d_keys, d_values, branch, second_t = refs[19:31]
    whole, grad_packed, grad_small, load_sems, out_sems = refs[31:35], refs[35], refs[36], refs[37], refs[38]
    refs = refs[39:]
    grads = [grad_packed, *whole[1:], grad_small]
    tiles, wide, qkv = SEQ // TILE, D // 2, D + 2 * HD

    def tile(k):
        return pl.ds(pl.multiple_of(k * TILE, TILE), TILE)

    pairs = [(tokens_h, tokens), (cosine_h, cosine), (sine_h, sine), (cotan_h, cotan)]
    if not linked:
        pairs += list(zip(given, whole))
    loads = [pltpu.make_async_copy(a, b, load_sems.at[k]) for k, (a, b) in enumerate(pairs)]
    for copy in loads:
        copy.start()
    if linked:
        query, pair, out, up, down, gains, biases = given
        packed, stages, square, gather_sems, refs = refs[0], refs[1:5], refs[5], refs[6:10], refs[10:]
        for p in range(H // 2):
            packed[:, place_of(p) : place_of(p) + 2 * HD] = query[:, 2 * HD * p : 2 * HD * (p + 1)]
        packed[:, PAIR : PAIR + 2 * HD] = pair[...]
        square[...] = jnp.zeros_like(square)
        square[0:2, 0:rows] = gains[...]
        square[2:4, 0:rows] = biases[...]
        spot = lax.broadcasted_iota(jnp.int32, (rows, 128), 1) == tags[0] + 4
        spot = jnp.where(lax.broadcasted_iota(jnp.int32, (rows, 128), 0) == 0, spot.astype(f32), 0.0)
        packed[:, qkv:] = square[...].T[:rows] + spot
        greet(lines)
        gather = Gather(lines, rows, blocks, [packed, out, up, down], stages, whole, gather_sems)
        scatter = Scatter(lines, rows, blocks, grads, results, refs[:30], refs[30:33])
        gather.begin(2)
        urgent, timed = gather.events()
    else:
        urgent, timed = [], []
    packed_w, out_w, up_w, down_w = whole

    steps = (PROJECT_STEPS, FORWARD_STEPS, OUTWARD_STEPS, BACKWARD_STEPS, CLOSE_STEPS, CHUNK_STEPS * 4, TOKEN_STEPS)
    starts, slots = [0], [0]
    for part_steps in steps:
        starts.append(starts[-1] + sum(part_steps))
        slots.append(slots[-1] + len(part_steps))
    if linked:
        edge = 0.01
        timed += scatter.timed(0, starts[3] - edge)
        ready = starts[3] + 4 * sum(BACKWARD_STEPS[:2])
        timed += [(ready - 2 * edge, 100, lambda: query_grads(0, PACK // 4))] + scatter.timed(1, ready - edge)
        timed += scatter.timed(2, starts[5] - edge)
        for q in range(4):
            start = starts[5] + q * sum(CHUNK_STEPS) + sum(CHUNK_STEPS[:6]) - edge
            timed += scatter.timed(3 + 2 * q, start) + scatter.timed(4 + 2 * q, start + sum(CHUNK_STEPS[6:]))
        timed += scatter.timed(11, starts[6] + sum(TOKEN_STEPS[:4]) + edge)
    plan = deal(timed, ends(0.0, *(step for part_steps in steps for step in part_steps)))

    def slot(section, index, values):
        run_at(index, [(v, plan[slots[section] + v]) for v in values])

    row = lax.broadcasted_iota(jnp.int32, (TILE, TILE), 0)
    column = lax.broadcasted_iota(jnp.int32, (TILE, TILE), 1)
    mask[...] = jnp.where(row <= column, 0.0, -1e30)
    sums[...] = jnp.zeros_like(sums)
    d_keys[...] = jnp.zeros_like(d_keys)
    d_values[...] = jnp.zeros_like(d_values)
    lane = lax.broadcasted_iota(jnp.int32, (TILE, 2 * HD), 1)
    left = lane < HD
    loads[0].wait()

    def normed(k):
        inputs = tokens[tile(k), :].astype(f32)
        centred = inputs - jnp.mean(inputs, axis=-1, keepdims=True)
        inv_std = lax.rsqrt(jnp.mean(centred * centred, axis=-1, keepdims=True) + eps_norm)
        return centred * inv_std, inv_std

    @pl.loop(0, tiles)
    def _(k):
        d_second[tile(k), :] = normed(k)[0]

    for copy in loads[1:]:
        copy.wait()
    for event in urgent:
        event()
    small[...] = columns(packed_w, qkv, 128).astype(f32).T

    @pl.loop(0, tiles)
    def _(k):
        norm = d_second[tile(k), :]
        a1 = (norm * small[0:1, :] + small[2:3, :]).astype(bf16)
        a2 = norm * small[1:2, :] + small[3:4, :]
        first_t[:, tile(k)] = a1.T
        second_in[tile(k), :] = a2.astype(bf16)
        second_t[:, tile(k)] = a2.astype(bf16).T
        mixed = jnp.dot(a1, columns(packed_w, 0, qkv), preferred_element_type=f32)
        cos_t, sin_t = cosine[tile(k), :], sine[tile(k), :]
        for p in range(H // 2):
            turn = swapped(mixed[:, place_of(p) : place_of(p) + 2 * HD], cos_t, sin_t).astype(bf16).astype(f32)
            turn = turn * (LOG2E / 8)
            high = turn.astype(bf16).astype(f32)
            low = turn - high
            queries[2 * p, tile(k), :] = jnp.where(left, high, pltpu.roll(low, HD, 1)).astype(bf16)
            queries[2 * p + 1, tile(k), :] = jnp.where(left, pltpu.roll(high, HD, 1), low).astype(bf16)
        pair_t = mixed[:, PAIR : PAIR + 2 * HD]
        pair_t = jnp.where(left, swapped(pair_t, cos_t, sin_t), pair_t).astype(bf16).astype(f32)
        other = pltpu.roll(pair_t, HD, 1)
        both = jnp.where(left, pair_t, other)
        keys[tile(k), :] = both.astype(bf16)
        keys_t[:, tile(k)] = both.T[:HD].astype(bf16)
        values[tile(k), :] = jnp.where(left, other, jnp.where(lane < HD + 2, -1.0, 0.0)).astype(bf16)
        values_t[:, tile(k)] = jnp.where(left, other, jnp.where(lane == HD, 1.0, 0.0)).T.astype(bf16)
        slot(0, k, range(tiles))

    @pl.loop(0, H // 2)
    def _(pr):
        work = [(i, hh) for i in range(tiles) for hh in range(2)]
        ready, shares, heads = {}, {}, {}

        def score(n):
            i, hh = work[n]
            count = TILE * (i + 1)
            ready[n] = turned(keys[0:count, :], queries[pr * 2 + hh, i * TILE : count, :])

        def weigh(n):
            i, hh = work[n]
            count = TILE * (i + 1)
            scores = ready.pop(n)
            last = scores[count - TILE :] + mask[...]
            peak = tallest(last)
            if i:
                peak = jnp.maximum(peak, tallest(scores[: count - TILE]))
            probs = jnp.exp2(last - peak).astype(bf16)
            if i:
                probs = jnp.concatenate([jnp.exp2(scores[: count - TILE] - peak).astype(bf16), probs], axis=0)
            shares[n] = peak, probs

        def collect(n):
            i, hh = work[n]
            count = TILE * (i + 1)
            peak, probs = shares.pop(n)
            got = jnp.dot(values_t[0:80, 0:count], probs, preferred_element_type=f32)
            total = got[HD : HD + 1]
            heads[hh] = got[:HD] * (1.0 / total)
            logsums[pr * 2 + hh, :, i * TILE : count] = peak + jnp.log2(total)
            if hh:
                both = jnp.concatenate([heads[0], heads[1]], axis=0).T
                attended[i * TILE : count, lanes(pr * 2 * HD, 2 * HD)] = both.astype(bf16)

        ahead = 2
        for n in range(len(work) + ahead + 2):
            if n < len(work):
                score(n)
            if 0 <= n - ahead < len(work):
                weigh(n - ahead)
            if 0 <= n - ahead - 2 < len(work):
                collect(n - ahead - 2)
        for i in (0, 1):
            slot(1, pr * 2 + i, range(i, 2 * (H // 2), 2))

    kind = lax.broadcasted_iota(jnp.int32, (128, D), 0)
    count = jnp.sum(jnp.where(kind == tags[0] + 4, small[...], 0.0), keepdims=True)
    subset = lax.broadcasted_iota(jnp.int32, subset_w.shape, 1)
    weight = jnp.sum(jnp.where(subset == tags[0], subset_w[...], 0.0), keepdims=True)
    scale = weight / count * (total_rows / SUBSETS)

    @pl.loop(0, tiles)
    def _(k):
        grad_out = (cotan[tile(k), :].astype(f32) * scale).astype(bf16)
        scaled[tile(k), :] = grad_out
        heads = attended[tile(k), :]
        out_m = out_w[...].reshape(D, D)
        branch[tile(k), :] = tokens[tile(k), :].astype(f32) + jnp.dot(heads, out_m, preferred_element_type=f32)
        d_heads_t = turned(grad_out, out_m).astype(bf16).astype(f32)
        for p in range(H // 2):
            block = d_heads_t[:, 2 * HD * p : 2 * HD * (p + 1)]
            product = block * heads[:, 2 * HD * p : 2 * HD * (p + 1)].astype(f32)
            for hh, (mine, there) in enumerate(((left, block), (~left, pltpu.roll(block, HD, 1)))):
                delta = jnp.sum(jnp.where(mine, product, 0.0), axis=1, keepdims=True)
                high = delta.astype(bf16).astype(f32)
                extra = jnp.where(lane == HD, high, jnp.where(lane == HD + 1, delta - high, 0.0))
                pool[2 * p + hh, tile(k), :] = jnp.where(left, there, extra).astype(bf16)
        slot(2, k, range(tiles))

    if linked:
        gather.sent(1)

    @pl.loop(0, 2)
    def _(k):
        got = crossed(attended[:, lanes(k * wide, wide)], scaled[...]).astype(bf16)
        grads[1][pl.ds(2 * k, 2)] = got.reshape(2, 2, 2, 1, D // 16, D)
        slot(2, tiles + k, range(tiles, tiles + 2))

    def query_grads(start, stop):
        for span in (slice(start, stop), slice(PACK // 2 + start, min(PACK // 2 + stop, qkv))):
            for k in range(2):
                got = jnp.dot(first_t[k * wide : (k + 1) * wide, :], packed_d[:, span], preferred_element_type=f32).astype(bf16)
                grad_packed[2 * k : 2 * k + 2, :, :, :, :, span] = got.reshape(2, 2, 2, 1, D // 16, -1)

    @pl.loop(0, H // 2)
    def _(pr):
        work = [(i, hh) for i in range(tiles) for hh in range(2)]
        ready, shares, d_query = {}, {}, {}

        def score(n):
            i, hh = work[n]
            count, span = TILE * (i + 1), slice(i * TILE, TILE * (i + 1))
            head = pr * 2 + hh
            ready[n] = turned(keys[0:count, :], queries[head, span, :]), turned(values[0:count, :], pool[head, span, :])

        def weigh(n):
            i, hh = work[n]
            count, span = TILE * (i + 1), slice(i * TILE, TILE * (i + 1))
            scores, d_probs = ready.pop(n)
            shift = logsums[pr * 2 + hh, :, span]
            probs = jnp.exp2(scores[count - TILE :] + mask[...] - shift)
            if i:
                probs = jnp.concatenate([jnp.exp2(scores[: count - TILE] - shift), probs], axis=0)
            shares[n] = probs.astype(bf16), (probs * d_probs).astype(bf16)

        def collect(n):
            i, hh = work[n]
            count, span = TILE * (i + 1), slice(i * TILE, TILE * (i + 1))
            d_query[hh] = jnp.dot(keys_t[:, 0:count], shares[n][1], preferred_element_type=f32)
            if hh:
                both = [shares.pop(n - 1), shares.pop(n)]
                for acc, k, other in ((d_values, 0, pool), (d_keys, 1, queries)):
                    two = jnp.concatenate([other[pr * 2, span, :], other[pr * 2 + 1, span, :]], axis=0)
                    parts = jnp.concatenate([both[0][k], both[1][k]], axis=1)
                    acc[0:count, :] += jnp.dot(parts, two, preferred_element_type=f32)
                d_q = jnp.concatenate([d_query[0], d_query[1]], axis=0).T * 0.125
                d_q = swapped(d_q, cosine[span, :], -sine[span, :])
                packed_d[span, lanes(place_of(pr), 2 * HD)] = d_q.astype(bf16)

        for n in range(len(work) + 2 + 1):
            if n < len(work):
                score(n)
            if 0 <= n - 2 < len(work):
                weigh(n - 2)
            if 0 <= n - 2 - 1 < len(work):
                collect(n - 2 - 1)
        for i in (0, 1):
            slot(3, pr * 2 + i, range(i, 2 * (H // 2), 2))

    @pl.loop(0, tiles)
    def _(k):
        d_key = d_keys[tile(k), :]
        d_key = (d_key + pltpu.roll(d_key, HD, 1)) * (1.0 / LOG2E)
        d_key = swapped(d_key, cosine[tile(k), :], -sine[tile(k), :])
        d_pair = jnp.where(left, d_key, pltpu.roll(d_values[tile(k), :], HD, 1)).astype(bf16)
        packed_d[tile(k), PAIR : PAIR + 2 * HD] = d_pair
        slot(4, k, range(tiles))

    if not linked:
        query_grads(0, PACK // 4)
    query_grads(PACK // 4, PACK // 2)
    grad_packed[:, :, :, :, :, qkv:] = jnp.zeros((4, 2, 2, 1, D // 16, PACK - qkv), bf16)
    for event in plan[slots[4] + tiles]:
        event()
    if linked:
        gather.sent(2, 3)

    @pl.loop(0, 4)
    def _(q):
        def up_m():
            return columns(up_w, pl.multiple_of(q * D, D), D)

        def down_m():
            return down_w[q].reshape(D, D)

        @pl.loop(0, tiles)
        def _(k):
            pre = jnp.dot(second_in[tile(k), :], up_m(), preferred_element_type=f32)
            d_hidden = turned(scaled[tile(k), :], down_m())
            cdf = 0.5 + 0.5 * lax.erf(pre * 0.7071067811865476)
            density = jnp.exp2(pre * pre * (-0.5 * LOG2E)) * 0.3989422804014327
            active = (pre * cdf).astype(bf16)
            d_up = (d_hidden * (cdf + pre * density)).astype(bf16)
            active_t = active.T
            for b in range(2):
                queries[2 * k + b, 0:D, :] = active_t[:, 128 * b : 128 * (b + 1)]
            for b in range(6):
                pool[b, tile(k), :] = d_up[:, 128 * b : 128 * (b + 1)]
            branch[tile(k), :] += jnp.dot(active, down_m(), preferred_element_type=f32)
            got = turned(d_up, up_m())
            d_second[tile(k), :] = jnp.where(q == 0, got, got + d_second[tile(k), :])
            slot(5, q * 8 + k, [v for v in range(32) if v % 8 < 4])

        hidden_t = jnp.concatenate([queries[b, 0:D, :] for b in range(8)], axis=1)
        got = jnp.dot(hidden_t, scaled[...], preferred_element_type=f32).astype(bf16)
        down_w[q] = got.reshape(2, 2, 2, 4 * D // 32, D)
        for v in (4, 5):
            slot(5, q * 8 + v, [8 * p + v for p in range(4)])
        if linked:
            run_at(q, [(v, [functools.partial(gather.sent, 4 + v)]) for v in range(4)])
        d_ups = jnp.concatenate([pool[b] for b in range(6)], axis=1)
        got = jnp.dot(second_t[...], d_ups, preferred_element_type=f32).astype(bf16)
        up_w[:, :, :, :, :, lanes(q * D, D)] = got.reshape(4, 2, 2, 1, D // 16, D)
        for v in (6, 7):
            slot(5, q * 8 + v, [8 * p + v for p in range(4)])

    @pl.loop(0, tiles)
    def _(k):
        attended[tile(k), :] = branch[tile(k), :].astype(bf16)
        d_first = turned(packed_d[tile(k), 0:qkv], columns(packed_w, 0, qkv))
        branch[tile(k), :] = d_first
        second, norm = d_second[tile(k), :], normed(k)[0]
        for n, value in enumerate((d_first * norm, second * norm, d_first, second)):
            sums[n : n + 1, :] += jnp.sum(value, axis=0, keepdims=True)
        slot(6, k, range(tiles))

    flushed = [pltpu.make_async_copy(attended, mixed_h, out_sems.at[0])]
    flushed[0].start()
    grad_small[:, :, :, :, :, 0:128] = sums[...].T.astype(bf16).reshape(4, 2, 2, 1, D // 16, 128)
    grad_small[:, :, :, :, :, 128:] = jnp.zeros((4, 2, 2, 1, D // 16, SMALL - 128), bf16)

    @pl.loop(0, tiles)
    def _(k):
        norm, inv_std = normed(k)
        d_normed = branch[tile(k), :] * small[0:1, :] + d_second[tile(k), :] * small[1:2, :]
        inner = jnp.mean(d_normed * norm, axis=-1, keepdims=True)
        d_inputs = inv_std * (d_normed - jnp.mean(d_normed, axis=-1, keepdims=True) - norm * inner)
        second_in[tile(k), :] = (cotan[tile(k), :].astype(f32) * scale + d_inputs).astype(bf16)
        slot(6, tiles + k, range(tiles, 2 * tiles))

    flushed.append(pltpu.make_async_copy(second_in, grad_tokens_h, out_sems.at[1]))
    flushed[-1].start()
    for event in plan[-1]:
        event()
    if linked:
        gather.sent(0)
        scatter.finish()
    else:
        for t in range(5):
            flushed.append(pltpu.make_async_copy(grads[t], results[t], out_sems.at[2 + t]))
            flushed[-1].start()
    for copy in flushed:
        copy.wait()


def layer(linked, lines, rows, rows_down, total_rows, tags, subset_w, tokens, cotan, cosine, sine, weights):
    blocks = layout(rows, rows_down)
    f32, bf16 = jnp.float32, jnp.bfloat16
    shapes = [(lines, 2, 2, g, r, k) for g, r, k in blocks]
    own_rows = [r if g == 2 else rows for g, r, k in blocks]
    vmem = pl.BlockSpec(memory_space=pltpu.VMEM)
    anywhere = pl.BlockSpec(memory_space=pl.ANY)
    if linked:
        results = [jax.ShapeDtypeStruct((o, k), f32) for o, (g, r, k) in zip(own_rows, blocks)]
    else:
        weights = [a.reshape(shape) for a, shape in zip(weights, shapes)]
        results = [jax.ShapeDtypeStruct(shape, bf16) for shape in shapes]
    tall = (SEQ, D)
    buffers = [
        (tall, bf16),
        (tall, bf16),
        ((SEQ, 2 * HD), f32),
        ((SEQ, 2 * HD), f32),
        (tall, f32),
        ((128, D), f32),
        ((D, SEQ), bf16),
        (tall, bf16),
        ((H, SEQ, 2 * HD), bf16),
        ((H, SEQ, 2 * HD), bf16),
        ((SEQ, 2 * HD), bf16),
        ((HD, SEQ), bf16),
        ((SEQ, 2 * HD), bf16),
        ((2 * HD, SEQ), bf16),
        (tall, bf16),
        ((H, 1, SEQ), f32),
        (tall, bf16),
        ((SEQ, D + 2 * HD), bf16),
        ((TILE, TILE), f32),
        ((128, D), f32),
        ((SEQ, 2 * HD), f32),
        ((SEQ, 2 * HD), f32),
        (tall, f32),
        ((D, SEQ), bf16),
    ]
    buffers += [(shape, bf16) for shape in shapes[:4]] + [(shapes[0], bf16), (shapes[4], bf16)]
    scratch = [pltpu.VMEM(shape, kind) for shape, kind in buffers]
    scratch += [pltpu.SemaphoreType.DMA((8,)), pltpu.SemaphoreType.DMA((7,))]
    if linked:
        scratch += [pltpu.VMEM((rows, PACK), f32)]
        scratch += [pltpu.VMEM((g, r, k // 2), f32) for g, r, k in blocks[:4]]
        scratch += [pltpu.VMEM((128, 128), f32)]
        count, kinds = len(gather_pieces(blocks)), 4 * lines + 3
        scratch += [pltpu.SemaphoreType.DMA((count,))] * 2 + [pltpu.SemaphoreType.DMA((count, kinds))] * 2
        near = [(2, lines, PACK // 4), (1, lines, D // 2), (SLOTS, lines, D // 2), (SLOTS, 1, D // 2), (1, lines, SMALL // 2)]
        scratch += [pltpu.VMEM((n, z, 2, 2, g, r, w), bf16) for (n, z, w), (g, r, k) in zip(near, blocks)]
        for lead in ((2, lines), (lines,), (lines - 1,)):
            scratch += [pltpu.VMEM((*lead, g, r, k // 2), bf16) for g, r, k in blocks]
        scratch += [pltpu.VMEM((g, r, k // 2), f32) for g, r, k in blocks]
        scratch += [pltpu.VMEM((o, k // 2), f32) for o, (g, r, k) in zip(own_rows, blocks)]
        count = len(scatter_pieces(blocks))
        scratch += [pltpu.SemaphoreType.DMA((count, lines + 4))] * 2 + [pltpu.SemaphoreType.REGULAR((2,))]
    return pl.pallas_call(
        functools.partial(layer_kernel, lines, rows, blocks, linked, total_rows),
        out_shape=[jax.ShapeDtypeStruct(tall, bf16)] * 2 + results,
        in_specs=[pl.BlockSpec(memory_space=pltpu.SMEM), vmem] + [anywhere] * 4 + [vmem if linked else anywhere] * len(weights),
        out_specs=[anywhere] * 2 + [vmem if linked else anywhere] * 5,
        scratch_shapes=scratch,
        compiler_params=pltpu.CompilerParams(
            collective_id=0 if linked else None, has_side_effects=linked, vmem_limit_bytes=63 * 2**20
        ),
        name="layer",
    )(tags, subset_w, tokens, cotan, cosine, sine, *weights)


def finish_kernel(rows, *refs):
    packed, small, *rest = refs[:7]
    query, pair, gains, biases, *to = refs[7:]
    for p in range(H // 2):
        query[:, 2 * HD * p : 2 * HD * (p + 1)] = packed[:, place_of(p) : place_of(p) + 2 * HD]
    pair[...] = packed[:, PAIR : PAIR + 2 * HD]
    turned_back = small[:, 0:128].T
    gains[...] = turned_back[0:2]
    biases[...] = turned_back[2:4]
    for a, b in zip(rest, to):
        b[...] = a[...]


def finish(rows, packed, small, *rest):
    f32 = jnp.float32
    vmem = pl.BlockSpec(memory_space=pltpu.VMEM)
    shapes = [(rows, D), (rows, 2 * HD), (2, rows), (2, rows)]
    return pl.pallas_call(
        functools.partial(finish_kernel, rows),
        out_shape=[jax.ShapeDtypeStruct(a, f32) for a in shapes] + [jax.ShapeDtypeStruct(a.shape, a.dtype) for a in rest],
        in_specs=[vmem] * (2 + len(rest)),
        out_specs=[vmem] * (4 + len(rest)),
        compiler_params=pltpu.CompilerParams(vmem_limit_bytes=63 * 2**20),
        name="finish",
    )(packed, small, *rest)


def is_linked(rows):
    return lax.axis_size("dp") == 8 and lax.axis_size("fsdp") == 4 and rows % 8 == 0


def fetch_weights(query_w, pair_w, out_w, up_w, down_w, gains, biases, tags):
    onehot = (tags[0] == jnp.arange(SUBSETS, dtype=jnp.int32)).astype(jnp.float32)
    own_counts = jnp.where((jnp.arange(query_w.shape[0]) == 0)[:, None], onehot[None, :], 0.0)
    small = jnp.concatenate([gains.T, biases.T, own_counts], axis=1)
    small = jnp.pad(small, ((0, 0), (0, 128 - small.shape[1])))
    pairs = [query_w[:, 2 * HD * p : 2 * HD * (p + 1)] for p in range(H // 2)]
    packed = jnp.concatenate([*pairs[0::2], pair_w, *pairs[1::2], small], axis=1)
    return [
        lax.all_gather(a.astype(jnp.bfloat16), ("dp", "fsdp"), axis=0, tiled=True)
        for a in (packed, out_w, up_w, down_w)
    ]


def body(
    tokens,
    w_query,
    w_pair,
    w_attn_out,
    w_up,
    w_down,
    ln_gains,
    ln_biases,
    cotangent,
    subset_tags,
    subset_weights,
):
    cosine, sine = tables()
    linked = is_linked(w_query.shape[0])
    shards = (w_query, w_pair, w_attn_out, w_up, w_down, ln_gains, ln_biases)
    total_rows = lax.axis_size("dp") * lax.axis_size("fsdp")
    if linked:
        lines, rows, rows_down = lax.axis_size("dp") // 2, w_query.shape[0], w_down.shape[0]
    else:
        lines, rows, rows_down = 4, D // 32, 4 * D // 32
        shards = fetch_weights(*shards, subset_tags)
    subset_w = subset_weights.reshape(1, SUBSETS)
    mixed, grad_tokens, *grads = layer(
        linked, lines, rows, rows_down, total_rows, subset_tags, subset_w, tokens, cotangent, cosine, sine, shards
    )
    if not linked:
        grads = [
            lax.psum_scatter(
                g.astype(jnp.float32).reshape(-1, g.shape[-1]), ("dp", "fsdp"), scatter_dimension=0, tiled=True
            )
            for g in grads
        ]
    packed_g, out_g, up_g, down_g, small_g = grads
    query_g, pair_g, gains_g, biases_g, out_g, up_g, down_g, grad_tokens, mixed = finish(
        w_query.shape[0], packed_g, small_g, out_g, up_g, down_g, grad_tokens, mixed
    )
    return mixed, grad_tokens, query_g, pair_g, out_g, up_g, down_g, gains_g, biases_g


def solution(mesh):
    in_specs = (
        P(("dp", "fsdp"), None),
        P(("dp", "fsdp"), None),
        P(("dp", "fsdp"), None),
        P(("dp", "fsdp"), None),
        P(("dp", "fsdp"), None),
        P(("dp", "fsdp"), None),
        P(None, ("dp", "fsdp")),
        P(None, ("dp", "fsdp")),
        P(("dp", "fsdp"), None),
        P(("dp", "fsdp")),
        P(),
    )
    out_specs = (
        P(("dp", "fsdp"), None),
        P(("dp", "fsdp"), None),
        P(("dp", "fsdp"), None),
        P(("dp", "fsdp"), None),
        P(("dp", "fsdp"), None),
        P(("dp", "fsdp"), None),
        P(("dp", "fsdp"), None),
        P(None, ("dp", "fsdp")),
        P(None, ("dp", "fsdp")),
    )
    return jax.shard_map(body, mesh=mesh, in_specs=in_specs, out_specs=out_specs, check_vma=False)
```

```python
import functools

import jax
import jax.numpy as jnp
import numpy as np
from jax import lax
from jax.experimental import pallas as pl
from jax.experimental.pallas import tpu as pltpu
from jax.sharding import PartitionSpec as P

D = 768
H = 12
HD = 64
ROT = 16
SUBSETS = 22
SEQ = 1024
PACK = 1024
TILE = 256
LOG2E = 1.4426950408889634
PAIR = 3 * 128
SMALL = 256
GATHER_STARTS = (0.0, -6.0, 0.0, 8.0, 17.0, 22.0, 27.0, 32.0)
GATHER_LAGS = (0.0, 10.0, 20.0, 22.0)
SCATTER_LAGS = (0.0, 2.5, 10.0, 17.0, 24.0, 27.0)
PROJECT_STEPS = (1.5,) * 4
FORWARD_STEPS = (3.3, 0.1, 0.1, 0.1) * 3
OUTWARD_STEPS = (1.5,) * 4 + (0.85,) * 2
BACKWARD_STEPS = (3.2, 0.1) * 6
CLOSE_STEPS = (0.2,) * 4 + (1.0,)
CHUNK_STEPS = (1.4, 1.4, 1.4, 1.4, 1.2, 0.1, 1.2, 0.1)
TOKEN_STEPS = (0.7,) * 4 + (0.5,) * 4
MESH = pl.DeviceIdType.MESH


eps_norm = 1e-05


def place_of(p):
    return (p % 2) * (PACK // 2) + (p // 2) * 2 * HD


def place():
    dp, fs = lax.axis_index("dp"), lax.axis_index("fsdp")
    return dp // 2, dp % 2, fs // 2, fs % 2


def device(z, x, y, c):
    return (z * 2 + x, y * 2 + c)


def partners():
    z, x, y, c = place()
    xa, ya = jnp.where(c == 0, 1 - x, x), jnp.where(c == 0, y, 1 - y)
    xb, yb = jnp.where(c == 0, x, 1 - x), jnp.where(c == 0, 1 - y, y)
    return xa, ya, xb, yb


def greet(lines):
    z, x, y, c = place()
    barrier = pltpu.get_barrier_semaphore()
    others = [device(lax.rem(z + d, lines), x, y, c) for d in range(1, lines)]
    others += [device(z, 1 - x, y, c), device(z, x, 1 - y, c), device(z, x, y, 1 - c)]
    for other in others:
        pl.semaphore_signal(barrier, inc=1, device_id=other, device_id_type=MESH)
    pl.semaphore_wait(barrier, len(others))


def remote(src, dst, send, recv, where):
    return pltpu.make_async_remote_copy(
        src_ref=src, dst_ref=dst, send_sem=send, recv_sem=recv, device_id=where, device_id_type=MESH
    )


def layout(rows, rows_down):
    return [(1, 2 * rows, PACK), (1, 2 * rows, D), (1, 2 * rows, 4 * D), (2, rows_down, D), (1, 2 * rows, SMALL)]


HALF = (PACK // 2, D // 2, D // 2, D // 2, SMALL // 2)


def lanes(start, size):
    return pl.ds(pl.multiple_of(start, 128), size)


def part(piece, ref, z, x, y, half):
    t, r0, nr, c0, _, w = piece
    return ref.at[z, x, y, :, pl.ds(r0, nr), lanes(half * HALF[t] + c0, w)]


def gather_pieces(blocks):
    r0, r1, r2, r3 = (r for _, r, _ in blocks[:4])
    w, half = D // 2, r3 // 2 // 16 * 16
    ups = [(2, 0, r2, 2 * w * k, w * k, w) for k in range(4)]
    downs = [(3, 0, half, 0, 0, w), (3, half, r3 - half, 0, 0, w)]
    return [(0, 0, r0, 0, 0, PACK // 2), (1, 0, r1, 0, 0, w), *downs, *ups]


class Gather:
    def __init__(self, lines, rows, blocks, sources, stages, whole, sems):
        self.lines, self.rows, self.blocks = lines, rows, blocks
        self.sources, self.stages, self.whole = sources, stages, whole
        self.swap_send, self.swap_recv, self.send, self.recv = sems
        self.pieces = gather_pieces(blocks)
        self.z, self.x, self.y, self.c = place()
        self.xa, self.ya, self.xb, self.yb = partners()
        self.sibling = device(self.z, self.x, self.y, 1 - self.c)
        self.started = []

    def go(self, p, make):
        make().start()
        self.started.append((p, make))

    def stage_rows(self, p, core):
        t, r0, nr, _, l0, w = self.pieces[p]
        if self.blocks[t][0] == 2:
            return self.stages[t].at[core, pl.ds(r0, nr), pl.ds(l0, w)]
        return self.stages[t].at[0, pl.ds(pl.multiple_of(core * self.rows, 8), self.rows), pl.ds(l0, w)]

    def source(self, p):
        t, r0, nr, c0, _, w = self.pieces[p]
        return self.sources[t].at[pl.ds(r0, nr) if self.blocks[t][0] == 2 else slice(None)], c0, w

    def swap(self, p):
        source, c0, w = self.source(p)
        mine = source.at[:, lanes((1 - self.c) * HALF[self.pieces[p][0]] + c0, w)]
        return remote(mine, self.stage_rows(p, self.c), self.swap_send.at[p], self.swap_recv.at[p], self.sibling)

    def block(self, p, d, x, y):
        z = lax.rem(self.z + self.lines - d, self.lines)
        return part(self.pieces[p], self.whole[self.pieces[p][0]], z, x, y, self.c)

    def direct(self, p, d, back=0):
        block = self.block(p, back, self.x, self.y)
        where = device(lax.rem(self.z + d, self.lines), self.x, self.y, self.c)
        return remote(block, block, self.send.at[p, d - 1], self.recv.at[p, d - 1], where)

    def to_a(self, p, d, x, y):
        block, k = self.block(p, d, x, y), self.lines - 1 + d
        return remote(block, block, self.send.at[p, k], self.recv.at[p, k], device(self.z, self.xa, self.ya, self.c))

    def to_b(self, p, d, x, y, second=0):
        block, k = self.block(p, d, x, y), self.lines * (2 + second) - 1 + d
        return remote(block, block, self.send.at[p, k], self.recv.at[p, k], device(self.z, self.xb, self.yb, self.c))

    def share(self, p, k, x, y, half):
        column = part(self.pieces[p], self.whole[self.pieces[p][0]], slice(None), x, y, half)
        k = 4 * self.lines - 1 + k
        return remote(column, column, self.send.at[p, k], self.recv.at[p, k], self.sibling)

    def own(self, p):
        x, y = self.x, self.y
        self.go(p, lambda: self.to_a(p, 0, x, y))
        self.go(p, lambda: self.to_b(p, 0, x, y))

    def begin(self, ahead):
        for p in range(len(self.pieces)):
            self.go(p, functools.partial(self.swap, p))
        self.ahead = ahead
        self.place_own(range(ahead))

    def place_own(self, some):
        for p in some:
            t, r0, nr, c0, l0, w = self.pieces[p]
            source, _, _ = self.source(p)
            kept = jnp.where(self.c == 0, source[:, c0 : c0 + w], source[:, HALF[t] + c0 : HALF[t] + c0 + w])
            self.stage_rows(p, self.c)[...] = kept
            self.swap(p).wait_recv()
            held = self.stages[t][:, r0 : r0 + nr, l0 : l0 + w]
            self.block(p, 0, self.x, self.y)[...] = held.astype(jnp.bfloat16)
            for d in range(1, self.lines):
                self.go(p, functools.partial(self.direct, p, d))
            if p < self.ahead:
                self.own(p)

    def first(self, p):
        x, y, c = self.x, self.y, self.c
        if p >= self.ahead:
            self.own(p)
        for d in range(1, self.lines):
            self.direct(p, d, back=d).wait_recv()
            self.go(p, functools.partial(self.to_a, p, d, x, y))
            self.go(p, functools.partial(self.to_b, p, d, x, y))
        self.go(p, lambda: self.share(p, 0, x, y, c))

    def second(self, p):
        for d in range(self.lines):
            self.to_a(p, d, self.xa, self.ya).wait_recv()
            self.go(p, functools.partial(self.to_b, p, d, self.xa, self.ya, 1))
        self.go(p, lambda: self.share(p, 1, self.xa, self.ya, self.c))

    def third(self, p):
        x, y = self.x, self.y
        for d in range(self.lines):
            self.to_b(p, d, self.xb, self.yb).wait_recv()
        self.go(p, lambda: self.share(p, 2, self.xb, self.yb, self.c))
        for d in range(self.lines):
            self.to_b(p, d, 1 - x, 1 - y, 1).wait_recv()
        self.go(p, lambda: self.share(p, 3, 1 - x, 1 - y, self.c))

    def fourth(self, p):
        x, y, c = self.x, self.y, 1 - self.c
        for k, sx, sy in ((0, x, y), (1, self.xb, self.yb), (2, self.xa, self.ya), (3, 1 - x, 1 - y)):
            self.share(p, k, sx, sy, c).wait_recv()

    def events(self):
        steps = (self.first, self.second, self.third, self.fourth)
        urgent = [(0, 0), (0, 1), (1, 0), (2, 0), (3, 0)]
        timed = []
        for p in range(1, len(self.pieces)):
            for k, lag in enumerate(GATHER_LAGS):
                if (k, p) not in urgent:
                    timed.append((GATHER_STARTS[p] + lag, len(timed), functools.partial(steps[k], p)))
        urgent = [functools.partial(steps[k], p) for k, p in urgent]
        rest = functools.partial(self.place_own, range(self.ahead, len(self.pieces)))
        return urgent[:1] + [rest] + urgent[1:], timed

    def sent(self, *pieces):
        for p, make in self.started:
            if p in pieces:
                make().wait_send()


def deal(timed, times):
    plan = [[] for _ in range(len(times) + 1)]
    for when, _, event in sorted(timed, key=lambda e: e[:2]):
        plan[next((k for k, t in enumerate(times) if t >= when), len(times))].append(event)
    return plan


def ends(start, *steps):
    out = []
    for step in steps:
        start += step
        out.append(start)
    return out


def run_at(index, values):
    for value, events in values:
        if events:

            @pl.when(index == value)
            def _(events=events):
                for event in events:
                    event()


def columns(ref, start, size):
    return ref[:, :, :, :, :, pl.ds(start, size)].reshape(-1, size)


def turned(a, b):
    return lax.dot_general(a, b, (((1,), (1,)), ((), ())), preferred_element_type=jnp.float32)


def tallest(scores):
    part_max = jnp.max(scores.reshape(-1, 64, scores.shape[1]), axis=0)
    return jnp.max(part_max, axis=0, keepdims=True)


def swapped(block, cosine, sine):
    lane = lax.broadcasted_iota(jnp.int32, block.shape, 1)
    other = jnp.where(lane % 16 < 8, pltpu.roll(block, 120, 1), pltpu.roll(block, 8, 1))
    return block * cosine + other * sine


def tables():
    half = ROT // 2
    inverse = np.float32(10000.0) ** (-(np.arange(half, dtype=np.float32) * 2) / ROT)
    phase = np.arange(SEQ, dtype=np.float32)[:, None] * inverse.astype(np.float32)[None, :]
    cos_t, sin_t = np.cos(phase.astype(np.float64)), np.sin(phase.astype(np.float64))
    rest = np.zeros((SEQ, HD - ROT))
    cosine = np.concatenate([cos_t, cos_t, rest + 1.0] * 2, axis=1)
    sine = np.concatenate([-sin_t, sin_t, rest] * 2, axis=1)
    return jnp.asarray(cosine.astype(np.float32)), jnp.asarray(sine.astype(np.float32))


def scatter_pieces(blocks):
    r0, r1, r2, r3, r4 = (r for _, r, _ in blocks)
    w, q = D // 2, PACK // 4
    pieces = [(1, 0, r1, 0, 0, w), (0, 0, r0, 0, 0, q), (0, 0, r0, q, q, q)]
    for k in range(4):
        pieces += [(3, 0, r3, 0, 0, w), (2, 0, r2, 2 * w * k, w * k, w)]
    return pieces + [(4, 0, r4, 0, 0, SMALL // 2)]


SLOTS = 2


class Scatter:
    def __init__(self, lines, rows, blocks, grads, outs, buffers, sems):
        self.lines, self.rows, self.blocks = lines, rows, blocks
        self.grads, self.outs = grads, outs
        kinds = len(blocks)
        self.near, self.from_b, self.from_a, self.from_z, self.total, self.last = (
            buffers[kinds * k : kinds * (k + 1)] for k in range(6)
        )
        self.send, self.recv, self.credit = sems
        self.pieces = scatter_pieces(blocks)
        self.only = [(p - 3) // 2 if piece[0] == 3 else None for p, piece in enumerate(self.pieces)]
        self.z, self.x, self.y, self.c = place()
        self.xa, self.ya, self.xb, self.yb = partners()
        self.sibling = device(self.z, self.x, self.y, 1 - self.c)
        self.started = []

    def go(self, make):
        make().start()
        self.started.append((None, make))

    def where(self, p, body):
        if self.only[p] is None:
            body()
        else:
            pl.when(self.z == self.only[p])(body)

    def every(self, p):
        return slice(None) if self.only[p] is None else pl.ds(self.only[p], 1)

    def planes(self, p, body):
        if self.only[p] is None:
            pl.loop(0, self.lines)(body)
        else:
            body(self.only[p])

    def cut(self, p, ref, *lead):
        t, r0, nr, _, l0, w = self.pieces[p]
        return ref[t].at[(*lead, slice(None), pl.ds(r0, nr), pl.ds(l0, w))]

    def grad(self, p, z, x, y, half=None):
        half = self.c if half is None else half
        return part(self.pieces[p], self.grads[self.pieces[p][0]], z, x, y, half)

    def slot(self, p):
        t, _, _, _, l0, w = self.pieces[p]
        return {0: l0 // w, 1: 0, 2: l0 // w % SLOTS, 3: (p - 3) // 2 % SLOTS, 4: 0}[t]

    def near_copy(self, p):
        every = slice(None)
        mine = self.grad(p, self.every(p), every, every, 1 - self.c)
        near = self.near[self.pieces[p][0]].at[self.slot(p)]
        return remote(mine, near, self.send.at[p, 0], self.recv.at[p, 0], self.sibling)

    def b_copy(self, p, k):
        at = (self.xb, self.yb) if k == 0 else (1 - self.x, 1 - self.y)
        return remote(
            self.grad(p, self.every(p), *at),
            self.cut(p, self.from_b, k, self.every(p)),
            self.send.at[p, 1 + k],
            self.recv.at[p, 1 + k],
            device(self.z, self.xb, self.yb, self.c),
        )

    def a_copy(self, p):
        return remote(
            self.grad(p, self.every(p), self.xa, self.ya),
            self.cut(p, self.from_a, self.every(p)),
            self.send.at[p, 3],
            self.recv.at[p, 3],
            device(self.z, self.xa, self.ya, self.c),
        )

    def z_copy(self, p, d):
        other = lax.rem(self.z + d, self.lines)
        return remote(
            self.grad(p, other, self.x, self.y),
            self.cut(p, self.from_z, d - 1),
            self.send.at[p, 3 + d],
            self.recv.at[p, 3 + d],
            device(other, self.x, self.y, self.c),
        )

    def last_copy(self, p):
        t, r0, nr, _, l0, w = self.pieces[p]
        if self.blocks[t][0] == 2:
            src = self.total[t].at[1 - self.c, pl.ds(r0, nr), pl.ds(l0, w)]
            dst = self.last[t].at[pl.ds(r0, nr), pl.ds(l0, w)]
        else:
            away = pl.ds(pl.multiple_of((1 - self.c) * self.rows, 8), self.rows)
            src = self.total[t].at[0, away, pl.ds(l0, w)]
            dst = self.last[t].at[:, pl.ds(l0, w)]
        k = 3 + self.lines
        return remote(src, dst, self.send.at[p, k], self.recv.at[p, k], self.sibling)

    def uses(self, p):
        t = self.pieces[p][0]
        if t not in (2, 3):
            return False, False
        return p - 2 * SLOTS >= 3, p + 2 * SLOTS <= 10

    def first(self, p):
        if self.uses(p)[0]:
            pl.semaphore_wait(self.credit.at[self.pieces[p][0] - 2], 1)
        self.go(lambda: self.near_copy(p))

    def second(self, p):
        f32 = jnp.float32
        self.near_copy(p).wait_recv()
        near = self.near[self.pieces[p][0]].at[self.slot(p)]

        def add(k):
            for x in range(2):
                for y in range(2):
                    kept = self.grad(p, k, x, y)
                    got = near[0 if self.only[p] is not None else k, x, y]
                    kept[...] = (kept[...].astype(f32) + got.astype(f32)).astype(jnp.bfloat16)

        self.planes(p, add)
        if self.uses(p)[1]:
            credit = self.credit.at[self.pieces[p][0] - 2]
            pl.semaphore_signal(credit, inc=1, device_id=self.sibling, device_id_type=MESH)
        self.go(lambda: self.b_copy(p, 1))
        self.go(lambda: self.b_copy(p, 0))

    def third(self, p):
        self.b_copy(p, 1).wait_recv()

        def add(k):
            kept, got = self.grad(p, k, self.xa, self.ya), self.cut(p, self.from_b, 1, k)
            kept[...] = (kept[...].astype(jnp.float32) + got[...].astype(jnp.float32)).astype(jnp.bfloat16)

        self.planes(p, add)
        self.go(lambda: self.a_copy(p))

    def mine(self, p, k):
        got = self.cut(p, self.from_b, 0, k)[...].astype(jnp.float32) + self.cut(p, self.from_a, k)[...].astype(jnp.float32)
        return self.grad(p, k, self.x, self.y)[...].astype(jnp.float32) + got

    def fourth(self, p):
        self.b_copy(p, 0).wait_recv()
        self.a_copy(p).wait_recv()
        q = self.only[p]

        def send():
            for d in range(1, self.lines):
                self.go(functools.partial(self.z_copy, p, d))

        def round_off(k):
            self.grad(p, k, self.x, self.y)[...] = self.mine(p, k).astype(jnp.bfloat16)

        if q is None:

            @pl.loop(1, self.lines)
            def _(d):
                round_off(lax.rem(self.z + d, self.lines))

            send()
        else:

            def to_owner():
                return self.z_copy(p, lax.rem(q - self.z + self.lines, self.lines))

            @pl.when(self.z != q)
            def _():
                round_off(q)
                to_owner().start()

            self.started.append((lambda: self.z != q, to_owner))

        def keep():
            self.cut(p, self.total)[...] = self.mine(p, self.z if q is None else q)

        self.where(p, keep)

    def fifth(self, p):
        def body():
            for d in range(1, self.lines):
                self.z_copy(p, d).wait_recv()
            total = self.cut(p, self.total)
            acc = total[...]
            for d in range(1, self.lines):
                acc = acc + self.cut(p, self.from_z, d - 1)[...].astype(jnp.float32)
            total[...] = acc
            self.last_copy(p).start()

        self.where(p, body)
        q = self.only[p]
        self.started.append((None if q is None else lambda: self.z == q, lambda: self.last_copy(p)))

    def sixth(self, p):
        t, r0, nr, c0, l0, w = self.pieces[p]

        def body():
            self.last_copy(p).wait_recv()
            if self.blocks[t][0] == 2:
                kept = self.total[t][self.c, r0 : r0 + nr, l0 : l0 + w]
                got = self.last[t][r0 : r0 + nr, l0 : l0 + w]
                to = slice(r0, r0 + nr)
            else:
                kept = self.total[t][0, pl.ds(pl.multiple_of(self.c * self.rows, 8), self.rows), l0 : l0 + w]
                got = self.last[t][:, l0 : l0 + w]
                to = slice(None)
            h = HALF[t] + c0
            self.outs[t][to, c0 : c0 + w] = jnp.where(self.c == 0, kept, got)
            self.outs[t][to, h : h + w] = jnp.where(self.c == 0, got, kept)

        self.where(p, body)

    def steps(self):
        return [self.first, self.second, self.third, self.fourth, self.fifth, self.sixth]

    def timed(self, p, start):
        return [(start + lag, p, functools.partial(step, p)) for step, lag in zip(self.steps(), SCATTER_LAGS)]

    def finish(self):
        for condition, make in self.started:
            if condition is None:
                make().wait_send()
            else:

                @pl.when(condition())
                def _(make=make):
                    make().wait_send()


def crossed(a, b):
    return lax.dot_general(a, b, (((0,), (0,)), ((), ())), preferred_element_type=jnp.float32)


def layer_kernel(lines, rows, blocks, linked, total_rows, *refs):
    f32, bf16 = jnp.float32, jnp.bfloat16
    tags, subset_w, tokens_h, cotan_h, cosine_h, sine_h = refs[:6]
    given, refs = (refs[6:13], refs[13:]) if linked else (refs[6:10], refs[10:])
    mixed_h, grad_tokens_h, *results = refs[:7]
    tokens, cotan, cosine, sine, d_second, small, first_t, second_in, queries, pool, keys, keys_t = refs[7:19]
    values, values_t, attended, logsums, scaled, packed_d, mask, sums, d_keys, d_values, branch, second_t = refs[19:31]
    whole, grad_packed, grad_small, load_sems, out_sems = refs[31:35], refs[35], refs[36], refs[37], refs[38]
    refs = refs[39:]
    grads = [grad_packed, *whole[1:], grad_small]
    tiles, wide, qkv = SEQ // TILE, D // 2, D + 2 * HD

    def tile(k):
        return pl.ds(pl.multiple_of(k * TILE, TILE), TILE)

    pairs = [(tokens_h, tokens), (cosine_h, cosine), (sine_h, sine), (cotan_h, cotan)]
    if not linked:
        pairs += list(zip(given, whole))
    loads = [pltpu.make_async_copy(a, b, load_sems.at[k]) for k, (a, b) in enumerate(pairs)]
    for copy in loads:
        copy.start()
    if linked:
        query, pair, out, up, down, gains, biases = given
        packed, stages, square, gather_sems, refs = refs[0], refs[1:5], refs[5], refs[6:10], refs[10:]
        for p in range(H // 2):
            packed[:, place_of(p) : place_of(p) + 2 * HD] = query[:, 2 * HD * p : 2 * HD * (p + 1)]
        packed[:, PAIR : PAIR + 2 * HD] = pair[...]
        square[...] = jnp.zeros_like(square)
        square[0:2, 0:rows] = gains[...]
        square[2:4, 0:rows] = biases[...]
        spot = lax.broadcasted_iota(jnp.int32, (rows, 128), 1) == tags[0] + 4
        spot = jnp.where(lax.broadcasted_iota(jnp.int32, (rows, 128), 0) == 0, spot.astype(f32), 0.0)
        packed[:, qkv:] = square[...].T[:rows] + spot
        greet(lines)
        gather = Gather(lines, rows, blocks, [packed, out, up, down], stages, whole, gather_sems)
        scatter = Scatter(lines, rows, blocks, grads, results, refs[:30], refs[30:33])
        gather.begin(2)
        urgent, timed = gather.events()
    else:
        urgent, timed = [], []
    packed_w, out_w, up_w, down_w = whole

    steps = (PROJECT_STEPS, FORWARD_STEPS, OUTWARD_STEPS, BACKWARD_STEPS, CLOSE_STEPS, CHUNK_STEPS * 4, TOKEN_STEPS)
    starts, slots = [0], [0]
    for part_steps in steps:
        starts.append(starts[-1] + sum(part_steps))
        slots.append(slots[-1] + len(part_steps))
    if linked:
        edge = 0.01
        timed += scatter.timed(0, starts[3] - edge)
        ready = starts[3] + 4 * sum(BACKWARD_STEPS[:2])
        timed += [(ready - 2 * edge, 100, lambda: query_grads(0, PACK // 4))] + scatter.timed(1, ready - edge)
        timed += scatter.timed(2, starts[5] - edge)
        for q in range(4):
            start = starts[5] + q * sum(CHUNK_STEPS) + sum(CHUNK_STEPS[:6]) - edge
            timed += scatter.timed(3 + 2 * q, start) + scatter.timed(4 + 2 * q, start + sum(CHUNK_STEPS[6:]))
        timed += scatter.timed(11, starts[6] + sum(TOKEN_STEPS[:4]) + edge)
    plan = deal(timed, ends(0.0, *(step for part_steps in steps for step in part_steps)))

    def slot(section, index, values):
        run_at(index, [(v, plan[slots[section] + v]) for v in values])

    row = lax.broadcasted_iota(jnp.int32, (TILE, TILE), 0)
    column = lax.broadcasted_iota(jnp.int32, (TILE, TILE), 1)
    mask[...] = jnp.where(row <= column, 0.0, -1e30)
    sums[...] = jnp.zeros_like(sums)
    d_keys[...] = jnp.zeros_like(d_keys)
    d_values[...] = jnp.zeros_like(d_values)
    lane = lax.broadcasted_iota(jnp.int32, (TILE, 2 * HD), 1)
    left = lane < HD
    loads[0].wait()

    def normed(k):
        inputs = tokens[tile(k), :].astype(f32)
        centred = inputs - jnp.mean(inputs, axis=-1, keepdims=True)
        inv_std = lax.rsqrt(jnp.mean(centred * centred, axis=-1, keepdims=True) + eps_norm)
        return centred * inv_std, inv_std

    @pl.loop(0, tiles)
    def _(k):
        d_second[tile(k), :] = normed(k)[0]

    for copy in loads[1:]:
        copy.wait()
    for event in urgent:
        event()
    small[...] = columns(packed_w, qkv, 128).astype(f32).T

    @pl.loop(0, tiles)
    def _(k):
        norm = d_second[tile(k), :]
        a1 = (norm * small[0:1, :] + small[2:3, :]).astype(bf16)
        a2 = norm * small[1:2, :] + small[3:4, :]
        first_t[:, tile(k)] = a1.T
        second_in[tile(k), :] = a2.astype(bf16)
        second_t[:, tile(k)] = a2.astype(bf16).T
        mixed = jnp.dot(a1, columns(packed_w, 0, qkv), preferred_element_type=f32)
        cos_t, sin_t = cosine[tile(k), :], sine[tile(k), :]
        for p in range(H // 2):
            turn = swapped(mixed[:, place_of(p) : place_of(p) + 2 * HD], cos_t, sin_t).astype(bf16).astype(f32)
            turn = turn * (LOG2E / 8)
            high = turn.astype(bf16).astype(f32)
            low = turn - high
            queries[2 * p, tile(k), :] = jnp.where(left, high, pltpu.roll(low, HD, 1)).astype(bf16)
            queries[2 * p + 1, tile(k), :] = jnp.where(left, pltpu.roll(high, HD, 1), low).astype(bf16)
        pair_t = mixed[:, PAIR : PAIR + 2 * HD]
        pair_t = jnp.where(left, swapped(pair_t, cos_t, sin_t), pair_t).astype(bf16).astype(f32)
        other = pltpu.roll(pair_t, HD, 1)
        both = jnp.where(left, pair_t, other)
        keys[tile(k), :] = both.astype(bf16)
        keys_t[:, tile(k)] = both.T[:HD].astype(bf16)
        values[tile(k), :] = jnp.where(left, other, jnp.where(lane < HD + 2, -1.0, 0.0)).astype(bf16)
        values_t[:, tile(k)] = jnp.where(left, other, jnp.where(lane == HD, 1.0, 0.0)).T.astype(bf16)
        slot(0, k, range(tiles))

    @pl.loop(0, H // 4)
    def _(two):
        work = [(i, hh, pp) for pp in range(2) for i in range(tiles) for hh in range(2)]
        ready, shares, heads = {}, {}, {}

        def score(n):
            i, hh, pp = work[n]
            pr = two * 2 + pp
            count = TILE * (i + 1)
            ready[n] = turned(keys[0:count, :], queries[pr * 2 + hh, i * TILE : count, :])

        def weigh(n):
            i, hh, pp = work[n]
            pr = two * 2 + pp
            count = TILE * (i + 1)
            scores = ready.pop(n)
            last = scores[count - TILE :] + mask[...]
            peak = tallest(last)
            if i:
                peak = jnp.maximum(peak, tallest(scores[: count - TILE]))
            probs = jnp.exp2(last - peak).astype(bf16)
            if i:
                probs = jnp.concatenate([jnp.exp2(scores[: count - TILE] - peak).astype(bf16), probs], axis=0)
            shares[n] = peak, probs

        def collect(n):
            i, hh, pp = work[n]
            pr = two * 2 + pp
            count = TILE * (i + 1)
            peak, probs = shares.pop(n)
            got = jnp.dot(values_t[0:80, 0:count], probs, preferred_element_type=f32)
            total = got[HD : HD + 1]
            heads[hh] = got[:HD] * (1.0 / total)
            logsums[pr * 2 + hh, :, i * TILE : count] = peak + jnp.log2(total)
            if hh:
                both = jnp.concatenate([heads[0], heads[1]], axis=0).T
                attended[i * TILE : count, lanes(pr * 2 * HD, 2 * HD)] = both.astype(bf16)

        ahead = 2
        for n in range(len(work) + ahead + 2):
            if n < len(work):
                score(n)
            if 0 <= n - ahead < len(work):
                weigh(n - ahead)
            if 0 <= n - ahead - 2 < len(work):
                collect(n - ahead - 2)
        for i in range(4):
            slot(1, two * 4 + i, range(i, 2 * (H // 2), 4))

    kind = lax.broadcasted_iota(jnp.int32, (128, D), 0)
    count = jnp.sum(jnp.where(kind == tags[0] + 4, small[...], 0.0), keepdims=True)
    subset = lax.broadcasted_iota(jnp.int32, subset_w.shape, 1)
    weight = jnp.sum(jnp.where(subset == tags[0], subset_w[...], 0.0), keepdims=True)
    scale = weight / count * (total_rows / SUBSETS)

    @pl.loop(0, tiles)
    def _(k):
        grad_out = (cotan[tile(k), :].astype(f32) * scale).astype(bf16)
        scaled[tile(k), :] = grad_out
        heads = attended[tile(k), :]
        out_m = out_w[...].reshape(D, D)
        branch[tile(k), :] = tokens[tile(k), :].astype(f32) + jnp.dot(heads, out_m, preferred_element_type=f32)
        d_heads_t = turned(grad_out, out_m).astype(bf16).astype(f32)
        for p in range(H // 2):
            block = d_heads_t[:, 2 * HD * p : 2 * HD * (p + 1)]
            product = block * heads[:, 2 * HD * p : 2 * HD * (p + 1)].astype(f32)
            for hh, (mine, there) in enumerate(((left, block), (~left, pltpu.roll(block, HD, 1)))):
                delta = jnp.sum(jnp.where(mine, product, 0.0), axis=1, keepdims=True)
                high = delta.astype(bf16).astype(f32)
                extra = jnp.where(lane == HD, high, jnp.where(lane == HD + 1, delta - high, 0.0))
                pool[2 * p + hh, tile(k), :] = jnp.where(left, there, extra).astype(bf16)
        slot(2, k, range(tiles))

    if linked:
        gather.sent(1)

    @pl.loop(0, 2)
    def _(k):
        got = crossed(attended[:, lanes(k * wide, wide)], scaled[...]).astype(bf16)
        grads[1][pl.ds(2 * k, 2)] = got.reshape(2, 2, 2, 1, D // 16, D)
        slot(2, tiles + k, range(tiles, tiles + 2))

    def query_grads(start, stop):
        for span in (slice(start, stop), slice(PACK // 2 + start, min(PACK // 2 + stop, qkv))):
            for k in range(2):
                got = jnp.dot(first_t[k * wide : (k + 1) * wide, :], packed_d[:, span], preferred_element_type=f32).astype(bf16)
                grad_packed[2 * k : 2 * k + 2, :, :, :, :, span] = got.reshape(2, 2, 2, 1, D // 16, -1)

    @pl.loop(0, H // 2)
    def _(pr):
        work = [(i, hh) for i in range(tiles) for hh in range(2)]
        ready, shares, d_query = {}, {}, {}

        def score(n):
            i, hh = work[n]
            count, span = TILE * (i + 1), slice(i * TILE, TILE * (i + 1))
            head = pr * 2 + hh
            ready[n] = turned(keys[0:count, :], queries[head, span, :]), turned(values[0:count, :], pool[head, span, :])

        def weigh(n):
            i, hh = work[n]
            count, span = TILE * (i + 1), slice(i * TILE, TILE * (i + 1))
            scores, d_probs = ready.pop(n)
            shift = logsums[pr * 2 + hh, :, span]
            probs = jnp.exp2(scores[count - TILE :] + mask[...] - shift)
            if i:
                probs = jnp.concatenate([jnp.exp2(scores[: count - TILE] - shift), probs], axis=0)
            shares[n] = probs.astype(bf16), (probs * d_probs).astype(bf16)

        def collect(n):
            i, hh = work[n]
            count, span = TILE * (i + 1), slice(i * TILE, TILE * (i + 1))
            d_query[hh] = jnp.dot(keys_t[:, 0:count], shares[n][1], preferred_element_type=f32)
            if hh:
                both = [shares.pop(n - 1), shares.pop(n)]
                for acc, k, other in ((d_values, 0, pool), (d_keys, 1, queries)):
                    two = jnp.concatenate([other[pr * 2, span, :], other[pr * 2 + 1, span, :]], axis=0)
                    parts = jnp.concatenate([both[0][k], both[1][k]], axis=1)
                    acc[0:count, :] += jnp.dot(parts, two, preferred_element_type=f32)
                d_q = jnp.concatenate([d_query[0], d_query[1]], axis=0).T * 0.125
                d_q = swapped(d_q, cosine[span, :], -sine[span, :])
                packed_d[span, lanes(place_of(pr), 2 * HD)] = d_q.astype(bf16)

        for n in range(len(work) + 2 + 1):
            if n < len(work):
                score(n)
            if 0 <= n - 2 < len(work):
                weigh(n - 2)
            if 0 <= n - 2 - 1 < len(work):
                collect(n - 2 - 1)
        for i in (0, 1):
            slot(3, pr * 2 + i, range(i, 2 * (H // 2), 2))

    @pl.loop(0, tiles)
    def _(k):
        d_key = d_keys[tile(k), :]
        d_key = (d_key + pltpu.roll(d_key, HD, 1)) * (1.0 / LOG2E)
        d_key = swapped(d_key, cosine[tile(k), :], -sine[tile(k), :])
        d_pair = jnp.where(left, d_key, pltpu.roll(d_values[tile(k), :], HD, 1)).astype(bf16)
        packed_d[tile(k), PAIR : PAIR + 2 * HD] = d_pair
        slot(4, k, range(tiles))

    if not linked:
        query_grads(0, PACK // 4)
    query_grads(PACK // 4, PACK // 2)
    grad_packed[:, :, :, :, :, qkv:] = jnp.zeros((4, 2, 2, 1, D // 16, PACK - qkv), bf16)
    for event in plan[slots[4] + tiles]:
        event()
    if linked:
        gather.sent(2, 3)

    @pl.loop(0, 4)
    def _(q):
        def up_m():
            return columns(up_w, pl.multiple_of(q * D, D), D)

        def down_m():
            return down_w[q].reshape(D, D)

        @pl.loop(0, tiles)
        def _(k):
            pre = jnp.dot(second_in[tile(k), :], up_m(), preferred_element_type=f32)
            d_hidden = turned(scaled[tile(k), :], down_m())
            cdf = 0.5 + 0.5 * lax.erf(pre * 0.7071067811865476)
            density = jnp.exp2(pre * pre * (-0.5 * LOG2E)) * 0.3989422804014327
            active = (pre * cdf).astype(bf16)
            d_up = (d_hidden * (cdf + pre * density)).astype(bf16)
            active_t = active.T
            for b in range(2):
                queries[2 * k + b, 0:D, :] = active_t[:, 128 * b : 128 * (b + 1)]
            for b in range(6):
                pool[b, tile(k), :] = d_up[:, 128 * b : 128 * (b + 1)]
            branch[tile(k), :] += jnp.dot(active, down_m(), preferred_element_type=f32)
            got = turned(d_up, up_m())
            d_second[tile(k), :] = jnp.where(q == 0, got, got + d_second[tile(k), :])
            slot(5, q * 8 + k, [v for v in range(32) if v % 8 < 4])

        hidden_t = jnp.concatenate([queries[b, 0:D, :] for b in range(8)], axis=1)
        got = jnp.dot(hidden_t, scaled[...], preferred_element_type=f32).astype(bf16)
        down_w[q] = got.reshape(2, 2, 2, 4 * D // 32, D)
        for v in (4, 5):
            slot(5, q * 8 + v, [8 * p + v for p in range(4)])
        if linked:
            run_at(q, [(v, [functools.partial(gather.sent, 4 + v)]) for v in range(4)])
        d_ups = jnp.concatenate([pool[b] for b in range(6)], axis=1)
        got = jnp.dot(second_t[...], d_ups, preferred_element_type=f32).astype(bf16)
        up_w[:, :, :, :, :, lanes(q * D, D)] = got.reshape(4, 2, 2, 1, D // 16, D)
        for v in (6, 7):
            slot(5, q * 8 + v, [8 * p + v for p in range(4)])

    @pl.loop(0, tiles)
    def _(k):
        attended[tile(k), :] = branch[tile(k), :].astype(bf16)
        d_first = turned(packed_d[tile(k), 0:qkv], columns(packed_w, 0, qkv))
        branch[tile(k), :] = d_first
        second, norm = d_second[tile(k), :], normed(k)[0]
        for n, value in enumerate((d_first * norm, second * norm, d_first, second)):
            sums[n : n + 1, :] += jnp.sum(value, axis=0, keepdims=True)
        slot(6, k, range(tiles))

    flushed = [pltpu.make_async_copy(attended, mixed_h, out_sems.at[0])]
    flushed[0].start()
    grad_small[:, :, :, :, :, 0:128] = sums[...].T.astype(bf16).reshape(4, 2, 2, 1, D // 16, 128)
    grad_small[:, :, :, :, :, 128:] = jnp.zeros((4, 2, 2, 1, D // 16, SMALL - 128), bf16)

    @pl.loop(0, tiles)
    def _(k):
        norm, inv_std = normed(k)
        d_normed = branch[tile(k), :] * small[0:1, :] + d_second[tile(k), :] * small[1:2, :]
        inner = jnp.mean(d_normed * norm, axis=-1, keepdims=True)
        d_inputs = inv_std * (d_normed - jnp.mean(d_normed, axis=-1, keepdims=True) - norm * inner)
        second_in[tile(k), :] = (cotan[tile(k), :].astype(f32) * scale + d_inputs).astype(bf16)
        slot(6, tiles + k, range(tiles, 2 * tiles))

    flushed.append(pltpu.make_async_copy(second_in, grad_tokens_h, out_sems.at[1]))
    flushed[-1].start()
    for event in plan[-1]:
        event()
    if linked:
        gather.sent(0)
        scatter.finish()
    else:
        for t in range(5):
            flushed.append(pltpu.make_async_copy(grads[t], results[t], out_sems.at[2 + t]))
            flushed[-1].start()
    for copy in flushed:
        copy.wait()


def layer(linked, lines, rows, rows_down, total_rows, tags, subset_w, tokens, cotan, cosine, sine, weights):
    blocks = layout(rows, rows_down)
    f32, bf16 = jnp.float32, jnp.bfloat16
    shapes = [(lines, 2, 2, g, r, k) for g, r, k in blocks]
    own_rows = [r if g == 2 else rows for g, r, k in blocks]
    vmem = pl.BlockSpec(memory_space=pltpu.VMEM)
    anywhere = pl.BlockSpec(memory_space=pl.ANY)
    if linked:
        results = [jax.ShapeDtypeStruct((o, k), f32) for o, (g, r, k) in zip(own_rows, blocks)]
    else:
        weights = [a.reshape(shape) for a, shape in zip(weights, shapes)]
        results = [jax.ShapeDtypeStruct(shape, bf16) for shape in shapes]
    tall = (SEQ, D)
    buffers = [
        (tall, bf16),
        (tall, bf16),
        ((SEQ, 2 * HD), f32),
        ((SEQ, 2 * HD), f32),
        (tall, f32),
        ((128, D), f32),
        ((D, SEQ), bf16),
        (tall, bf16),
        ((H, SEQ, 2 * HD), bf16),
        ((H, SEQ, 2 * HD), bf16),
        ((SEQ, 2 * HD), bf16),
        ((HD, SEQ), bf16),
        ((SEQ, 2 * HD), bf16),
        ((2 * HD, SEQ), bf16),
        (tall, bf16),
        ((H, 1, SEQ), f32),
        (tall, bf16),
        ((SEQ, D + 2 * HD), bf16),
        ((TILE, TILE), f32),
        ((128, D), f32),
        ((SEQ, 2 * HD), f32),
        ((SEQ, 2 * HD), f32),
        (tall, f32),
        ((D, SEQ), bf16),
    ]
    buffers += [(shape, bf16) for shape in shapes[:4]] + [(shapes[0], bf16), (shapes[4], bf16)]
    scratch = [pltpu.VMEM(shape, kind) for shape, kind in buffers]
    scratch += [pltpu.SemaphoreType.DMA((8,)), pltpu.SemaphoreType.DMA((7,))]
    if linked:
        scratch += [pltpu.VMEM((rows, PACK), f32)]
        scratch += [pltpu.VMEM((g, r, k // 2), f32) for g, r, k in blocks[:4]]
        scratch += [pltpu.VMEM((128, 128), f32)]
        count, kinds = len(gather_pieces(blocks)), 4 * lines + 3
        scratch += [pltpu.SemaphoreType.DMA((count,))] * 2 + [pltpu.SemaphoreType.DMA((count, kinds))] * 2
        near = [(2, lines, PACK // 4), (1, lines, D // 2), (SLOTS, lines, D // 2), (SLOTS, 1, D // 2), (1, lines, SMALL // 2)]
        scratch += [pltpu.VMEM((n, z, 2, 2, g, r, w), bf16) for (n, z, w), (g, r, k) in zip(near, blocks)]
        for lead in ((2, lines), (lines,), (lines - 1,)):
            scratch += [pltpu.VMEM((*lead, g, r, k // 2), bf16) for g, r, k in blocks]
        scratch += [pltpu.VMEM((g, r, k // 2), f32) for g, r, k in blocks]
        scratch += [pltpu.VMEM((o, k // 2), f32) for o, (g, r, k) in zip(own_rows, blocks)]
        count = len(scatter_pieces(blocks))
        scratch += [pltpu.SemaphoreType.DMA((count, lines + 4))] * 2 + [pltpu.SemaphoreType.REGULAR((2,))]
    return pl.pallas_call(
        functools.partial(layer_kernel, lines, rows, blocks, linked, total_rows),
        out_shape=[jax.ShapeDtypeStruct(tall, bf16)] * 2 + results,
        in_specs=[pl.BlockSpec(memory_space=pltpu.SMEM), vmem] + [anywhere] * 4 + [vmem if linked else anywhere] * len(weights),
        out_specs=[anywhere] * 2 + [vmem if linked else anywhere] * 5,
        scratch_shapes=scratch,
        compiler_params=pltpu.CompilerParams(
            collective_id=0 if linked else None, has_side_effects=linked, vmem_limit_bytes=63 * 2**20
        ),
        name="layer",
    )(tags, subset_w, tokens, cotan, cosine, sine, *weights)


def finish_kernel(rows, *refs):
    packed, small, *rest = refs[:7]
    query, pair, gains, biases, *to = refs[7:]
    for p in range(H // 2):
        query[:, 2 * HD * p : 2 * HD * (p + 1)] = packed[:, place_of(p) : place_of(p) + 2 * HD]
    pair[...] = packed[:, PAIR : PAIR + 2 * HD]
    turned_back = small[:, 0:128].T
    gains[...] = turned_back[0:2]
    biases[...] = turned_back[2:4]
    for a, b in zip(rest, to):
        b[...] = a[...]


def finish(rows, packed, small, *rest):
    f32 = jnp.float32
    vmem = pl.BlockSpec(memory_space=pltpu.VMEM)
    shapes = [(rows, D), (rows, 2 * HD), (2, rows), (2, rows)]
    return pl.pallas_call(
        functools.partial(finish_kernel, rows),
        out_shape=[jax.ShapeDtypeStruct(a, f32) for a in shapes] + [jax.ShapeDtypeStruct(a.shape, a.dtype) for a in rest],
        in_specs=[vmem] * (2 + len(rest)),
        out_specs=[vmem] * (4 + len(rest)),
        compiler_params=pltpu.CompilerParams(vmem_limit_bytes=63 * 2**20),
        name="finish",
    )(packed, small, *rest)


def is_linked(rows):
    return lax.axis_size("dp") == 8 and lax.axis_size("fsdp") == 4 and rows % 8 == 0


def fetch_weights(query_w, pair_w, out_w, up_w, down_w, gains, biases, tags):
    onehot = (tags[0] == jnp.arange(SUBSETS, dtype=jnp.int32)).astype(jnp.float32)
    own_counts = jnp.where((jnp.arange(query_w.shape[0]) == 0)[:, None], onehot[None, :], 0.0)
    small = jnp.concatenate([gains.T, biases.T, own_counts], axis=1)
    small = jnp.pad(small, ((0, 0), (0, 128 - small.shape[1])))
    pairs = [query_w[:, 2 * HD * p : 2 * HD * (p + 1)] for p in range(H // 2)]
    packed = jnp.concatenate([*pairs[0::2], pair_w, *pairs[1::2], small], axis=1)
    return [
        lax.all_gather(a.astype(jnp.bfloat16), ("dp", "fsdp"), axis=0, tiled=True)
        for a in (packed, out_w, up_w, down_w)
    ]


def body(
    tokens,
    w_query,
    w_pair,
    w_attn_out,
    w_up,
    w_down,
    ln_gains,
    ln_biases,
    cotangent,
    subset_tags,
    subset_weights,
):
    cosine, sine = tables()
    linked = is_linked(w_query.shape[0])
    shards = (w_query, w_pair, w_attn_out, w_up, w_down, ln_gains, ln_biases)
    total_rows = lax.axis_size("dp") * lax.axis_size("fsdp")
    if linked:
        lines, rows, rows_down = lax.axis_size("dp") // 2, w_query.shape[0], w_down.shape[0]
    else:
        lines, rows, rows_down = 4, D // 32, 4 * D // 32
        shards = fetch_weights(*shards, subset_tags)
    subset_w = subset_weights.reshape(1, SUBSETS)
    mixed, grad_tokens, *grads = layer(
        linked, lines, rows, rows_down, total_rows, subset_tags, subset_w, tokens, cotangent, cosine, sine, shards
    )
    if not linked:
        grads = [
            lax.psum_scatter(
                g.astype(jnp.float32).reshape(-1, g.shape[-1]), ("dp", "fsdp"), scatter_dimension=0, tiled=True
            )
            for g in grads
        ]
    packed_g, out_g, up_g, down_g, small_g = grads
    query_g, pair_g, gains_g, biases_g, out_g, up_g, down_g, grad_tokens, mixed = finish(
        w_query.shape[0], packed_g, small_g, out_g, up_g, down_g, grad_tokens, mixed
    )
    return mixed, grad_tokens, query_g, pair_g, out_g, up_g, down_g, gains_g, biases_g


def solution(mesh):
    in_specs = (
        P(("dp", "fsdp"), None),
        P(("dp", "fsdp"), None),
        P(("dp", "fsdp"), None),
        P(("dp", "fsdp"), None),
        P(("dp", "fsdp"), None),
        P(("dp", "fsdp"), None),
        P(None, ("dp", "fsdp")),
        P(None, ("dp", "fsdp")),
        P(("dp", "fsdp"), None),
        P(("dp", "fsdp")),
        P(),
    )
    out_specs = (
        P(("dp", "fsdp"), None),
        P(("dp", "fsdp"), None),
        P(("dp", "fsdp"), None),
        P(("dp", "fsdp"), None),
        P(("dp", "fsdp"), None),
        P(("dp", "fsdp"), None),
        P(("dp", "fsdp"), None),
        P(None, ("dp", "fsdp")),
        P(None, ("dp", "fsdp")),
    )
    return jax.shard_map(body, mesh=mesh, in_specs=in_specs, out_specs=out_specs, check_vma=False)
```
